32 devices in a mesh: fsdp: 2 (over x), ctx: 4 (over y, core), head: 4 (over z).
Axes of the slice: x: 2, y: 2, z: 4, core: 2. Of those that a mesh axis runs over, the one named last changes fastest.
Arguments:
- tokens: bfloat16 [4096, 4, 768], P(('ctx', 'head'), 'fsdp'), may hold values from -6 to 6
- segment_ids: int32 [4, 4096], P('fsdp', 'ctx'), may hold values from 0 to 4095, as said below
- routes: int32 [16, 2, 512, 2], P(('ctx', 'head'), 'fsdp'), may hold values from 0 to 3, all different within a row; in each aligned block of 512 rows (0 to 511, 512 to 1023, ..., all dimensions but the last counted through in order) at most 384 rows name the same one
- cotangent: bfloat16 [4096, 4, 768], P(('ctx', 'head'), 'fsdp'), may hold values from -6 to 6
- norm1_gain: bfloat16 [768], P('fsdp'), may hold values from 0.25 to 1.75
- qkv_weight: bfloat16 [768, 2304], P('fsdp'), may hold values from -0.21875 to 0.21875
- out_weight: bfloat16 [768, 768], P('fsdp'), may hold values from -0.875 to 0.875
- norm2_gain: bfloat16 [768], P('fsdp'), may hold values from 0.25 to 1.75
- router_weight: bfloat16 [768, 4], P('fsdp'), may hold values from -0.15625 to 0.15625
- shared_in: bfloat16 [768, 4096], P('fsdp'), may hold values from -0.21875 to 0.21875
- shared_out: bfloat16 [2048, 768], P('fsdp'), may hold values from -0.125 to 0.125
- expert_in: bfloat16 [4, 768, 4096], P(None, 'fsdp'), may hold values from -0.21875 to 0.21875
- expert_out: bfloat16 [4, 2048, 768], P(None, 'fsdp'), may hold values from -0.125 to 0.125
Outputs:
- output: bfloat16 [4096, 4, 768], P(('ctx', 'head'), 'fsdp')
- tokens_grad: float32 [4096, 4, 768], P(('ctx', 'head'), 'fsdp')
- norm1_gain_grad: float32 [768], P('fsdp')
- qkv_weight_grad: float32 [768, 2304], P('fsdp')
- out_weight_grad: float32 [768, 768], P('fsdp')
- norm2_gain_grad: float32 [768], P('fsdp')
- router_weight_grad: float32 [768, 4], P('fsdp')
- shared_in_grad: float32 [768, 4096], P('fsdp')
- shared_out_grad: float32 [2048, 768], P('fsdp')
- expert_in_grad: float32 [4, 768, 4096], P(None, 'fsdp')
- expert_out_grad: float32 [4, 2048, 768], P(None, 'fsdp')
The draws below stay inside these ranges and needn't reach their ends.
Inputs may be any that keep to these rules, and one draw needn't show every extreme that they name: `segment_ids`: each entry is the position in its sequence at which its document starts, so entries never fall along a sequence and each sequence begins with 0. `routes`: each token names two different experts. Among the rows of one device no expert is named more than 384 times, and in every draw some device's rows name one expert exactly 384 times.
All inputs are finite; a program needn't handle non-finite values.
Results may differ from the reference program's by a relative error of at most 0.023.
Values may be sent and summed in bfloat16 or wider, within the bound.
A program may use at most 256 MiB of HBM per device.

```python
import math
import jax
import jax.numpy as jnp
import numpy as np
from jax import lax

D = 768
HEADS = 12
HEAD_DIM = 64
FF = 2048
FS = 2048
EXPERTS = 4
SEQS = 2
SPAN = 256
TOK_DEV = 512
CAP = 384
SEQ_LEN = 4096
NSEQ = 4
N_FSDP = 2
N_CTX = 4
N_HEAD = 4


def draw_segment_ids(key, part):
    key = jax.random.fold_in(key, 11)
    level_key, flag_key, pick_key = jax.random.split(key, 3)
    seq_total = N_FSDP * SEQS
    doc_level = jax.random.randint(level_key, (seq_total, 1), 0, 3)
    spacing = jnp.where(doc_level == 0, 24, jnp.where(doc_level == 1, 384, 4 * SEQ_LEN))
    raw_draws = jax.random.randint(flag_key, (seq_total, SEQ_LEN), 0, 1 << 24)
    position = jnp.arange(SEQ_LEN, dtype=jnp.int32)[None, :]
    starting = (raw_draws % spacing == 0) | (position == 0) | (position == SEQ_LEN - 1)
    whole_pick = jax.random.randint(pick_key, (N_FSDP, 1), 0, SEQS)
    whole_seq = (jnp.arange(SEQS)[None, :] == whole_pick).reshape(seq_total, 1)
    starting = jnp.where(whole_seq, position == 0, starting)
    return lax.cummax(jnp.where(starting, position, 0), axis=1).astype(jnp.int32)


def levels(key, extent, shards, least, largest):
    loudness, own = 1.0, jax.random.fold_in(key, 6)
    for axis_at, blocks in shards:
        heights = jnp.exp(jax.random.uniform(jax.random.fold_in(own, axis_at), (blocks,), jnp.float32, least / len(shards), largest / len(shards)))
        loudness = loudness * jnp.repeat(heights, extent[axis_at] // blocks).reshape([-1 if axis == axis_at else 1 for axis in range(len(extent))])
    return loudness


def deal_out(rng, own, number, rows, count, top, reach, lean):
    order = jax.random.permutation(rng, count)
    crowded, usual = portions_of(count, rows * top, reach, lean, True), portions_of(count, rows * top, reach, lean, False)
    places = jnp.arange(count)

    def named(lengths, turn):
        used = int((lengths > 0).sum())
        fixed = max(1, used // 4)
        shifted = fixed + (places - fixed + turn * (used - fixed)) % max(1, count - fixed)
        return jnp.zeros((count,), jnp.int32).at[order[jnp.where(places < fixed, places, shifted)]].set(jnp.asarray(lengths, jnp.int32))

    lengths = jnp.where(number % 4 == 0, named(crowded, number // 4), named(usual, number - number // 4 - 1))
    mixed = jax.random.permutation(jax.random.fold_in(own, 3), count)
    giver, sink = mixed[0:count // 2 * 2:2], mixed[1:count // 2 * 2:2]
    margin = jnp.minimum(lengths[giver] - 1, reach - lengths[sink]) // 2
    margin = jnp.where((giver == order[0]) | (sink == order[0]) | (lengths[sink] == 0), 0, jnp.maximum(margin, 0))
    shifted = jax.random.randint(jax.random.fold_in(own, 4), (count // 2,), 0, 1 << 20) % (margin + 1)
    lengths = lengths.at[giver].add(-shifted).at[sink].add(shifted)
    labels = jnp.searchsorted(jnp.cumsum(lengths), jnp.arange(rows * top), side="right").astype(jnp.int32)
    table = labels.reshape(top, rows).T
    table = table[jax.random.permutation(jax.random.fold_in(own, 1), rows)]
    turn = jax.random.randint(jax.random.fold_in(own, 2), (rows, 1), 0, top)
    return jnp.take_along_axis(table, (jnp.arange(top)[None, :] + turn) % top, axis=1)


def portions_of(number_of, total, bound, skew, full):
    portions = [(1 << 20) // math.isqrt(grade ** skew) + 1 for grade in range(1, number_of + 1)]
    largest = bound if full else min(bound, max(-(-total // number_of), total * portions[0] // sum(portions)))
    least = 1 if total - largest >= number_of - 1 else 0
    given, rest = [largest] + [least] * (number_of - 1), total - largest - least * (number_of - 1)
    while rest > 0:
        free = [i for i in range(1, number_of) if given[i] < largest] or [i for i in range(1, number_of) if given[i] < bound]
        pool, budget = sum([portions[i] for i in free]), rest
        for i in free:
            more = min(bound - given[i], max(1, budget * portions[i] // pool), rest)
            given[i] = given[i] + more
            rest = rest - more
    return np.array(given)


def gaussian(key, dims, deviation, most, cuts=(), kind=jnp.bfloat16):
    array = jax.random.normal(key, dims, jnp.float32) * deviation
    if len(cuts) > 0:
        array = levels(key, dims, cuts, -0.22, 0.18) * array
    return jnp.clip(array, min=-most, max=most).astype(kind)


def setup_inputs(seed: int = 0) -> dict:
    key_list = jax.random.split(jax.random.key(seed), 14)
    tokens = gaussian(key_list[0], (SEQ_LEN, NSEQ, D), 1.0, 6.0, ((0, 16), (1, 2)))
    segment_ids = draw_segment_ids(jax.random.fold_in(key_list[13], 71), 0)
    routes_keys = jax.random.split(jax.random.fold_in(key_list[2], 1), (N_CTX * N_HEAD) * N_FSDP * TOK_DEV // TOK_DEV)
    routes_turns = jax.random.permutation(jax.random.fold_in(key_list[2], 3), (N_CTX * N_HEAD) * N_FSDP * TOK_DEV // TOK_DEV)
    routes = jax.vmap(lambda own, number: deal_out(jax.random.fold_in(key_list[2], 2), own, number, TOK_DEV, EXPERTS, 2, CAP, 1))(routes_keys, routes_turns).reshape((N_CTX * N_HEAD, N_FSDP, TOK_DEV, 2))
    cotangent = gaussian(key_list[3], (SEQ_LEN, NSEQ, D), 1.0, 6.0, ((0, 16), (1, 2)))
    norm1_gain = jnp.clip(1.0 + 0.15 * jax.random.normal(key_list[4], (D,), jnp.float32), 0.25, 1.75).astype(jnp.bfloat16)
    qkv_weight = gaussian(key_list[5], (D, 3 * D), D ** -0.5, 0.21875, ((0, 2),))
    out_weight = gaussian(key_list[6], (D, D), (D // 16) ** -0.5, 0.875, ((0, 2),))
    norm2_gain = jnp.clip(1.0 + 0.15 * jax.random.normal(key_list[7], (D,), jnp.float32), 0.25, 1.75).astype(jnp.bfloat16)
    router_weight = gaussian(key_list[8], (D, EXPERTS), (2 * D) ** -0.5, 0.15625, ((0, 2),))
    shared_in = gaussian(key_list[9], (D, 2 * FS), D ** -0.5, 0.21875, ((0, 2),))
    shared_out = gaussian(key_list[10], (FS, D), FS ** -0.5, 0.125, ((0, 2),))
    expert_in = gaussian(key_list[11], (EXPERTS, D, 2 * FF), D ** -0.5, 0.21875, ((1, 2),))
    expert_out = gaussian(key_list[12], (EXPERTS, FF, D), FF ** -0.5, 0.125, ((1, 2),))
    return {"tokens": tokens, "segment_ids": segment_ids, "routes": routes, "cotangent": cotangent, "norm1_gain": norm1_gain, "qkv_weight": qkv_weight, "out_weight": out_weight, "norm2_gain": norm2_gain, "router_weight": router_weight, "shared_in": shared_in, "shared_out": shared_out, "expert_in": expert_in, "expert_out": expert_out}


EPS = 1e-06
NEG = -1e+30
ROPE_BASE = 10000.0
PRECISE = lax.Precision.HIGHEST

@jax.custom_vjp
def low(v):
    return lax.optimization_barrier(v.astype(jnp.bfloat16)).astype(jnp.float32)

@jax.custom_vjp
def low_back(v):
    return v

def low_keep(v):
    return (low(v), None)

def low_pass(kept, grad):
    return (grad,)

def back_keep(v):
    return (v, None)

def back_low(kept, grad):
    return (low(grad),)
low.defvjp(low_keep, low_pass)
low_back.defvjp(back_keep, back_low)

def rms_norm(values, gain):
    return values * lax.rsqrt(lax.optimization_barrier(jnp.mean(values * values, axis=-1, keepdims=True)) + EPS) * gain

def rotate(values, position):
    half_dim = values.shape[-1] // 2
    freq_index = jnp.arange(half_dim).astype(jnp.float32)
    freq_table = jnp.exp(-math.log(ROPE_BASE) * 2.0 * freq_index / values.shape[-1])
    angle_table = position.astype(jnp.float32)[:, None] * freq_table[None, :]
    cosine = jnp.cos(angle_table)[:, None, :]
    sine_part = jnp.sin(angle_table)[:, None, :]
    first_half = values[..., :half_dim]
    second_half = values[..., half_dim:]
    return jnp.concatenate([first_half * cosine - second_half * sine_part, second_half * cosine + first_half * sine_part], axis=-1)

def swiglu(values, hidden_width):
    gate_part = values[:, :hidden_width]
    return gate_part * jax.nn.sigmoid(gate_part) * values[:, hidden_width:]

def softmax_rows(values):
    row_top = lax.optimization_barrier(jnp.max(values, axis=-1, keepdims=True))
    weights = jnp.exp(values - row_top)
    return weights / lax.optimization_barrier(jnp.sum(weights, axis=-1, keepdims=True))

def mix_weights(logits, route_rows):
    router_prob = softmax_rows(logits)
    picked = (route_rows[:, :, None] == jnp.arange(logits.shape[-1])[None, None, :]).astype(logits.dtype)
    chosen = lax.optimization_barrier(jnp.sum(router_prob[:, None, :] * picked, axis=-1))
    gate_value = chosen / lax.optimization_barrier(jnp.sum(chosen, axis=-1, keepdims=True))
    return lax.optimization_barrier(jnp.sum(gate_value[:, :, None] * picked, axis=1))

def block_layer(params, seq_rows, seq_marks, seq_routes):
    norm_one, w_qkv, w_attn, norm_two, w_router, w_shared_in, w_shared_out, w_expert_in, w_expert_out = params
    seq_len = seq_rows.shape[0]
    score_scale = HEAD_DIM ** (-0.5)
    normed = low(rms_norm(seq_rows, norm_one))
    mixed_qkv = low_back(jnp.dot(normed, w_qkv, precision=PRECISE))
    position = jnp.arange(seq_len, dtype=jnp.int32)
    rotated = rotate(mixed_qkv[:, :2 * D].reshape(seq_len, 2 * HEADS, HEAD_DIM), position)
    queries = low(low_back(rotated[:, :HEADS]))
    keys_rot = low(low_back(rotated[:, HEADS:]))
    values_all = low(low_back(mixed_qkv[:, 2 * D:].reshape(seq_len, HEADS, HEAD_DIM)))
    block_rows = min(512, seq_len)
    block_count = seq_len // block_rows

    def attend(item_data):
        query_block, query_pos, query_marks = item_data
        scores = low_back(jnp.einsum('qhd,khd->hqk', query_block, keys_rot, precision=PRECISE)) * score_scale
        visible = (position[None, :] <= query_pos[:, None]) & (seq_marks[None, :] == query_marks[:, None])
        scores = jnp.where(visible[None], scores, NEG)
        return jnp.einsum('hqk,khd->qhd', low(softmax_rows(scores)), values_all, precision=PRECISE)
    attended = lax.map(jax.checkpoint(attend), (queries.reshape(block_count, block_rows, HEADS, HEAD_DIM), position.reshape(block_count, block_rows), seq_marks.reshape(block_count, block_rows)))
    attn_rows = low(low_back(attended.reshape(seq_len, D)))
    hidden = seq_rows + low_back(jnp.dot(attn_rows, w_attn, precision=PRECISE))
    normed_two = low(rms_norm(hidden, norm_two))
    mixing = mix_weights(low_back(jnp.dot(normed_two, w_router, precision=PRECISE)), seq_routes)
    shared_pre = low_back(jnp.dot(normed_two, w_shared_in, precision=PRECISE))
    shared_act = low(swiglu(shared_pre, FS))
    result = hidden + low_back(jnp.dot(shared_act, w_shared_out, precision=PRECISE))
    for expert in range(EXPERTS):
        expert_pre = low_back(jnp.dot(normed_two, w_expert_in[expert], precision=PRECISE))
        expert_act = low(swiglu(expert_pre, FF))
        expert_result = low_back(jnp.dot(expert_act, w_expert_out[expert], precision=PRECISE))
        result = result + mixing[:, expert:expert + 1] * expert_result
    return result

def reference(tokens, segment_ids, routes, cotangent, norm1_gain, qkv_weight, out_weight, norm2_gain, router_weight, shared_in, shared_out, expert_in, expert_out):
    route_table = routes.reshape(N_CTX * N_HEAD, N_FSDP, SPAN, SEQS, 2).transpose(1, 3, 0, 2, 4).reshape(NSEQ, SEQ_LEN, 2)
    params = (norm1_gain.astype(jnp.float32), qkv_weight.astype(jnp.float32), out_weight.astype(jnp.float32), norm2_gain.astype(jnp.float32), router_weight.astype(jnp.float32), shared_in.astype(jnp.float32), shared_out.astype(jnp.float32), expert_in.astype(jnp.float32), expert_out.astype(jnp.float32))
    inputs = tokens.astype(jnp.float32)
    layer_saved = jax.checkpoint(block_layer)

    def forward(token_rows, weights):
        per_seq = jnp.transpose(token_rows, (1, 0, 2))

        def seq_step(carry, item_data):
            seq_rows, seq_marks, seq_routes = item_data
            return (carry, layer_saved(weights, seq_rows, seq_marks, seq_routes))
        _, outputs = lax.scan(seq_step, jnp.zeros((), jnp.float32), (per_seq, segment_ids, route_table))
        return jnp.transpose(outputs, (1, 0, 2))
    result, pullback = jax.vjp(forward, inputs, params)
    token_grad, weight_grads = pullback(cotangent.astype(jnp.float32))
    return (result.astype(jnp.bfloat16), token_grad, weight_grads[0], weight_grads[1], weight_grads[2], weight_grads[3], weight_grads[4], weight_grads[5], weight_grads[6], weight_grads[7], weight_grads[8])
```

```python
import functools
import math

import jax
import jax.numpy as jnp
from jax import lax
from jax.experimental import pallas as pl
from jax.experimental.pallas import tpu as pltpu
from jax.sharding import PartitionSpec as P

HEAD_DIM = 64
EPS = 1e-06
NEG = -1e30
ROPE_BASE = 10000.0
BF = jnp.bfloat16
F32 = jnp.float32
MB = 1 << 20


def swap_with(value, axis_name, bit):
    size = lax.axis_size(axis_name)
    return lax.ppermute(value, axis_name, [(i, i ^ bit) for i in range(size)])


def fsdp_gather(value, axis):
    return lax.all_gather(value, "fsdp", axis=axis, tiled=True)


def fsdp_scatter(value, axis):
    count = lax.axis_size("fsdp")
    if count != 2:
        return lax.psum_scatter(value, "fsdp", scatter_dimension=axis, tiled=True)
    mine = lax.axis_index("fsdp")
    part = value.shape[axis] // 2
    sent = lax.dynamic_slice_in_dim(value, (1 - mine) * part, part, axis)
    kept = lax.dynamic_slice_in_dim(value, mine * part, part, axis)
    got = swap_with(sent, "fsdp", 1)
    return (kept.astype(F32) + got.astype(F32)).astype(value.dtype)


def line_gather(value, axis):
    count = lax.axis_size("head")
    mine = lax.axis_index("head")
    part = value.shape[axis]
    up = [(i, i + 1) for i in range(count - 1)]
    down = [(i + 1, i) for i in range(count - 1)]
    below, above = [], []
    rising, falling = value, value
    for _ in range(count - 1):
        rising = lax.ppermute(rising, "head", up)
        falling = lax.ppermute(falling, "head", down)
        below.insert(0, rising)
        above.append(falling)
    line = jnp.concatenate(below + [value] + above, axis=axis)
    return lax.dynamic_slice_in_dim(line, (count - 1 - mine) * part, count * part, axis)


def line_scatter(value, axis):
    count = lax.axis_size("head")
    mine = lax.axis_index("head")
    part = value.shape[axis] // count
    up = [(i, i + 1) for i in range(count - 1)]
    down = [(i + 1, i) for i in range(count - 1)]

    def block(index):
        index = jnp.clip(index, 0, count - 1)
        return lax.dynamic_slice_in_dim(value, index * part, part, axis).astype(F32)

    rising, falling = None, None
    for step in range(count - 1):
        upward = block(count - 1 - step + mine)
        downward = block(step - (count - 1) + mine)
        if step:
            upward = upward + rising.astype(F32)
            downward = downward + falling.astype(F32)
        rising = lax.ppermute(upward.astype(BF), "head", up)
        falling = lax.ppermute(downward.astype(BF), "head", down)
    return block(mine) + rising.astype(F32) + falling.astype(F32)


def ctx_gather(value):
    blocks = [value]
    bit = lax.axis_size("ctx") // 2
    found = {0: value}
    while bit:
        for k in list(found):
            found[k ^ bit] = swap_with(found[k], "ctx", bit)
        bit //= 2
    blocks = [found[k] for k in range(len(found))]
    return blocks


def ctx_scatter(blocks):
    held = {k: blocks[k] for k in range(len(blocks))}
    bit = 1
    while len(held) > 1:
        kept = {}
        for k in list(held):
            if not k & bit:
                got = swap_with(held[k | bit], "ctx", bit)
                kept[k] = held[k].astype(F32) + got.astype(F32)
        held = {k: (v if len(kept) == 1 else v.astype(BF)) for k, v in kept.items()}
        bit *= 2
    return held[0]


def dot_t(a, b):
    return lax.dot_general(a, b, (((1,), (1,)), ((), ())), preferred_element_type=F32)


def dot_l(a, b):
    return lax.dot_general(a, b, (((0,), (0,)), ((), ())), preferred_element_type=F32)


def dot(a, b):
    return jnp.dot(a, b, preferred_element_type=F32)


def attend_forward(ctx, bounds, queries, keys_values, starts):
    seqs, rows, width = queries.shape
    heads = width // HEAD_DIM
    blocks = keys_values.shape[0]
    tq, tk = min(256, rows), min(512, rows)
    per = rows // tk

    def kernel(ctx_ref, bounds_ref, q_ref, kv_ref, seg_ref, o_ref, low_ref, lse_ref):
        s, i = pl.program_id(0), pl.program_id(1)
        here = ctx_ref[0]
        seg = seg_ref[0]
        row_pos = here * rows + i * tq + lax.broadcasted_iota(jnp.int32, (tq, tk), 0)
        lane = lax.broadcasted_iota(jnp.int32, (tq, tk), 1)

        def step(masked, t, carry):
            at = lax.div(t, per) ^ here
            off = pl.multiple_of(lax.rem(t, per) * tk, tk)
            new = []
            if masked:
                key_pos = t * tk + lane
                seen = (key_pos <= row_pos) & (key_pos >= seg)
            for h in range(heads):
                top, total, acc = carry[3 * h : 3 * h + 3]
                cols = slice(h * HEAD_DIM, (h + 1) * HEAD_DIM)
                vals = slice(width + h * HEAD_DIM, width + (h + 1) * HEAD_DIM)
                scores = dot_t(q_ref[0, :, cols], kv_ref[at, 0, pl.ds(off, tk), cols])
                if masked:
                    scores = jnp.where(seen, scores, NEG)
                new_top = jnp.maximum(top, jnp.max(scores, axis=1, keepdims=True))
                weights = jnp.exp(scores - new_top)
                fade = jnp.exp(top - new_top)
                total = total * fade + jnp.sum(weights, axis=1, keepdims=True)
                acc = acc * fade + dot(weights.astype(BF), kv_ref[at, 0, pl.ds(off, tk), vals])
                new += [new_top, total, acc]
            return tuple(new)

        carry = (
            jnp.full((tq, 1), NEG, F32),
            jnp.zeros((tq, 1), F32),
            jnp.zeros((tq, HEAD_DIM), F32),
        ) * heads
        b = [bounds_ref[s, i, n] for n in range(4)]
        carry = lax.fori_loop(b[0], b[1], functools.partial(step, True), carry)
        carry = lax.fori_loop(b[1], b[2], functools.partial(step, False), carry)
        carry = lax.fori_loop(b[2], b[3], functools.partial(step, True), carry)
        column = lax.broadcasted_iota(jnp.int32, (tq, 128), 1)
        lse = jnp.zeros((tq, 128), F32)
        outs = []
        for h in range(heads):
            top, total, acc = carry[3 * h : 3 * h + 3]
            outs.append(acc / total)
            lse = jnp.where(column == h, top + jnp.log(total), lse)
        result = jnp.concatenate(outs, axis=1)
        o_ref[0] = result
        low_ref[0] = result.astype(BF)
        lse_ref[0] = lse

    return pl.pallas_call(
        kernel,
        out_shape=(
            jax.ShapeDtypeStruct((seqs, rows, width), F32),
            jax.ShapeDtypeStruct((seqs, rows, width), BF),
            jax.ShapeDtypeStruct((seqs, rows, 128), F32),
        ),
        grid_spec=pltpu.PrefetchScalarGridSpec(
            num_scalar_prefetch=2,
            grid=(seqs, rows // tq),
            in_specs=[
                pl.BlockSpec((1, tq, width), lambda s, i, *_: (s, i, 0)),
                pl.BlockSpec((blocks, 1, rows, 2 * width), lambda s, i, *_: (0, s, 0, 0)),
                pl.BlockSpec((1, tq, 1), lambda s, i, *_: (s, i, 0)),
            ],
            out_specs=[
                pl.BlockSpec((1, tq, width), lambda s, i, *_: (s, i, 0)),
                pl.BlockSpec((1, tq, width), lambda s, i, *_: (s, i, 0)),
                pl.BlockSpec((1, tq, 128), lambda s, i, *_: (s, i, 0)),
            ],
        ),
        compiler_params=pltpu.CompilerParams(vmem_limit_bytes=48 * MB),
        name="attend_forward",
        cost_estimate=pl.CostEstimate(
            flops=int(2 * 2 * seqs * heads * rows * rows * 3.5 * HEAD_DIM * 4),
            bytes_accessed=16 * MB,
            transcendentals=int(seqs * heads * rows * rows * 3.5),
        ),
    )(ctx, bounds, queries, keys_values, starts)


def attend_backward(ctx, bounds, edges, queries, keys_values, grads, stats, starts):
    seqs, rows, width = queries.shape
    heads = width // HEAD_DIM
    blocks = keys_values.shape[0]
    tq, tk = min(512, rows), min(512, rows)
    per = rows // tk

    def kernel(ctx_ref, bounds_ref, edges_ref, q_ref, kv_ref, do_ref, stat_ref, seg_ref, dq_ref, dkv_ref, acc):
        s, t = pl.program_id(0), pl.program_id(1)
        here = ctx_ref[0]

        @pl.when(t == 0)
        def _():
            dq_ref[...] = jnp.zeros_like(dq_ref)

        acc[...] = jnp.zeros_like(acc)
        lane = lax.broadcasted_iota(jnp.int32, (tk, tq), 1)
        key_pos = t * tk + lax.broadcasted_iota(jnp.int32, (tk, tq), 0)

        def tile(masked, i):
            off = pl.multiple_of(i * tq, tq)
            if masked:
                row_pos = here * rows + off + lane
                seen = (key_pos <= row_pos) & (key_pos >= seg_ref[0, 0:1, pl.ds(off, tq)])
            for h in range(heads):
                cols = slice(h * HEAD_DIM, (h + 1) * HEAD_DIM)
                vals = slice(width + h * HEAD_DIM, width + (h + 1) * HEAD_DIM)
                q = q_ref[0, pl.ds(off, tq), cols]
                do = do_ref[0, pl.ds(off, tq), cols]
                k = kv_ref[0, 0, :, cols]
                v = kv_ref[0, 0, :, vals]
                scores = dot_t(k, q)
                weights = jnp.exp(scores - stat_ref[0, h : h + 1, pl.ds(off, tq)])
                if masked:
                    weights = jnp.where(seen, weights, 0.0)
                dweights = dot_t(v, do)
                dscores = weights * (dweights - stat_ref[0, heads + h : heads + h + 1, pl.ds(off, tq)])
                dscores = dscores.astype(BF)
                acc[h] += dot(dscores, q)
                acc[heads + h] += dot(weights.astype(BF), do)
                dq_ref[0, pl.ds(off, tq), cols] += dot_l(dscores, k)

        def step(i, carry):
            first = here * rows + i * tq
            clear = (edges_ref[s, i] <= t * tk) & (t * tk + tk - 1 <= first)

            @pl.when(clear)
            def _():
                tile(False, i)

            @pl.when(jnp.logical_not(clear))
            def _():
                tile(True, i)

            return carry

        lax.fori_loop(bounds_ref[s, t, 0], bounds_ref[s, t, 1], step, 0)
        dkv_ref[0, 0] = jnp.concatenate([acc[n] for n in range(2 * heads)], axis=1).astype(BF)

    return pl.pallas_call(
        kernel,
        out_shape=(
            jax.ShapeDtypeStruct((seqs, rows, width), F32),
            jax.ShapeDtypeStruct((blocks, seqs, rows, 2 * width), BF),
        ),
        grid_spec=pltpu.PrefetchScalarGridSpec(
            num_scalar_prefetch=3,
            grid=(seqs, blocks * per),
            in_specs=[
                pl.BlockSpec((1, rows, width), lambda s, t, *_: (s, 0, 0)),
                pl.BlockSpec((1, 1, tk, 2 * width), lambda s, t, c, *_: ((t // per) ^ c[0], s, t % per, 0)),
                pl.BlockSpec((1, rows, width), lambda s, t, *_: (s, 0, 0)),
                pl.BlockSpec((1, 8, rows), lambda s, t, *_: (s, 0, 0)),
                pl.BlockSpec((1, 1, rows), lambda s, t, *_: (s, 0, 0)),
            ],
            out_specs=[
                pl.BlockSpec((1, rows, width), lambda s, t, *_: (s, 0, 0)),
                pl.BlockSpec((1, 1, tk, 2 * width), lambda s, t, c, *_: ((t // per) ^ c[0], s, t % per, 0)),
            ],
            scratch_shapes=[pltpu.VMEM((2 * heads, tk, HEAD_DIM), F32)],
        ),
        compiler_params=pltpu.CompilerParams(vmem_limit_bytes=48 * MB),
        name="attend_backward",
        cost_estimate=pl.CostEstimate(
            flops=int(5 * 2 * seqs * heads * rows * rows * 3.5 * HEAD_DIM * 4),
            bytes_accessed=32 * MB,
            transcendentals=int(seqs * heads * rows * rows * 3.5),
        ),
    )(ctx, bounds, edges, queries, keys_values, grads, stats, starts)


def gated_mlp(rows_in, rows_in_t, grads, grads_t, gates, w_in, w_out, y_before, dx_before):
    count, width = rows_in.shape
    hidden = w_out.shape[0]
    tile = min(256, hidden)
    chunk = min(512, count)
    steps = hidden // tile
    first = y_before is None

    def kernel(*refs):
        x_ref, xt_ref, d_ref, dt_ref, c_ref, wg_ref, wu_ref, wo_ref = refs[:8]
        refs = refs[8:]
        if not first:
            yb_ref, dxb_ref = refs[:2]
            refs = refs[2:]
        y_ref, dx_ref, dc_ref, din_ref, dout_ref, a_s, g_s, u_s = refs
        j = pl.program_id(0)

        @pl.when(j == 0)
        def _():
            dc_ref[...] = jnp.zeros_like(dc_ref)
            if first:
                y_ref[...] = jnp.zeros_like(y_ref)
                dx_ref[...] = jnp.zeros_like(dx_ref)
            else:
                y_ref[...] = yb_ref[...]
                dx_ref[...] = dxb_ref[...]

        def body(n, carry):
            at = pl.ds(pl.multiple_of(n * chunk, chunk), chunk)
            x = x_ref[at, :]
            gate = dot(x, wg_ref[...])
            up = dot(x, wu_ref[...])
            raw = dot_t(d_ref[at, :], wo_ref[...])
            c = c_ref[at, :]
            sig = 1.0 / (1.0 + jnp.exp(-gate))
            silu = gate * sig
            act = silu * up
            dc_ref[at, :] += jnp.sum(act * raw, axis=1, keepdims=True)
            back = raw * c
            a_low = (act * c).astype(BF)
            dg = (back * up * (sig + silu * (1.0 - sig))).astype(BF)
            du = (back * silu).astype(BF)
            a_s[at, :] = a_low
            g_s[at, :] = dg
            u_s[at, :] = du
            y_ref[at, :] += dot(a_low, wo_ref[...])
            dx_ref[at, :] += dot_t(dg, wg_ref[...]) + dot_t(du, wu_ref[...])
            return carry

        lax.fori_loop(0, count // chunk, body, 0)
        part = min(256, width)

        def weights(n, carry):
            at = pl.ds(pl.multiple_of(n * part, part), part)
            xt = xt_ref[at, :]
            din_ref[0, at, :] = dot(xt, g_s[...]).astype(BF)
            din_ref[1, at, :] = dot(xt, u_s[...]).astype(BF)
            return carry

        lax.fori_loop(0, width // part, weights, 0)
        for n in range(width // part):
            dout_ref[:, n * part : (n + 1) * part] = dot(dt_ref[n * part : (n + 1) * part, :], a_s[...]).T.astype(BF)

    once = pl.Buffered(1)
    whole = lambda *shape: pl.BlockSpec(shape, lambda j: (0,) * len(shape), pipeline_mode=once)
    in_specs = [
        whole(count, width),
        whole(width, count),
        whole(count, width),
        whole(width, count),
        whole(count, 1),
        pl.BlockSpec((width, tile), lambda j: (0, j)),
        pl.BlockSpec((width, tile), lambda j: (0, j + steps)),
        pl.BlockSpec((tile, width), lambda j: (j, 0)),
    ]
    operands = [rows_in, rows_in_t, grads, grads_t, gates, w_in, w_in, w_out]
    if not first:
        in_specs += [whole(count, width), whole(count, width)]
        operands += [y_before, dx_before]
    return pl.pallas_call(
        kernel,
        out_shape=(
            jax.ShapeDtypeStruct((count, width), F32),
            jax.ShapeDtypeStruct((count, width), F32),
            jax.ShapeDtypeStruct((count, 1), F32),
            jax.ShapeDtypeStruct((2, width, hidden), BF),
            jax.ShapeDtypeStruct((hidden, width), BF),
        ),
        grid=(steps,),
        in_specs=in_specs,
        out_specs=[
            whole(count, width),
            whole(count, width),
            whole(count, 1),
            pl.BlockSpec((2, width, tile), lambda j: (0, 0, j)),
            pl.BlockSpec((tile, width), lambda j: (j, 0)),
        ],
        scratch_shapes=[pltpu.VMEM((count, tile), BF)] * 3,
        compiler_params=pltpu.CompilerParams(vmem_limit_bytes=60 * MB),
        name="gated_mlp",
        cost_estimate=pl.CostEstimate(
            flops=9 * 2 * count * width * hidden,
            bytes_accessed=40 * MB,
            transcendentals=count * hidden,
        ),
    )(*operands)


def inverse_rms(values):
    return lax.rsqrt(jnp.mean(values * values, axis=-1, keepdims=True) + EPS)


def norm_back(values, inverse, gain, grad):
    scaled = grad * gain
    dotted = jnp.mean(scaled * values, axis=-1, keepdims=True)
    return inverse * scaled - values * (inverse * inverse * inverse) * dotted


def swap_halves(weight, heads):
    rows = weight.shape[0]
    pairs = weight.reshape(rows, heads, 2, HEAD_DIM // 2)
    return pairs[:, :, ::-1].reshape(rows, heads * HEAD_DIM)


def on_device(
    tokens,
    segment_ids,
    routes,
    cotangent,
    norm1_gain,
    qkv_weight,
    out_weight,
    norm2_gain,
    router_weight,
    shared_in,
    shared_out,
    expert_in,
    expert_out,
):
    local_len, seqs, width = tokens.shape
    count = local_len * seqs
    groups = lax.axis_size("head")
    ctxs = lax.axis_size("ctx")
    shards = lax.axis_size("fsdp")
    ctx = lax.axis_index("ctx")
    head = lax.axis_index("head")
    shard = lax.axis_index("fsdp")
    group_width = width // groups
    heads = group_width // HEAD_DIM
    block = local_len * groups
    span = seqs * block
    experts = expert_in.shape[0]
    ff = expert_in.shape[2] // 2
    fs = shared_in.shape[1] // 2
    fs_part = fs // ctxs
    ctx_word = ctx.astype(jnp.int32).reshape(1)

    x_own = tokens.transpose(1, 0, 2)
    x_line = line_gather(x_own, 1)
    small = jnp.concatenate([norm1_gain[None], norm2_gain[None], router_weight.T], axis=0)
    small = fsdp_gather(small, 1)
    gain_one, gain_two = small[0].astype(F32), small[1].astype(F32)
    w_router = small[2:]
    w_group = lax.dynamic_index_in_dim(qkv_weight.reshape(-1, 3, groups, group_width), head, 2, keepdims=False)
    w_group = fsdp_gather(w_group.reshape(-1, 3 * group_width), 0)
    w_rot = w_group[:, : 2 * group_width]
    w_all = jnp.concatenate([w_rot, swap_halves(w_rot, 2 * heads), w_group[:, 2 * group_width :]], axis=1)

    dz_own = cotangent.transpose(1, 0, 2).reshape(count, width)
    dz_all = jnp.concatenate(ctx_gather(dz_own), axis=0)
    w_attn = fsdp_gather(out_weight, 0)
    w_expert_in = fsdp_gather(lax.dynamic_index_in_dim(expert_in, ctx, 0, keepdims=False), 0)
    w_expert_out = fsdp_gather(lax.dynamic_index_in_dim(expert_out, ctx, 0, keepdims=False), 0)
    piece = fs // shards // ctxs
    s_in = shared_in.reshape(-1, 2, shards, ctxs, piece)
    s_in = lax.dynamic_index_in_dim(s_in, ctx, 3, keepdims=False).reshape(-1, 2 * fs_part)
    w_shared_in = fsdp_gather(s_in, 0)
    w_shared_out = fsdp_gather(lax.dynamic_slice_in_dim(shared_out, ctx * piece, piece, 0), 0)

    index = jnp.arange(HEAD_DIM // 2).astype(F32)
    freq = jnp.exp(-math.log(ROPE_BASE) * 2.0 * index / HEAD_DIM)
    position = ctx * block + jnp.arange(block, dtype=jnp.int32)
    angle = position.astype(F32)[:, None] * freq[None, :]
    cosine, sine = jnp.cos(angle), jnp.sin(angle)
    cos_all = jnp.tile(cosine, (1, 4 * heads))[None]
    sin_all = jnp.tile(jnp.concatenate([-sine, sine], axis=1), (1, 2 * heads))[None]

    x_f = x_line.astype(F32)
    inverse_one = inverse_rms(x_f)
    normed = (x_f * inverse_one * gain_one).astype(BF)
    mixed = dot(normed.reshape(span, width), w_all).reshape(seqs, block, 5 * group_width)
    rot = 2 * group_width
    rotated = mixed[:, :, :rot] * cos_all + mixed[:, :, rot : 2 * rot] * sin_all
    queries = rotated[:, :, :group_width].astype(BF) * jnp.asarray(HEAD_DIM**-0.5, BF)
    key_value = jnp.concatenate([rotated[:, :, group_width:], mixed[:, :, 2 * rot :]], axis=2).astype(BF)
    kv_all = jnp.stack(ctx_gather(key_value))

    def forward_bounds(tq, tk):
        nq = block // tq
        first = ctx * block + jnp.arange(nq, dtype=jnp.int32) * tq
        low = segment_ids[:, ::tq] // tk
        last_start = segment_ids[:, tq - 1 :: tq]
        clear_to = jnp.broadcast_to(first // tk, low.shape)
        clear_from = jnp.minimum((last_start + tk - 1) // tk, clear_to)
        clear_from = jnp.maximum(clear_from, low)
        clear_to = jnp.maximum(clear_to, clear_from)
        high = jnp.broadcast_to((first + tq - 1) // tk + 1, low.shape)
        return jnp.stack([low, clear_from, clear_to, high], axis=2).astype(jnp.int32)

    attended, attended_low, lse = attend_forward(
        ctx_word,
        forward_bounds(min(256, block), min(512, block)),
        queries,
        kv_all,
        segment_ids[:, :, None],
    )
    sent = attended_low.reshape(seqs, groups, local_len, group_width)
    back = lax.all_to_all(sent, "head", split_axis=1, concat_axis=3, tiled=True)
    attn_rows = back.reshape(count, width)

    x_rows = x_own.reshape(count, width).astype(F32)
    hidden = x_rows + dot(attn_rows, w_attn)
    inverse_two = inverse_rms(hidden)
    normed_two = (hidden * inverse_two * gain_two).astype(BF)
    route_rows = routes.reshape(local_len, seqs, 2).transpose(1, 0, 2).reshape(count, 2)
    logits = dot_t(normed_two, w_router)
    ids = jnp.arange(experts, dtype=jnp.int32)
    picks = (route_rows[:, :, None] == ids).astype(F32)
    chosen = jnp.sum(logits[:, None, :] * picks, axis=2)
    gate_first = 1.0 / (1.0 + jnp.exp(chosen[:, 1:] - chosen[:, :1]))
    gates = jnp.concatenate([gate_first, 1.0 - gate_first], axis=1)
    combine = jnp.sum(gates[:, :, None] * picks, axis=1)

    xn_all = jnp.concatenate(ctx_gather(normed_two), axis=0)
    combine_all = jnp.concatenate(ctx_gather(combine.T), axis=1)
    c_own = lax.dynamic_index_in_dim(combine_all, ctx, 0, keepdims=False)[:, None]
    xn_t = xn_all.T
    dz_t = dz_all.T
    y_part, dx_part, dc, ge_in, ge_out = gated_mlp(
        xn_all, xn_t, dz_all, dz_t, c_own, w_expert_in, w_expert_out, None, None
    )
    y_part, dx_part, _, gs_in, gs_out = gated_mlp(
        xn_all, xn_t, dz_all, dz_t, jnp.ones_like(c_own), w_shared_in, w_shared_out, y_part, dx_part
    )
    dc_blocks = dc.reshape(ctxs, count)
    dc_got = [dc_blocks[0]] + [
        lax.ppermute(dc_blocks[k], "ctx", [(i, i ^ k) for i in range(ctxs)]) for k in range(1, ctxs)
    ]
    dcombine = sum(
        dc_got[k][:, None] * ((ctx ^ k) == ids).astype(F32)[None, :] for k in range(ctxs)
    )
    dx_low = dx_part.astype(BF).reshape(ctxs, count, width)
    dxn2 = ctx_scatter([dx_low[k] for k in range(ctxs)])
    y_low = y_part.astype(BF).reshape(ctxs, count, width)
    y_own = ctx_scatter([y_low[k] for k in range(ctxs)])
    output = (hidden + y_own).astype(BF).reshape(seqs, local_len, width).transpose(1, 0, 2)

    dchosen = jnp.sum(dcombine[:, None, :] * picks, axis=2)
    dfirst = gates[:, :1] * gates[:, 1:] * (dchosen[:, :1] - dchosen[:, 1:])
    dlogits = (dfirst * (picks[:, 0] - picks[:, 1])).astype(BF)
    router_grad = dot_l(dlogits, normed_two)
    dxn2 = dxn2 + dot(dlogits, w_router)
    dz_rows = dz_own.astype(F32)
    dh = dz_rows + norm_back(hidden, inverse_two, gain_two, dxn2)
    gain_two_grad = jnp.sum(dxn2 * hidden * inverse_two, axis=0)
    dh_low = dh.astype(BF)
    g_attn = dot_l(attn_rows, dh_low).astype(BF)
    dattn = dot_t(dh_low, w_attn).astype(BF).reshape(seqs, local_len, width)
    grad_out = lax.all_to_all(
        dattn.reshape(seqs, local_len, groups, group_width), "head", split_axis=2, concat_axis=1, tiled=True
    ).reshape(seqs, block, group_width)

    delta = jnp.sum((grad_out.astype(F32) * attended).reshape(seqs, block, heads, HEAD_DIM), axis=3)
    stats = jnp.concatenate(
        [lse[:, :, :heads].transpose(0, 2, 1), delta.transpose(0, 2, 1), jnp.zeros((seqs, 8 - 2 * heads, block), F32)],
        axis=1,
    )
    tq = tk = min(512, block)
    tile_last = ctx * block + (jnp.arange(block // tq, dtype=jnp.int32) + 1) * tq - 1
    tile_key = jnp.arange(ctxs * block // tk, dtype=jnp.int32)
    q_low = jnp.sum((tile_last[None, :] < (tile_key * tk)[:, None]).astype(jnp.int32), axis=1)
    q_high = jnp.sum(((segment_ids[:, ::tq] // tk)[:, None, :] <= tile_key[None, :, None]).astype(jnp.int32), axis=2)
    q_low = jnp.broadcast_to(q_low, q_high.shape)
    back_bounds = jnp.stack([q_low, q_high], axis=2).astype(jnp.int32)
    dq, dkv_parts = attend_backward(
        ctx_word,
        back_bounds,
        segment_ids[:, tq - 1 :: tq],
        queries,
        kv_all,
        grad_out,
        stats,
        segment_ids[:, None, :],
    )
    dkv = ctx_scatter([dkv_parts[k] for k in range(ctxs)])
    dq = dq * (HEAD_DIM**-0.5)
    d_rot = jnp.concatenate([dq, dkv[:, :, :group_width]], axis=2).astype(BF).astype(F32)
    d_all = jnp.concatenate(
        [d_rot * cos_all, d_rot * sin_all, dkv[:, :, group_width:]], axis=2
    ).astype(BF).reshape(span, 5 * group_width)
    dxn1_part = dot_t(d_all, w_all).reshape(seqs, block, width)
    g_all = dot_l(normed.reshape(span, width), d_all)
    g_rot = g_all[:, :rot] + swap_halves(g_all[:, rot : 2 * rot], 2 * heads)
    g_qkv = jnp.concatenate([g_rot, g_all[:, 2 * rot :]], axis=1).astype(BF)
    gain_one_grad = jnp.sum(dxn1_part * x_f * inverse_one, axis=(0, 1))
    dxn1 = line_scatter(dxn1_part.astype(BF), 1).reshape(count, width)
    dx_norm = norm_back(x_rows, inverse_rms(x_rows), gain_one, dxn1)
    tokens_grad = (dh + dx_norm).reshape(seqs, local_len, width).transpose(1, 0, 2)

    def share(grad, axis, split):
        part = fsdp_scatter(grad, axis)
        part = line_scatter(part, split).astype(BF)
        return line_gather(part, split)

    def place(blocks, shape):
        out = jnp.zeros((ctxs,) + shape, F32)
        for k, blk in enumerate(blocks):
            out = lax.dynamic_update_slice_in_dim(out, blk.astype(F32).reshape((1,) + shape), ctx ^ k, 0)
        return out

    ge_in = ctx_gather(share(ge_in, 1, 1))
    ge_out = ctx_gather(share(ge_out, 0, 0))
    gs_in = ctx_gather(share(gs_in, 1, 1))
    gs_out = ctx_gather(share(gs_out, 0, 0))
    rows_per = width // shards
    expert_in_grad = place([g.transpose(1, 0, 2) for g in ge_in], (rows_per, 2 * ff))
    expert_out_grad = place(ge_out, (ff // shards, width))
    shared_in_grad = place(gs_in, (2, rows_per, shards, piece)).transpose(2, 1, 3, 0, 4).reshape(rows_per, 2 * fs)
    shared_out_grad = place(gs_out, (piece, width)).reshape(fs // shards, width)

    g_qkv = fsdp_scatter(g_qkv, 0)
    g_qkv = lax.psum(g_qkv, "ctx")
    g_qkv = line_gather(g_qkv[:, None], 1).astype(F32)
    qkv_grad = g_qkv.reshape(rows_per, groups, 3, group_width).transpose(0, 2, 1, 3).reshape(rows_per, 3 * width)
    g_attn = fsdp_scatter(g_attn, 0)
    out_grad = lax.psum(g_attn, ("ctx", "head")).astype(F32)
    tiny = jnp.concatenate([gain_one_grad[None], gain_two_grad[None], router_grad], axis=0)
    tiny = lax.psum(tiny, ("fsdp", "ctx", "head"))
    tiny = lax.dynamic_slice_in_dim(tiny, shard * rows_per, rows_per, 1)
    return (
        output,
        tokens_grad,
        tiny[0],
        qkv_grad,
        out_grad,
        tiny[1],
        tiny[2:].T,
        shared_in_grad,
        shared_out_grad,
        expert_in_grad,
        expert_out_grad,
    )


def solution(mesh):
    rows = P(("ctx", "head"), "fsdp", None)
    vector = P("fsdp")
    matrix = P("fsdp", None)
    stack = P(None, "fsdp", None)
    return jax.shard_map(
        on_device,
        mesh=mesh,
        in_specs=(
            rows,
            P("fsdp", "ctx"),
            P(("ctx", "head"), "fsdp", None, None),
            rows,
            vector,
            matrix,
            matrix,
            vector,
            matrix,
            matrix,
            matrix,
            stack,
            stack,
        ),
        out_specs=(rows, rows, vector, matrix, matrix, vector, matrix, matrix, matrix, stack, stack),
        check_vma=False,
    )
```

```python
import functools
import math

import jax
import jax.numpy as jnp
from jax import lax
from jax.experimental import pallas as pl
from jax.experimental.pallas import tpu as pltpu
from jax.sharding import PartitionSpec as P

HEAD_DIM = 64
EPS = 1e-06
NEG = -1e30
ROPE_BASE = 10000.0
BF = jnp.bfloat16
F32 = jnp.float32
MB = 1 << 20


def swap_with(value, axis_name, bit):
    size = lax.axis_size(axis_name)
    return lax.ppermute(value, axis_name, [(i, i ^ bit) for i in range(size)])


def fsdp_gather(value, axis):
    return lax.all_gather(value, "fsdp", axis=axis, tiled=True)


def fsdp_gather_small(value, axis):
    if lax.axis_size("fsdp") != 2:
        return fsdp_gather(value, axis)
    other = swap_with(value, "fsdp", 1)
    first = lax.axis_index("fsdp") == 0
    return jnp.where(
        first, jnp.concatenate([value, other], axis=axis), jnp.concatenate([other, value], axis=axis)
    )


def line_gather(value, axis):
    count = lax.axis_size("head")
    mine = lax.axis_index("head")
    part = value.shape[axis]
    up = [(i, i + 1) for i in range(count - 1)]
    down = [(i + 1, i) for i in range(count - 1)]
    below, above = [], []
    rising, falling = value, value
    for _ in range(count - 1):
        rising = lax.ppermute(rising, "head", up)
        falling = lax.ppermute(falling, "head", down)
        below.insert(0, rising)
        above.append(falling)
    line = jnp.concatenate(below + [value] + above, axis=axis)
    return lax.dynamic_slice_in_dim(line, (count - 1 - mine) * part, count * part, axis)


def line_scatter(value, axis):
    count = lax.axis_size("head")
    mine = lax.axis_index("head")
    part = value.shape[axis] // count
    up = [(i, i + 1) for i in range(count - 1)]
    down = [(i + 1, i) for i in range(count - 1)]

    def block(index):
        index = jnp.clip(index, 0, count - 1)
        return lax.dynamic_slice_in_dim(value, index * part, part, axis).astype(F32)

    rising, falling = None, None
    for step in range(count - 1):
        upward = block(count - 1 - step + mine)
        downward = block(step - (count - 1) + mine)
        if step:
            upward = upward + rising.astype(F32)
            downward = downward + falling.astype(F32)
        rising = lax.ppermute(upward.astype(BF), "head", up)
        falling = lax.ppermute(downward.astype(BF), "head", down)
    return block(mine) + rising.astype(F32) + falling.astype(F32)


def after(value, *others):
    return lax.optimization_barrier((value, *others))[0] if others else value


def corner(value):
    return lax.slice(value, (0,) * value.ndim, (1,) * value.ndim)


def paired():
    return lax.axis_size("fsdp") == 2


def group_member():
    ctx = lax.axis_index("ctx")
    return (ctx // 2) * 2 + lax.axis_index("fsdp") if paired() else ctx


def group_swap(value, bit):
    if paired() and bit == 1:
        return swap_with(value, "fsdp", 1)
    return swap_with(value, "ctx", bit)


def group_gather(value):
    half = value.shape[0] // 2
    one, two = group_swap(value, 1), group_swap(value, 2)
    far = jnp.concatenate([group_swap(one[:half], 2), group_swap(two[half:], 1)], axis=0)
    return [value, one, two, far]


def group_scatter_near(blocks):
    own, one, two, far = blocks
    half = far.shape[0] // 2
    by_one, by_two = group_swap(far[:half], 1), group_swap(far[half:], 2)
    two = jnp.concatenate([(two[:half].astype(F32) + by_one.astype(F32)).astype(BF), two[half:]], axis=0)
    one = jnp.concatenate([one[:half], (one[half:].astype(F32) + by_two.astype(F32)).astype(BF)], axis=0)
    return own, one, two


def group_scatter(blocks):
    own, one, two = group_scatter_near(blocks)
    return own.astype(F32) + group_swap(one, 1).astype(F32) + group_swap(two, 2).astype(F32)


def half_sum(value, axis, axis_name, bit_value, bit):
    part = value.shape[axis] // 2
    sent = lax.dynamic_slice_in_dim(value, (1 - bit_value) * part, part, axis)
    kept = lax.dynamic_slice_in_dim(value, bit_value * part, part, axis)
    got = swap_with(sent, axis_name, bit)
    return kept.astype(F32) + got.astype(F32)


def pack(d_in, d_out, parts, wide):
    packed = []
    for d in (d_in, d_out):
        j, r, w = d.shape
        d = d.reshape(j, parts, r // parts, w // wide, wide).transpose(1, 0, 3, 2, 4)
        packed.append(d.reshape(parts, j, -1, wide))
    return jnp.concatenate(packed, axis=2)


def sum_parts(one, two, more=None):
    wide = 256
    groups, shards = lax.axis_size("head"), lax.axis_size("fsdp")
    if paired():
        parts, over = groups, "head"
        packed = one.astype(F32) + swap_with(two, "ctx", 1).astype(F32)
        packed = packed.astype(BF).reshape(parts, -1, wide)
        if more is not None:
            more = half_sum(more, 1, "ctx", lax.axis_index("ctx") % 2, 1).astype(BF)
    else:
        parts, over = groups * shards, ("fsdp", "head")
        packed = pack(one, two, parts, wide).reshape(parts, -1, wide)
    if more is not None:
        j, r, w = more.shape
        more = more.reshape(j, parts, r // parts, w // wide, wide).transpose(1, 0, 3, 2, 4)
        packed = jnp.concatenate([packed, more.reshape(parts, -1, wide)], axis=1)
    packed = packed.reshape(-1, wide)
    return lax.psum_scatter(packed, over, scatter_dimension=0, tiled=True)


def exchange_parts(part):
    if not paired():
        return part
    core, shard = lax.axis_index("ctx") % 2, lax.axis_index("fsdp")
    ctxs = lax.axis_size("ctx")
    moves = [(f * ctxs + c, (1 - f) * ctxs + (c ^ 1)) for f in range(2) for c in range(ctxs) if c % 2 != f]
    got = lax.ppermute(part, ("fsdp", "ctx"), moves)
    return jnp.where(core == shard, part, got)


def share_parts(part):
    whole = lax.all_gather(part, ("ctx", "head"), axis=0, tiled=False)
    return whole.reshape((lax.axis_size("ctx"), lax.axis_size("head")) + part.shape)


def ctx_gather(value):
    blocks = [value]
    bit = lax.axis_size("ctx") // 2
    found = {0: value}
    while bit:
        for k in list(found):
            found[k ^ bit] = swap_with(found[k], "ctx", bit)
        bit //= 2
    blocks = [found[k] for k in range(len(found))]
    return blocks


def ctx_scatter(blocks):
    held = {k: blocks[k] for k in range(len(blocks))}
    bit = 1
    while len(held) > 1:
        kept = {}
        for k in list(held):
            if not k & bit:
                got = swap_with(held[k | bit], "ctx", bit)
                kept[k] = held[k].astype(F32) + got.astype(F32)
        held = {k: (v if len(kept) == 1 else v.astype(BF)) for k, v in kept.items()}
        bit *= 2
    return held[0]


MESH_ID = pl.DeviceIdType.MESH


def enter(partners):
    barrier = pltpu.get_barrier_semaphore()
    for there, device in partners:
        if there is None:
            pl.semaphore_signal(barrier, inc=1, device_id=device, device_id_type=MESH_ID)
        else:

            @pl.when(there)
            def _(device=device):
                pl.semaphore_signal(barrier, inc=1, device_id=device, device_id_type=MESH_ID)

    here = sum(1 if there is None else there.astype(jnp.int32) for there, _ in partners)
    pl.semaphore_wait(barrier, here)


def send(src, dst, sems, device):
    return pltpu.make_async_remote_copy(
        src_ref=src, dst_ref=dst, send_sem=sems[0], recv_sem=sems[1], device_id=device, device_id_type=MESH_ID
    )


def line_relay(place, z, count, up, down, up_sems, down_sems):
    def copy(b, device, sems):
        return send(place(b), place(b), (sems[0].at[b], sems[1].at[b]), device)

    def pass_on(far):
        low, high = z - far, z + far

        @pl.when((low >= 0) & (z < count - 1))
        def _():
            if far:
                copy(low, up, up_sems).wait_recv()
            copy(low, up, up_sems).start()

        @pl.when((high < count) & (z > 0))
        def _():
            if far:
                copy(high, down, down_sems).wait_recv()
            copy(high, down, down_sems).start()

    def last(b):
        @pl.when((b < z) & (z == count - 1))
        def _():
            copy(b, up, up_sems).wait_recv()

        @pl.when((b > z) & (z == 0))
        def _():
            copy(b, down, down_sems).wait_recv()

    def sent(b):
        @pl.when((b <= z) & (z < count - 1))
        def _():
            copy(b, up, up_sems).wait_send()

        @pl.when((b >= z) & (z > 0))
        def _():
            copy(b, down, down_sems).wait_send()

    blocks = range(count)
    run = [functools.partial(pass_on, far) for far in blocks]
    return run, [functools.partial(last, b) for b in blocks], [functools.partial(sent, b) for b in blocks]


def line_gather_kernel(value, cid):
    count = lax.axis_size("head")
    seqs, rows, width = value.shape

    def kernel(v_ref, o_ref, us, ur, ds, dr, local):
        z = lax.axis_index("head")
        up, down = {"head": jnp.minimum(z + 1, count - 1)}, {"head": jnp.maximum(z - 1, 0)}

        def place(b):
            return o_ref.at[:, pl.ds(pl.multiple_of(b * rows, rows), rows), :]

        own = pltpu.make_async_copy(v_ref, o_ref.at[:, pl.ds(pl.multiple_of(z * rows, rows), rows), :], local)
        own.start()
        enter([(z < count - 1, up), (z > 0, down)])
        own.wait()
        run, last, sent = line_relay(place, z, count, up, down, (us, ur), (ds, dr))
        for step in (*run, *last, *sent):
            step()

    any_space = pl.BlockSpec(memory_space=pltpu.VMEM)
    return pl.pallas_call(
        kernel,
        out_shape=jax.ShapeDtypeStruct((seqs, count * rows, width), value.dtype),
        in_specs=[any_space],
        out_specs=any_space,
        scratch_shapes=[pltpu.SemaphoreType.DMA((count,))] * 4 + [pltpu.SemaphoreType.DMA],
        compiler_params=pltpu.CompilerParams(
            collective_id=cid, has_side_effects=True, vmem_limit_bytes=16 * MB
        ),
        name="line_gather",
        cost_estimate=pl.CostEstimate(flops=0, bytes_accessed=180 * MB, transcendentals=0),
    )(value)


def tail_kernel(parts, grads, cid):
    count, rows, width = parts.shape
    high, wide = grads.shape
    half, quarter, eighth = high // 2, high // 4, high // 8

    def kernel(p_ref, g_ref, o_ref, q_ref, gain_ref, q_s, up_in, up_out, dn_in, dn_out, s1, r1, s2, r2, r3, *sems):
        us, ur, ds, dr, gus, gur, gds, gdr, xs, ys, cs, yg, cg = sems
        z, f, c = lax.axis_index("head"), lax.axis_index("fsdp"), lax.axis_index("ctx")
        core, upper = lax.rem(c, 2), lax.div(c, 2)
        up, down = {"head": jnp.minimum(z + 1, count - 1)}, {"head": jnp.maximum(z - 1, 0)}
        over_x = {"fsdp": 1 - f}
        over_core = {"ctx": upper * 2 + 1 - core}
        over_y = {"ctx": (1 - upper) * 2 + core}
        enter([(z < count - 1, up), (z > 0, down), (None, over_x), (None, over_core), (None, over_y)])

        def rise(d):
            return send(up_out.at[d], up_in.at[d], (us.at[d], ur.at[d]), up)

        def fall(d):
            return send(dn_out.at[d], dn_in.at[d], (ds.at[d], dr.at[d]), down)

        def rising(d):
            @pl.when(z < d)
            def _():
                @pl.when(z == 0)
                def _():
                    up_out[d] = p_ref[d]

                @pl.when(z > 0)
                def _():
                    rise(d).wait_recv()
                    up_out[d] = (p_ref[d].astype(F32) + up_in[d].astype(F32)).astype(BF)

                rise(d).start()

        def falling(d):
            @pl.when(z > d)
            def _():
                @pl.when(z == count - 1)
                def _():
                    dn_out[d] = p_ref[d]

                @pl.when(z < count - 1)
                def _():
                    fall(d).wait_recv()
                    dn_out[d] = (p_ref[d].astype(F32) + dn_in[d].astype(F32)).astype(BF)

                fall(d).start()

        by_x = send(g_ref.at[pl.ds(pl.multiple_of((1 - f) * half, half), half), :], r1, (xs.at[0], xs.at[1]), over_x)
        by_core = send(
            s1.at[pl.ds(pl.multiple_of((1 - core) * quarter, quarter), quarter), :], r2, (cs.at[0], cs.at[1]), over_core
        )
        by_y = send(
            s2.at[pl.ds(pl.multiple_of((1 - upper) * eighth, eighth), eighth), :], r3, (ys.at[0], ys.at[1]), over_y
        )
        by_x.start()
        at_low, at_high = z == 0, z == count - 1
        pl.when(at_low)(lambda: rising(count - 1))
        pl.when(at_high)(lambda: falling(0))
        by_x.wait_recv()
        s1[...] = (g_ref[pl.ds(pl.multiple_of(f * half, half), half), :].astype(F32) + r1[...].astype(F32)).astype(BF)
        by_core.start()
        by_core.wait_recv()
        mine = s1[pl.ds(pl.multiple_of(core * quarter, quarter), quarter), :]
        s2[...] = (mine.astype(F32) + r2[...].astype(F32)).astype(BF)
        by_y.start()
        by_y.wait_recv()
        mine = s2[pl.ds(pl.multiple_of(upper * eighth, eighth), eighth), :]
        q_s[core, upper, z] = (mine.astype(F32) + r3[...].astype(F32)).astype(BF)
        run, last, sent = line_relay(
            lambda b: q_s.at[core, upper, b], z, count, up, down, (gus, gur), (gds, gdr)
        )
        run[0]()
        for d in range(1, count - 1):
            pl.when(at_low)(lambda d=d: rising(count - 1 - d))
            pl.when(at_high)(lambda d=d: falling(d))
        pl.when(jnp.logical_not(at_low))(lambda: rising(count - 1))
        run[1]()
        pl.when(jnp.logical_not(at_high))(lambda: falling(0))
        run[2]()
        for d in range(1, count - 1):
            pl.when(jnp.logical_not(at_low))(lambda d=d: rising(count - 1 - d))
            pl.when(jnp.logical_not(at_high))(lambda d=d: falling(d))
        for step in (*run[3:], *last):
            step()
        to_y = send(q_s.at[core, upper], q_s.at[core, upper], (yg.at[0], yg.at[1]), over_y)
        to_y.start()

        total = p_ref[z].astype(F32)
        o_ref[...] = total

        @pl.when(z > 0)
        def _():
            rise(z).wait_recv()
            o_ref[...] += up_in[z].astype(F32)

        @pl.when(z < count - 1)
        def _():
            fall(z).wait_recv()
            o_ref[...] += dn_in[z].astype(F32)

        to_y.wait_recv()
        to_core = send(q_s.at[core], q_s.at[core], (cg.at[0], cg.at[1]), over_core)
        to_core.start()
        to_core.wait_recv()
        part = width // count
        for a in range(2):
            for b in range(2):
                at = slice((a * 2 + b) * eighth, (a * 2 + b + 1) * eighth)
                gain = jnp.zeros((eighth, 128), F32)
                for n in range(count):
                    block = q_s[a, b, n].astype(F32)
                    for t in range(3):
                        col = t * width + n * part
                        q_ref[at, col : col + part] = block[:, t * part : (t + 1) * part]
                    gain += block[:, wide - 128 :]
                gain_ref[at, :] = gain
        for d in range(count):

            @pl.when(z < d)
            def _(d=d):
                rise(d).wait_send()

            @pl.when(z > d)
            def _(d=d):
                fall(d).wait_send()

        for step in sent:
            step()
        for copy in (by_x, by_core, by_y, to_y, to_core):
            copy.wait_send()

    vmem = pl.BlockSpec(memory_space=pltpu.VMEM)
    block = lambda *shape: pltpu.VMEM(shape, BF)
    return pl.pallas_call(
        kernel,
        out_shape=(
            jax.ShapeDtypeStruct((rows, width), F32),
            jax.ShapeDtypeStruct((half, 3 * width), F32),
            jax.ShapeDtypeStruct((half, 128), F32),
        ),
        in_specs=[vmem, vmem],
        out_specs=[vmem, vmem, vmem],
        scratch_shapes=[block(2, 2, count, eighth, wide)]
        + [block(count, rows, width)] * 4
        + [block(half, wide), block(half, wide), block(quarter, wide), block(quarter, wide), block(eighth, wide)]
        + [pltpu.SemaphoreType.DMA((count,))] * 8
        + [pltpu.SemaphoreType.DMA((2,))] * 5,
        compiler_params=pltpu.CompilerParams(
            collective_id=cid, has_side_effects=True, vmem_limit_bytes=40 * MB
        ),
        name="tail",
        cost_estimate=pl.CostEstimate(flops=0, bytes_accessed=220 * MB, transcendentals=0),
    )(parts, grads)


def dot_t(a, b):
    return lax.dot_general(a, b, (((1,), (1,)), ((), ())), preferred_element_type=F32)


def dot_l(a, b):
    return lax.dot_general(a, b, (((0,), (0,)), ((), ())), preferred_element_type=F32)


def dot(a, b):
    return jnp.dot(a, b, preferred_element_type=F32)


def attend_forward(words, bounds, queries, keys_values, starts, tq, tk, state):
    seqs, rows, width = queries.shape
    heads = width // HEAD_DIM
    blocks = keys_values.shape[0]
    per = rows // tk

    def kernel(word_ref, bounds_ref, q_ref, kv_ref, seg_ref, *refs):
        if state is None:
            acc_ref, row_ref = refs
        else:
            acc_in, row_in, o_ref, low_ref, lse_ref = refs
        s, i = pl.program_id(0), pl.program_id(1)
        here, first = word_ref[0], word_ref[1]
        seg = seg_ref[0]
        row_pos = here * rows + i * tq + lax.broadcasted_iota(jnp.int32, (tk, tq), 1)
        under = lax.broadcasted_iota(jnp.int32, (tk, tq), 0)

        def step(masked, t, carry):
            at = (lax.div(t, per) ^ here) - first
            off = pl.multiple_of(lax.rem(t, per) * tk, tk)
            new = []
            if masked:
                key_pos = t * tk + under
                seen = (key_pos <= row_pos) & (key_pos >= seg)
            for h in range(heads):
                top, total, acc = carry[3 * h : 3 * h + 3]
                cols = slice(h * HEAD_DIM, (h + 1) * HEAD_DIM)
                vals = slice(width + h * HEAD_DIM, width + (h + 1) * HEAD_DIM)
                scores = dot_t(kv_ref[at, 0, pl.ds(off, tk), cols], q_ref[0, :, cols])
                if masked:
                    scores = jnp.where(seen, scores, NEG)
                new_top = jnp.maximum(top, jnp.max(scores, axis=0, keepdims=True))
                weights = jnp.exp(scores - new_top)
                fade = jnp.exp(top - new_top)
                total = total * fade + jnp.sum(weights, axis=0, keepdims=True)
                acc = acc * fade + dot_l(kv_ref[at, 0, pl.ds(off, tk), vals], weights.astype(BF))
                new += [new_top, total, acc]
            return tuple(new)

        carry = []
        for h in range(heads):
            if state is None:
                carry += [jnp.full((1, tq), NEG, F32), jnp.zeros((1, tq), F32), jnp.zeros((HEAD_DIM, tq), F32)]
            else:
                carry += [
                    row_in[0, h : h + 1, :],
                    row_in[0, heads + h : heads + h + 1, :],
                    acc_in[0, h * HEAD_DIM : (h + 1) * HEAD_DIM, :],
                ]
        carry = tuple(carry)
        b = [bounds_ref[s, i, n] for n in range(4)]
        carry = lax.fori_loop(b[0], b[1], functools.partial(step, True), carry)
        carry = lax.fori_loop(b[1], b[2], functools.partial(step, False), carry)
        carry = lax.fori_loop(b[2], b[3], functools.partial(step, True), carry)
        tops, totals, accs = carry[::3], carry[1::3], carry[2::3]
        filler = jnp.zeros((8 - 2 * heads, tq), F32)
        if state is None:
            acc_ref[0] = jnp.concatenate(accs, axis=0)
            row_ref[0] = jnp.concatenate([*tops, *totals, filler], axis=0)
        else:
            result = jnp.concatenate([acc / total for acc, total in zip(accs, totals)], axis=0).T
            o_ref[0] = result
            low_ref[0] = result.astype(BF)
            logs = [top + jnp.log(total) for top, total in zip(tops, totals)]
            lse_ref[0] = jnp.concatenate([*logs, *totals, filler], axis=0)

    rows_spec = pl.BlockSpec((1, tq, width), lambda s, i, *_: (s, i, 0))
    acc_spec = pl.BlockSpec((1, width, tq), lambda s, i, *_: (s, 0, i))
    stat_spec = pl.BlockSpec((1, 8, tq), lambda s, i, *_: (s, 0, i))
    stat_shape = jax.ShapeDtypeStruct((seqs, 8, rows), F32)
    if state is None:
        out_shape = (jax.ShapeDtypeStruct((seqs, width, rows), F32), stat_shape)
        more, out_specs = [], [acc_spec, stat_spec]
    else:
        shape = (seqs, rows, width)
        out_shape = (jax.ShapeDtypeStruct(shape, F32), jax.ShapeDtypeStruct(shape, BF), stat_shape)
        more, out_specs = [acc_spec, stat_spec], [rows_spec, rows_spec, stat_spec]
    return pl.pallas_call(
        kernel,
        out_shape=out_shape,
        grid_spec=pltpu.PrefetchScalarGridSpec(
            num_scalar_prefetch=2,
            grid=(seqs, rows // tq),
            in_specs=[
                rows_spec,
                pl.BlockSpec((blocks, 1, rows, 2 * width), lambda s, i, *_: (0, s, 0, 0)),
                pl.BlockSpec((1, 1, tq), lambda s, i, *_: (s, 0, i)),
                *more,
            ],
            out_specs=out_specs,
        ),
        compiler_params=pltpu.CompilerParams(vmem_limit_bytes=48 * MB),
        name="attend_forward",
        cost_estimate=pl.CostEstimate(
            flops=int(2 * 2 * seqs * heads * rows * rows * 2 * HEAD_DIM * 4),
            bytes_accessed=64 * MB,
            transcendentals=int(seqs * heads * rows * rows * 2),
        ),
    )(words, bounds, queries, keys_values, starts, *(state or ()))


def attend_backward(words, bounds, edges, queries, keys_values, grads, stats, starts, tq, tk):
    seqs, rows, width = queries.shape
    heads = width // HEAD_DIM
    blocks = keys_values.shape[0]
    per = rows // tk

    def kernel(word_ref, bounds_ref, edges_ref, q_ref, kv_ref, do_ref, stat_ref, seg_ref, dq_ref, dkv_ref, acc):
        s = pl.program_id(0)
        here = word_ref[0]
        t = word_ref[2] * per + pl.program_id(1)

        @pl.when(pl.program_id(1) == 0)
        def _():
            dq_ref[...] = jnp.zeros_like(dq_ref)

        acc[...] = jnp.zeros_like(acc)
        lane = lax.broadcasted_iota(jnp.int32, (tk, tq), 1)
        key_pos = t * tk + lax.broadcasted_iota(jnp.int32, (tk, tq), 0)

        def tile(masked, i):
            off = pl.multiple_of(i * tq, tq)
            if masked:
                row_pos = here * rows + off + lane
                seen = (key_pos <= row_pos) & (key_pos >= seg_ref[0, 0:1, pl.ds(off, tq)])
            for h in range(heads):
                cols = slice(h * HEAD_DIM, (h + 1) * HEAD_DIM)
                vals = slice(width + h * HEAD_DIM, width + (h + 1) * HEAD_DIM)
                q = q_ref[0, pl.ds(off, tq), cols]
                do = do_ref[0, pl.ds(off, tq), cols]
                k = kv_ref[0, 0, :, cols]
                v = kv_ref[0, 0, :, vals]
                scores = dot_t(k, q)
                weights = jnp.exp(scores - stat_ref[0, h : h + 1, pl.ds(off, tq)])
                if masked:
                    weights = jnp.where(seen, weights, 0.0)
                dweights = dot_t(v, do)
                dscores = weights * (dweights - stat_ref[0, heads + h : heads + h + 1, pl.ds(off, tq)])
                dscores = dscores.astype(BF)
                acc[h] += dot(dscores, q)
                acc[heads + h] += dot(weights.astype(BF), do)
                dq_ref[0, pl.ds(off, tq), cols] += dot_l(dscores, k)

        def step(i, carry):
            first = here * rows + i * tq
            clear = (edges_ref[s, i] <= t * tk) & (t * tk + tk - 1 <= first)

            @pl.when(clear)
            def _():
                tile(False, i)

            @pl.when(jnp.logical_not(clear))
            def _():
                tile(True, i)

            return carry

        lax.fori_loop(bounds_ref[s, t, 0], bounds_ref[s, t, 1], step, 0)
        dkv_ref[0, 0] = jnp.concatenate([acc[n] for n in range(2 * heads)], axis=1).astype(BF)

    at = lambda s, t, w, *_: (((w[2] + t // per) ^ w[0]) - w[1], s, t % per, 0)
    return pl.pallas_call(
        kernel,
        out_shape=(
            jax.ShapeDtypeStruct((seqs, rows, width), F32),
            jax.ShapeDtypeStruct((blocks, seqs, rows, 2 * width), BF),
        ),
        grid_spec=pltpu.PrefetchScalarGridSpec(
            num_scalar_prefetch=3,
            grid=(seqs, blocks * per),
            in_specs=[
                pl.BlockSpec((1, rows, width), lambda s, t, *_: (s, 0, 0)),
                pl.BlockSpec((1, 1, tk, 2 * width), at),
                pl.BlockSpec((1, rows, width), lambda s, t, *_: (s, 0, 0)),
                pl.BlockSpec((1, 8, rows), lambda s, t, *_: (s, 0, 0)),
                pl.BlockSpec((1, 1, rows), lambda s, t, *_: (s, 0, 0)),
            ],
            out_specs=[
                pl.BlockSpec((1, rows, width), lambda s, t, *_: (s, 0, 0)),
                pl.BlockSpec((1, 1, tk, 2 * width), at),
            ],
            scratch_shapes=[pltpu.VMEM((2 * heads, tk, HEAD_DIM), F32)],
        ),
        compiler_params=pltpu.CompilerParams(vmem_limit_bytes=48 * MB),
        name="attend_backward",
        cost_estimate=pl.CostEstimate(
            flops=int(5 * 2 * seqs * heads * rows * rows * 2 * HEAD_DIM * 4),
            bytes_accessed=100 * MB,
            transcendentals=int(seqs * heads * rows * rows * 2),
        ),
    )(words, bounds, edges, queries, keys_values, grads, stats, starts)


def gated_mlp(rows_in, grads, grads_t, gates, words, routed, shared, steps, s_steps, groups):
    block_rows, width = rows_in[0].shape
    n_rows = len(rows_in)
    count = block_rows * n_rows
    tile = 256
    chunk = min(512, count)
    all_steps = steps + s_steps
    pieces = [(piece, held, where) for where, lists in enumerate((routed, shared)) for held in (0, 1) for piece in lists[held]]

    def kernel(word_ref, *refs):
        row_refs, refs = refs[:n_rows], refs[n_rows:]
        d_ref, dt_ref, c_in = refs[:3]
        piece_refs, refs = refs[3 : 3 + len(pieces)], refs[3 + len(pieces) :]
        y_out, dx_out, dc_ref, one_ref, two_ref, x_ref, xt_ref, c_ref, y_ref, dx_ref, w_s, wt_s, wo_s, wot_s, a_s, g_s = refs
        j = pl.program_id(0)

        @pl.when(j == 0)
        def _():
            dc_ref[...] = jnp.zeros_like(dc_ref)
            c_ref[...] = c_in[...]
            y_ref[...] = jnp.zeros_like(y_ref)
            dx_ref[...] = jnp.zeros_like(dx_ref)
            for n, ref in enumerate(row_refs):
                at = slice(n * block_rows, (n + 1) * block_rows)
                x_ref[at, :] = ref[...]
                xt_ref[:, at] = ref[...].T

        @pl.when(j == steps)
        def _():
            c_ref[...] = jnp.ones_like(c_ref)

        def fill(kind):
            for ref, (piece, held, where) in zip(piece_refs, pieces):
                if where != kind:
                    continue
                tall, wide = ref.shape
                row, times, lane_word, lane_times, lane = piece[3:]
                at = pl.ds(pl.multiple_of(word_ref[row], times), tall)
                if lane_word is None:
                    lanes = slice(lane, lane + wide)
                else:
                    lanes = pl.ds(pl.multiple_of(word_ref[lane_word], lane_times), wide)
                (w_s, wo_s)[held][at, lanes] = ref[...]

        pl.when(j < steps)(lambda: fill(0))
        pl.when(j >= steps)(lambda: fill(1))
        wt_s[...] = w_s[...].T
        wot_s[...] = wo_s[...].T

        routed_here = jnp.where(j < steps, 1.0, 0.0)

        def body(n, carry):
            at = pl.ds(pl.multiple_of(n * chunk, chunk), chunk)
            both = dot(x_ref[at, :], w_s[...])
            gate, up = both[:, :tile], both[:, tile:]
            raw = dot(d_ref[at, :], wot_s[...])
            c = c_ref[at, :]
            sig = 0.5 + 0.5 * jnp.tanh(0.5 * gate)
            silu = gate * sig
            act = silu * up

            dc_ref[at, :] += jnp.sum(act * raw, axis=1, keepdims=True) * routed_here
            back = raw * c
            a_low = (act * c).astype(BF)
            dg = (back * up * (sig + silu * (1.0 - sig))).astype(BF)
            du = (back * silu).astype(BF)
            a_s[at, :] = a_low
            g_s[at, :tile] = dg
            g_s[at, tile:] = du
            y_ref[at, :] += dot(a_low, wo_s[...])
            dx_ref[at, :] += dot(g_s[at, :], wt_s[...])
            return carry

        lax.fori_loop(0, count // chunk, body, 0)

        if groups:
            keep = word_ref[1]
            half = width // 2
            r, q = half // groups, tile // 2 // groups
            for ref, which in ((one_ref, keep), (two_ref, 1 - keep)):
                got = dot(xt_ref[pl.ds(pl.multiple_of(which * half, half), half), :], g_s[...]).astype(BF)
                for z in range(groups):
                    for g in range(2):
                        ref[z, 0, g * r : (g + 1) * r, :] = got[z * r : (z + 1) * r, g * tile : (g + 1) * tile]
            for n in range(width // tile):
                got = dot(dt_ref[n * tile : (n + 1) * tile, :], a_s[...]).T.astype(BF)
                low, high = got[: tile // 2], got[tile // 2 :]
                for ref, which in ((one_ref, keep), (two_ref, 1 - keep)):
                    mine = jnp.where(which == 0, low, high)
                    for z in range(groups):
                        ref[z, 0, 2 * r + n * q : 2 * r + (n + 1) * q, :] = mine[z * q : (z + 1) * q]
        else:
            one_ref[0] = dot(xt_ref[...], g_s[...]).astype(BF)
            for n in range(width // tile):
                at = slice(n * tile, (n + 1) * tile)
                two_ref[0, :, at] = dot(dt_ref[at, :], a_s[...]).T.astype(BF)

        @pl.when(j == all_steps - 1)
        def _():
            y_out[...] = y_ref[...].astype(BF)
            dx_out[...] = dx_ref[...].astype(BF)

    once = pl.Buffered(1)
    whole = lambda *shape: pl.BlockSpec(shape, lambda j, *_: (0,) * len(shape), pipeline_mode=once)

    def piece_spec(piece, where):
        index = piece[2]
        if where == 0:
            return pl.BlockSpec(piece[1], lambda j, w: index(jnp.minimum(j, steps - 1), w))
        return pl.BlockSpec(piece[1], lambda j, w: index(jnp.maximum(j - steps, 0), w))

    in_specs = [whole(block_rows, width)] * n_rows + [whole(count, width), whole(width, count), whole(count, 1)]
    in_specs += [piece_spec(piece, where) for piece, _, where in pieces]
    operands = [*rows_in, grads, grads_t, gates, *(piece[0] for piece, _, _ in pieces)]
    if groups:
        rows = width // groups + 3 * tile // 2 // groups
        grad_shape = [(groups, all_steps, rows, tile)] * 2
        grad_spec = [pl.BlockSpec((groups, 1, rows, tile), lambda j, *_: (0, j, 0, 0))] * 2
    else:
        grad_shape = [(all_steps, width, 2 * tile), (all_steps, tile, width)]
        grad_spec = [pl.BlockSpec((1,) + shape[1:], lambda j, *_: (j, 0, 0)) for shape in grad_shape]
    return pl.pallas_call(
        kernel,
        out_shape=(
            jax.ShapeDtypeStruct((count, width), BF),
            jax.ShapeDtypeStruct((count, width), BF),
            jax.ShapeDtypeStruct((count, 1), F32),
            *(jax.ShapeDtypeStruct(shape, BF) for shape in grad_shape),
        ),
        grid_spec=pltpu.PrefetchScalarGridSpec(
            num_scalar_prefetch=1,
            grid=(all_steps,),
            in_specs=in_specs,
            out_specs=[whole(count, width), whole(count, width), whole(count, 1), *grad_spec],
            scratch_shapes=[
                pltpu.VMEM((count, width), BF),
                pltpu.VMEM((width, count), BF),
                pltpu.VMEM((count, 1), F32),
                pltpu.VMEM((count, width), F32),
                pltpu.VMEM((count, width), F32),
                pltpu.VMEM((width, 2 * tile), BF),
                pltpu.VMEM((2 * tile, width), BF),
                pltpu.VMEM((tile, width), BF),
                pltpu.VMEM((width, tile), BF),
                pltpu.VMEM((count, tile), BF),
                pltpu.VMEM((count, 2 * tile), BF),
            ],
        ),
        compiler_params=pltpu.CompilerParams(vmem_limit_bytes=60 * MB),
        name="gated_mlp",
        cost_estimate=pl.CostEstimate(
            flops=9 * 2 * count * width * tile * all_steps,
            bytes_accessed=40 * MB,
            transcendentals=count * tile * all_steps,
        ),
    )(words, *operands)


def unpack(parts, shards, steps, s_steps, width):
    ctxs, groups, total, wide = parts.shape
    per = wide // shards
    r = width // shards // groups
    q = per // groups
    cols = width // wide
    tall = 2 * r + cols * q
    ff, piece = steps * wide, s_steps * per
    shapes = (
        (ctxs, groups * r, 2 * ff),
        (ctxs, steps * per, width),
        (groups * r, 2 * shards * ctxs * piece),
        (ctxs * piece, width),
    )
    if per % 128 or q % 16:
        made = parts[:, :, : (steps + s_steps) * tall].reshape(ctxs, groups, -1, tall, wide)
        d_in = made[:, :, :, : 2 * r].reshape(ctxs, groups, -1, 2, r, shards, per)
        d_out = made[:, :, :, 2 * r :].reshape(ctxs, groups, -1, cols, q, wide)
        e_in = d_in[:, :, :steps].transpose(0, 1, 4, 3, 5, 2, 6)
        e_out = d_out[:, :, :steps].transpose(0, 2, 1, 4, 3, 5)
        s_in = d_in[:, :, steps:].transpose(1, 4, 3, 5, 0, 2, 6)
        s_out = d_out[:, :, steps:].transpose(0, 2, 1, 4, 3, 5)
        return [g.astype(F32).reshape(shape) for g, shape in zip((e_in, e_out, s_in, s_out), shapes)]

    def kernel(in_ref, ein_ref, eout_ref, sin_ref, sout_ref):
        c = pl.program_id(0)

        def get(z, row, high):
            return in_ref[0, z, row : row + high, :].astype(F32)

        for z in range(groups):
            at = slice(z * r, (z + 1) * r)
            for j in range(steps):
                for g in range(2):
                    got = get(z, j * tall + g * r, r)
                    for n in range(shards):
                        col = g * ff + n * (ff // shards) + j * per
                        ein_ref[0, at, col : col + per] = got[:, n * per : (n + 1) * per]
                for b in range(cols):
                    row = j * per + z * q
                    got = get(z, j * tall + 2 * r + b * q, q)
                    eout_ref[0, row : row + q, b * wide : (b + 1) * wide] = got
            for j in range(s_steps):
                first = (steps + j) * tall
                for g in range(2):
                    got = get(z, first + g * r, r)
                    for n in range(shards):
                        col = ((g * shards + n) * ctxs + c) * piece + j * per
                        sin_ref[at, pl.ds(pl.multiple_of(col, 128), per)] = got[:, n * per : (n + 1) * per]
                for b in range(cols):
                    row = j * per + z * q
                    got = get(z, first + 2 * r + b * q, q)
                    sout_ref[row : row + q, b * wide : (b + 1) * wide] = got

    outs = pl.pallas_call(
        kernel,
        out_shape=tuple(jax.ShapeDtypeStruct(shape, F32) for shape in shapes),
        grid=(ctxs,),
        in_specs=[pl.BlockSpec((1, groups, total, wide), lambda c: (c, 0, 0, 0))],
        out_specs=(
            pl.BlockSpec((1,) + shapes[0][1:], lambda c: (c, 0, 0)),
            pl.BlockSpec((1,) + shapes[1][1:], lambda c: (c, 0, 0)),
            pl.BlockSpec(shapes[2], lambda c: (0, 0), pipeline_mode=pl.Buffered(1)),
            pl.BlockSpec((piece, width), lambda c: (c, 0)),
        ),
        compiler_params=pltpu.CompilerParams(vmem_limit_bytes=58 * MB),
        name="unpack",
        cost_estimate=pl.CostEstimate(flops=0, bytes_accessed=6 * parts.size, transcendentals=0),
    )(parts)
    return outs


def weight_pieces(
    shared_in, shared_out, expert_in, expert_out, member, core, shard, shards, ctxs, steps, s_steps, per, piece
):
    rows, width = shared_in.shape[0], shared_out.shape[1]
    ff, tile = steps * per * shards, per * shards
    s_split = shared_in.reshape(rows, 2, shards, ctxs, piece)
    pick = lambda array, who, axis: lax.dynamic_index_in_dim(array, who, axis, keepdims=False)

    if shards != 2:

        def tiles(e, s):
            gathered = []
            for v, count in ((e, steps), (s, s_steps)):
                v = v.reshape(rows, 2, shards, count, per).transpose(3, 0, 1, 2, 4).reshape(count, rows, 2 * tile)
                gathered.append(lax.all_gather(v, "fsdp", axis=1, tiled=True))
            return gathered

        e_in, s_in = tiles(pick(expert_in, member, 0), pick(s_split, member, 3))
        e_out = pick(expert_out, member, 0).reshape(steps, per, width)
        s_out = lax.dynamic_slice_in_dim(shared_out, member * piece, piece, 0).reshape(s_steps, per, width)
        e_out, s_out = (lax.all_gather(v, "fsdp", axis=1, tiled=True) for v in (e_out, s_out))
        made = [
            (
                [(v, (None, width, 2 * tile), lambda j, w: (j, 0, 0), 0, width, None, 0, 0)],
                [(o, (None, tile, width), lambda j, w: (j, 0, 0), 0, tile, None, 0, 0)],
            )
            for v, o in ((e_in, e_out), (s_in, s_out))
        ]
        return made[0], made[1], jnp.zeros((2,), jnp.int32), ((), (), ())

    who, part = member ^ 1, rows // 2
    half = width // 2
    sent = [
        lax.dynamic_slice(expert_in, (who, core * part, 0), (1, part, 2 * ff))[0],
        lax.dynamic_slice(expert_out, (who, 0, core * half), (1, expert_out.shape[1], half))[0],
        jnp.concatenate(
            [
                lax.dynamic_slice(shared_in, (core * part, ((g * shards + n) * ctxs + who) * piece), (part, piece))
                for g in range(2)
                for n in range(shards)
            ],
            axis=1,
        ),
        lax.dynamic_slice(shared_out, (who * piece, core * half), (piece, half)),
    ]
    got = [swap_with(v, "fsdp", 1) for v in sent]
    sib = [swap_with(v, "ctx", 1) for v in got]
    far_row, far_out = (1 - shard) * rows, (1 - shard) * per
    words = [
        member, core, shard * rows, far_row + core * part, far_row + (1 - core) * part,
        shard * per, far_out, core * half, (1 - core) * half,
    ]
    words = jnp.stack(words).astype(jnp.int32)
    blocks, s_blocks = ff // shards // per, piece // per
    e_ins, s_ins = [], []
    for g in range(2):
        for n in range(shards):
            lane = g * tile + n * per
            e_col = lambda j, g=g, n=n: (g * shards + n) * blocks + j
            s_own = lambda j, w, g=g, n=n: ((g * shards + n) * ctxs + w[0]) * s_blocks + j
            s_far = lambda j, g=g, n=n: (g * shards + n) * s_blocks + j
            e_own = lambda j, w, col=e_col: (w[0], 0, col(j))
            e_ins.append((expert_in, (None, rows, per), e_own, 2, 16, None, 0, lane))
            s_ins.append((shared_in, (rows, per), lambda j, w, col=s_own: (0, col(j, w)), 2, 16, None, 0, lane))
            for word, source in ((3, got), (4, sib)):
                e_ins.append((source[0], (part, per), lambda j, w, col=e_col: (0, col(j)), word, 16, None, 0, lane))
                s_ins.append((source[2], (part, per), lambda j, w, col=s_far: (0, col(j)), word, 16, None, 0, lane))
    e_outs = [(expert_out, (None, per, width), lambda j, w: (w[0], j, 0), 5, per, None, 0, 0)]
    s_outs = [(shared_out, (per, width), lambda j, w: (w[0] * s_blocks + j, 0), 5, per, None, 0, 0)]
    for word, source in ((7, got), (8, sib)):
        e_outs.append((source[1], (per, half), lambda j, w: (j, 0), 6, per, word, 128, 0))
        s_outs.append((source[3], (per, half), lambda j, w: (j, 0), 6, per, word, 128, 0))
    return (e_ins, e_outs), (s_ins, s_outs), words, (sent, got, sib)


def inverse_rms(values):
    return lax.rsqrt(jnp.mean(values * values, axis=-1, keepdims=True) + EPS)


def norm_back(values, inverse, gain, grad):
    scaled = grad * gain
    dotted = jnp.mean(scaled * values, axis=-1, keepdims=True)
    return inverse * scaled - values * (inverse * inverse * inverse) * dotted


def half_turn(pairs):
    size = pairs * HEAD_DIM
    row = lax.broadcasted_iota(jnp.int32, (size, size), 0)
    col = lax.broadcasted_iota(jnp.int32, (size, size), 1)
    return (row == (col ^ (HEAD_DIM // 2))).astype(BF)


def on_device(
    tokens,
    segment_ids,
    routes,
    cotangent,
    norm1_gain,
    qkv_weight,
    out_weight,
    norm2_gain,
    router_weight,
    shared_in,
    shared_out,
    expert_in,
    expert_out,
):
    local_len, seqs, width = tokens.shape
    count = local_len * seqs
    groups = lax.axis_size("head")
    ctxs = lax.axis_size("ctx")
    shards = lax.axis_size("fsdp")
    ctx = lax.axis_index("ctx")
    head = lax.axis_index("head")
    shard = lax.axis_index("fsdp")
    group_width = width // groups
    heads = group_width // HEAD_DIM
    block = local_len * groups
    span = seqs * block
    experts = expert_in.shape[0]
    rows_per = width // shards
    ff = expert_in.shape[2] // 2
    fs = shared_in.shape[1] // 2
    fs_part = fs // ctxs
    ctx_word = ctx.astype(jnp.int32).reshape(1)

    member = group_member()
    piece = fs // shards // ctxs
    tile = 256
    per = tile // shards
    steps, s_steps = ff // tile, fs_part // tile
    x_own = tokens.transpose(1, 0, 2)
    w_group = lax.dynamic_index_in_dim(qkv_weight.reshape(-1, 3, groups, group_width), head, 2, keepdims=False)
    w_group = fsdp_gather_small(w_group.reshape(-1, 3 * group_width), 0)
    small = jnp.concatenate([norm1_gain[None], norm2_gain[None], router_weight.T], axis=0)
    small = fsdp_gather_small(small, 1)
    x_line = line_gather_kernel(x_own, 0)
    gain_one, gain_two = small[0].astype(F32), small[1].astype(F32)
    w_router = small[2:]
    w_q, w_kv = w_group[:, :group_width], w_group[:, group_width:]
    w_q_turned = dot(w_q, half_turn(heads)).astype(BF)
    w_kv_turned = dot(w_kv, half_turn(2 * heads)).astype(BF)

    dz_own = cotangent.transpose(1, 0, 2).reshape(count, width)
    index = jnp.arange(HEAD_DIM // 2).astype(F32)
    freq = jnp.exp(-math.log(ROPE_BASE) * 2.0 * index / HEAD_DIM)
    position = ctx * block + jnp.arange(block, dtype=jnp.int32)
    angle = position.astype(F32)[:, None] * freq[None, :]
    cosine, sine = jnp.cos(angle), jnp.sin(angle)
    scale = HEAD_DIM**-0.5
    cos_q = jnp.tile(cosine, (1, 2 * heads))
    sin_q = jnp.tile(jnp.concatenate([-sine, sine], axis=1), (1, heads))
    cos_kv = jnp.concatenate([cos_q, jnp.ones_like(cos_q)], axis=1)[None]
    sin_kv = jnp.concatenate([sin_q, jnp.zeros_like(sin_q)], axis=1)[None]
    cos_q, sin_q = cos_q[None] * scale, sin_q[None] * scale

    x_f = x_line.astype(F32)
    inverse_one = inverse_rms(x_f)
    normed = (x_f * inverse_one * gain_one).astype(BF)
    normed_rows = normed.reshape(span, width)

    def turned(weight, weight_turned, cos_table, sin_table):
        plain = dot(normed_rows, weight).reshape(seqs, block, -1)
        other = dot(normed_rows, weight_turned).reshape(seqs, block, -1)
        return (plain * cos_table + other * sin_table).astype(BF)

    key_value = turned(w_kv, w_kv_turned, cos_kv, sin_kv)
    kv_blocks = ctx_gather(key_value)
    queries = turned(w_q, w_q_turned, cos_q, sin_q)
    e_pieces, s_pieces, words, sent = weight_pieces(
        shared_in, shared_out, expert_in, expert_out, after(member, corner(key_value)), ctx % 2, shard, shards, ctxs, steps, s_steps, per, piece
    )
    kv_near = jnp.stack(kv_blocks[:2])
    kv_far = jnp.stack(kv_blocks[2:])
    dz_all = jnp.concatenate(group_gather(after(dz_own, corner(key_value))), axis=0)
    w_attn = fsdp_gather_small(out_weight, 0)

    def forward_bounds(tq, tk):
        nq = block // tq
        first = ctx * block + jnp.arange(nq, dtype=jnp.int32) * tq
        low = segment_ids[:, ::tq] // tk
        last_start = segment_ids[:, tq - 1 :: tq]
        clear_to = jnp.broadcast_to(first // tk, low.shape)
        clear_from = jnp.minimum((last_start + tk - 1) // tk, clear_to)
        clear_from = jnp.maximum(clear_from, low)
        clear_to = jnp.maximum(clear_to, clear_from)
        high = jnp.broadcast_to((first + tq - 1) // tk + 1, low.shape)
        return jnp.stack([low, clear_from, clear_to, high], axis=2).astype(jnp.int32)

    fwd_q, fwd_k = min(1024, block), min(512, block)
    bounds = forward_bounds(fwd_q, fwd_k)
    near_base = (ctx // 2) * 2
    far_base = near_base ^ 2
    near_words = jnp.stack([ctx, 0 * ctx, near_base]).astype(jnp.int32)
    far_words = jnp.stack([ctx, 0 * ctx + 2, far_base]).astype(jnp.int32)
    edge = near_base * (block // fwd_k)
    starts = segment_ids[:, None, :]
    state = attend_forward(near_words, jnp.maximum(bounds, edge), queries, kv_near, starts, fwd_q, fwd_k, None)
    dz_t = dz_all.T
    state = [after(state[0], *sent[1], dz_t), state[1]]
    attended, attended_low, lse = attend_forward(
        far_words, jnp.minimum(bounds, edge), queries, kv_far, starts, fwd_q, fwd_k, state
    )
    attended_low = after(attended_low, *sent[2], w_attn)
    sent = attended_low.reshape(seqs, groups, local_len, group_width)
    back = lax.all_to_all(sent, "head", split_axis=1, concat_axis=3, tiled=True)
    attn_rows = back.reshape(count, width)

    x_rows = x_own.reshape(count, width).astype(F32)
    hidden = x_rows + dot(attn_rows, w_attn)
    inverse_two = inverse_rms(hidden)
    normed_two = (hidden * inverse_two * gain_two).astype(BF)
    route_rows = routes.reshape(local_len, seqs, 2).transpose(1, 0, 2).reshape(count, 2)
    logits = dot_t(normed_two, w_router)
    ids = jnp.arange(experts, dtype=jnp.int32)
    picks = (route_rows[:, :, None] == ids).astype(F32)
    chosen = jnp.sum(logits[:, None, :] * picks, axis=2)
    gate_first = 1.0 / (1.0 + jnp.exp(chosen[:, 1:] - chosen[:, :1]))
    gates = jnp.concatenate([gate_first, 1.0 - gate_first], axis=1)
    combine = jnp.sum(gates[:, :, None] * picks, axis=1)

    xn_blocks = group_gather(normed_two)
    combine_t = combine.T
    c_one, c_two = group_swap(combine_t, 1), group_swap(combine_t, 2)
    combine_all = jnp.concatenate([combine_t, c_one, c_two, group_swap(c_one, 2)], axis=1)
    c_own = lax.dynamic_index_in_dim(combine_all, member, 0, keepdims=False)[:, None]
    y_part, dx_part, dc, g_one, g_two = gated_mlp(
        xn_blocks, dz_all, dz_t, c_own, words, e_pieces, s_pieces, steps, s_steps, groups if paired() else 0
    )
    g_part = sum_parts(g_one, g_two)
    dc_blocks = dc.reshape(ctxs, count)
    dc_got = [
        dc_blocks[0],
        group_swap(dc_blocks[1], 1),
        group_swap(dc_blocks[2], 2),
        group_swap(group_swap(dc_blocks[3], 1), 2),
    ]
    dcombine = sum(
        dc_got[k][:, None] * ((member ^ k) == ids).astype(F32)[None, :] for k in range(ctxs)
    )
    dx_blocks = dx_part.reshape(ctxs, count, width)
    dxn2 = group_scatter([dx_blocks[k] for k in range(ctxs)])

    dchosen = jnp.sum(dcombine[:, None, :] * picks, axis=2)
    dfirst = gates[:, :1] * gates[:, 1:] * (dchosen[:, :1] - dchosen[:, 1:])
    dlogits = (dfirst * (picks[:, 0] - picks[:, 1])).astype(BF)
    router_part = dot_l(normed_two, dlogits)
    dxn2 = dxn2 + dot(dlogits, w_router)
    dz_rows = dz_own.astype(F32)
    dh = dz_rows + norm_back(hidden, inverse_two, gain_two, dxn2)
    gain_two_part = jnp.sum(dxn2 * hidden * inverse_two, axis=0)
    dh_low = dh.astype(BF)
    g_attn = dot_l(attn_rows, dh_low)
    g_attn = jnp.concatenate(
        [g_attn, gain_two_part[:, None], router_part, jnp.zeros((width, 255 - experts), F32)], axis=1
    ).astype(BF)
    dattn = dot_t(dh_low, w_attn).astype(BF).reshape(seqs, local_len, width)
    grad_out = lax.all_to_all(
        dattn.reshape(seqs, local_len, groups, group_width), "head", split_axis=2, concat_axis=1, tiled=True
    ).reshape(seqs, block, group_width)

    y_blocks = after(y_part, dh_low).reshape(ctxs, count, width)
    y_near = group_scatter_near([y_blocks[k] for k in range(ctxs)])
    grad_out = after(grad_out, *y_near)
    y_near = [y_near[0], group_swap(y_near[1], 1), group_swap(y_near[2], 2)]
    y_own = sum(v.astype(F32) for v in y_near)
    output = (hidden + y_own).astype(BF).reshape(seqs, local_len, width).transpose(1, 0, 2)

    delta = jnp.sum((grad_out.astype(F32) * attended).reshape(seqs, block, heads, HEAD_DIM), axis=3)
    stats = jnp.concatenate(
        [lse[:, :heads], delta.transpose(0, 2, 1), jnp.zeros((seqs, 8 - 2 * heads, block), F32)],
        axis=1,
    )
    tq = tk = min(512, block)
    tile_last = ctx * block + (jnp.arange(block // tq, dtype=jnp.int32) + 1) * tq - 1
    tile_key = jnp.arange(ctxs * block // tk, dtype=jnp.int32)
    q_low = jnp.sum((tile_last[None, :] < (tile_key * tk)[:, None]).astype(jnp.int32), axis=1)
    q_high = jnp.sum(((segment_ids[:, ::tq] // tk)[:, None, :] <= tile_key[None, :, None]).astype(jnp.int32), axis=2)
    q_low = jnp.broadcast_to(q_low, q_high.shape)
    back_bounds = jnp.stack([q_low, q_high], axis=2).astype(jnp.int32)
    edges = segment_ids[:, tq - 1 :: tq]
    dq_far, far_parts = attend_backward(
        far_words, back_bounds, edges, queries, kv_far, grad_out, stats, starts, tq, tk
    )
    far_sum = (far_parts[0].astype(F32) + swap_with(far_parts[1], "ctx", 1).astype(F32)).astype(BF)
    far_got = swap_with(far_sum, "ctx", 2)
    g_attn = lax.psum_scatter(g_attn, ("fsdp", "ctx"), scatter_dimension=0, tiled=True)
    g_attn = after(g_attn, corner(dq_far))
    g_attn = g_attn.reshape(-1, (width + tile) // tile, tile).transpose(1, 0, 2).reshape(-1, tile)
    whole_parts = jnp.concatenate([exchange_parts(after(g_part, corner(dq_far))), g_attn], axis=0)
    gathered = share_parts(whole_parts)
    dq_near, near_parts = attend_backward(
        near_words, back_bounds, edges, queries, kv_near, after(grad_out, corner(whole_parts), corner(far_sum)), stats, starts, tq, tk
    )
    near_parts = after(near_parts, *y_near)
    dkv = near_parts[0].astype(F32) + swap_with(near_parts[1], "ctx", 1).astype(F32) + far_got.astype(F32)
    dq = ((dq_far + dq_near) * scale).astype(BF).astype(F32)
    dkv = dkv.astype(BF).astype(F32)

    def turned_back(grad, cos_table, sin_table, pairs):
        other = (grad * sin_table).astype(BF).reshape(span, -1)
        back = dot(other, half_turn(pairs)).reshape(seqs, block, -1)
        return (grad * cos_table + back).astype(BF).reshape(span, -1)

    d_q = turned_back(dq, cos_q * HEAD_DIM**0.5, sin_q * HEAD_DIM**0.5, heads)
    d_kv = turned_back(dkv, cos_kv, sin_kv, 2 * heads)
    dxn1_part = (dot_t(d_q, w_q) + dot_t(d_kv, w_kv)).reshape(seqs, block, width)
    g_q, g_kv = dot_l(normed_rows, d_q), dot_l(normed_rows, d_kv)
    gain_one_part = jnp.sum(dxn1_part * x_f * inverse_one, axis=(0, 1))
    filler = jnp.zeros((width, 128 - 3 * group_width % 128 - 1), F32)
    g_qkv = jnp.concatenate([g_q, g_kv, gain_one_part[:, None], filler], axis=1).astype(BF)
    if paired():
        blocks = dxn1_part.astype(BF).reshape(seqs, groups, local_len, width).transpose(1, 0, 2, 3)
        dxn1, qkv_grad, side = tail_kernel(blocks.reshape(groups, count, width), g_qkv, 1)
        gain_one_grad = side[:, 3 * group_width % 128]
    else:
        dxn1 = line_scatter(dxn1_part.astype(BF), 1).reshape(count, width)
        g_qkv = lax.psum(lax.psum_scatter(g_qkv, "fsdp", scatter_dimension=0, tiled=True), "ctx")
        g_qkv = line_gather(g_qkv[:, None], 1).astype(F32)
        qkv_grad = g_qkv[..., : 3 * group_width].reshape(rows_per, groups, 3, group_width)
        qkv_grad = qkv_grad.transpose(0, 2, 1, 3).reshape(rows_per, 3 * width)
        gain_one_grad = jnp.sum(g_qkv[..., 3 * group_width], axis=1)
    dx_norm = norm_back(x_rows, inverse_rms(x_rows), gain_one, dxn1)
    tokens_grad = (dh + dx_norm).reshape(seqs, local_len, width).transpose(1, 0, 2)

    expert_in_grad, expert_out_grad, shared_in_grad, shared_out_grad = unpack(
        gathered, shards, steps, s_steps, width
    )
    g_attn = jnp.sum(gathered[:, :, (steps + s_steps) * (rows_per // groups * 2 + 3 * per // groups) :].astype(F32), axis=1)
    g_attn = g_attn.reshape(ctxs, (width + tile) // tile, -1, tile).transpose(0, 2, 1, 3).reshape(rows_per, width + tile)
    out_grad, side = g_attn[:, :width], g_attn[:, width:]
    return (
        output,
        tokens_grad,
        gain_one_grad,
        qkv_grad,
        out_grad,
        side[:, 0],
        side[:, 1 : 1 + experts],
        shared_in_grad,
        shared_out_grad,
        expert_in_grad,
        expert_out_grad,
    )


def solution(mesh):
    rows = P(("ctx", "head"), "fsdp", None)
    vector = P("fsdp")
    matrix = P("fsdp", None)
    stack = P(None, "fsdp", None)
    return jax.shard_map(
        on_device,
        mesh=mesh,
        in_specs=(
            rows,
            P("fsdp", "ctx"),
            P(("ctx", "head"), "fsdp", None, None),
            rows,
            vector,
            matrix,
            matrix,
            vector,
            matrix,
            matrix,
            matrix,
            stack,
            stack,
        ),
        out_specs=(rows, rows, vector, matrix, matrix, vector, matrix, matrix, matrix, stack, stack),
        check_vma=False,
    )
```

```python
import functools
import math

import jax
import jax.numpy as jnp
from jax import lax
from jax.experimental import pallas as pl
from jax.experimental.pallas import tpu as pltpu
from jax.sharding import PartitionSpec as P

HEAD_DIM = 64
EPS = 1e-06
NEG = -1e30
ROPE_BASE = 10000.0
BF = jnp.bfloat16
F32 = jnp.float32
MB = 1 << 20


def swap_with(value, axis_name, bit):
    size = lax.axis_size(axis_name)
    return lax.ppermute(value, axis_name, [(i, i ^ bit) for i in range(size)])


def fsdp_gather(value, axis):
    return lax.all_gather(value, "fsdp", axis=axis, tiled=True)


def fsdp_gather_small(value, axis):
    if lax.axis_size("fsdp") != 2:
        return fsdp_gather(value, axis)
    other = swap_with(value, "fsdp", 1)
    first = lax.axis_index("fsdp") == 0
    return jnp.where(
        first, jnp.concatenate([value, other], axis=axis), jnp.concatenate([other, value], axis=axis)
    )


def line_gather(value, axis):
    count = lax.axis_size("head")
    mine = lax.axis_index("head")
    part = value.shape[axis]
    up = [(i, i + 1) for i in range(count - 1)]
    down = [(i + 1, i) for i in range(count - 1)]
    below, above = [], []
    rising, falling = value, value
    for _ in range(count - 1):
        rising = lax.ppermute(rising, "head", up)
        falling = lax.ppermute(falling, "head", down)
        below.insert(0, rising)
        above.append(falling)
    line = jnp.concatenate(below + [value] + above, axis=axis)
    return lax.dynamic_slice_in_dim(line, (count - 1 - mine) * part, count * part, axis)


def line_scatter(value, axis):
    count = lax.axis_size("head")
    mine = lax.axis_index("head")
    part = value.shape[axis] // count
    up = [(i, i + 1) for i in range(count - 1)]
    down = [(i + 1, i) for i in range(count - 1)]

    def block(index):
        index = jnp.clip(index, 0, count - 1)
        return lax.dynamic_slice_in_dim(value, index * part, part, axis).astype(F32)

    rising, falling = None, None
    for step in range(count - 1):
        upward = block(count - 1 - step + mine)
        downward = block(step - (count - 1) + mine)
        if step:
            upward = upward + rising.astype(F32)
            downward = downward + falling.astype(F32)
        rising = lax.ppermute(upward.astype(BF), "head", up)
        falling = lax.ppermute(downward.astype(BF), "head", down)
    return block(mine) + rising.astype(F32) + falling.astype(F32)


def after(value, *others):
    return lax.optimization_barrier((value, *others))[0] if others else value


def once_there(value, *others):
    zero = jnp.float32(0)
    for other in others:
        first = lax.slice(other, (0,) * other.ndim, (1,) * other.ndim)
        zero += first.reshape(()).astype(F32) * 0.0
    return value + zero.astype(value.dtype)


def paired():
    return lax.axis_size("fsdp") == 2


def group_member():
    ctx = lax.axis_index("ctx")
    return (ctx // 2) * 2 + lax.axis_index("fsdp") if paired() else ctx


def group_swap(value, bit):
    if paired() and bit == 1:
        return swap_with(value, "fsdp", 1)
    return swap_with(value, "ctx", bit)


def group_gather(value):
    half = value.shape[0] // 2
    one, two = group_swap(value, 1), group_swap(value, 2)
    far = jnp.concatenate([group_swap(one[:half], 2), group_swap(two[half:], 1)], axis=0)
    return [value, one, two, far]


def group_scatter_near(blocks):
    own, one, two, far = blocks
    half = far.shape[0] // 2
    by_one, by_two = group_swap(far[:half], 1), group_swap(far[half:], 2)
    two = jnp.concatenate([(two[:half].astype(F32) + by_one.astype(F32)).astype(BF), two[half:]], axis=0)
    one = jnp.concatenate([one[:half], (one[half:].astype(F32) + by_two.astype(F32)).astype(BF)], axis=0)
    return own, one, two


def half_sum(value, axis, axis_name, bit_value, bit, *others):
    part = value.shape[axis] // 2
    sent = lax.dynamic_slice_in_dim(value, (1 - bit_value) * part, part, axis)
    kept = lax.dynamic_slice_in_dim(value, bit_value * part, part, axis)
    got = once_there(swap_with(sent, axis_name, bit), *others)
    return kept.astype(F32) + got.astype(F32)


def pack(d_in, d_out, parts, wide):
    packed = []
    for d in (d_in, d_out):
        j, r, w = d.shape
        d = d.reshape(j, parts, r // parts, w // wide, wide).transpose(1, 0, 3, 2, 4)
        packed.append(d.reshape(parts, j, -1, wide))
    return jnp.concatenate(packed, axis=2)


def sum_parts(one, two, more=None):
    wide = 256
    groups, shards = lax.axis_size("head"), lax.axis_size("fsdp")
    if paired():
        parts, over = groups, "head"
        packed = one.astype(F32) + swap_with(two, "ctx", 1).astype(F32)
        packed = packed.astype(BF).reshape(parts, -1, wide)
        if more is not None:
            more = half_sum(more, 1, "ctx", lax.axis_index("ctx") % 2, 1).astype(BF)
    else:
        parts, over = groups * shards, ("fsdp", "head")
        packed = pack(one, two, parts, wide).reshape(parts, -1, wide)
    if more is not None:
        j, r, w = more.shape
        more = more.reshape(j, parts, r // parts, w // wide, wide).transpose(1, 0, 3, 2, 4)
        packed = jnp.concatenate([packed, more.reshape(parts, -1, wide)], axis=1)
    packed = packed.reshape(-1, wide)
    return lax.psum_scatter(packed, over, scatter_dimension=0, tiled=True)


def exchange_parts(part):
    if not paired():
        return part
    core, shard = lax.axis_index("ctx") % 2, lax.axis_index("fsdp")
    ctxs = lax.axis_size("ctx")
    moves = [(f * ctxs + c, (1 - f) * ctxs + (c ^ 1)) for f in range(2) for c in range(ctxs) if c % 2 != f]
    got = lax.ppermute(part, ("fsdp", "ctx"), moves)
    return jnp.where(core == shard, part, got)


def share_parts(part):
    whole = lax.all_gather(part, ("ctx", "head"), axis=0, tiled=False)
    return whole.reshape((lax.axis_size("ctx"), lax.axis_size("head")) + part.shape)


def ctx_gather(value):
    blocks = [value]
    bit = lax.axis_size("ctx") // 2
    found = {0: value}
    while bit:
        for k in list(found):
            found[k ^ bit] = swap_with(found[k], "ctx", bit)
        bit //= 2
    blocks = [found[k] for k in range(len(found))]
    return blocks


def ctx_scatter(blocks):
    held = {k: blocks[k] for k in range(len(blocks))}
    bit = 1
    while len(held) > 1:
        kept = {}
        for k in list(held):
            if not k & bit:
                got = swap_with(held[k | bit], "ctx", bit)
                kept[k] = held[k].astype(F32) + got.astype(F32)
        held = {k: (v if len(kept) == 1 else v.astype(BF)) for k, v in kept.items()}
        bit *= 2
    return held[0]


MESH_ID = pl.DeviceIdType.MESH


def enter(partners):
    barrier = pltpu.get_barrier_semaphore()
    for there, device in partners:
        if there is None:
            pl.semaphore_signal(barrier, inc=1, device_id=device, device_id_type=MESH_ID)
        else:

            @pl.when(there)
            def _(device=device):
                pl.semaphore_signal(barrier, inc=1, device_id=device, device_id_type=MESH_ID)

    here = sum(1 if there is None else there.astype(jnp.int32) for there, _ in partners)
    pl.semaphore_wait(barrier, here)


def send(src, dst, sems, device):
    return pltpu.make_async_remote_copy(
        src_ref=src, dst_ref=dst, send_sem=sems[0], recv_sem=sems[1], device_id=device, device_id_type=MESH_ID
    )


def line_relay(place, z, count, up, down, up_sems, down_sems):
    def copy(b, device, sems):
        return send(place(b), place(b), (sems[0].at[b], sems[1].at[b]), device)

    def pass_on(far):
        low, high = z - far, z + far

        @pl.when((low >= 0) & (z < count - 1))
        def _():
            if far:
                copy(low, up, up_sems).wait_recv()
            copy(low, up, up_sems).start()

        @pl.when((high < count) & (z > 0))
        def _():
            if far:
                copy(high, down, down_sems).wait_recv()
            copy(high, down, down_sems).start()

    def last(b):
        @pl.when((b < z) & (z == count - 1))
        def _():
            copy(b, up, up_sems).wait_recv()

        @pl.when((b > z) & (z == 0))
        def _():
            copy(b, down, down_sems).wait_recv()

    def sent(b):
        @pl.when((b <= z) & (z < count - 1))
        def _():
            copy(b, up, up_sems).wait_send()

        @pl.when((b >= z) & (z > 0))
        def _():
            copy(b, down, down_sems).wait_send()

    blocks = range(count)
    run = [functools.partial(pass_on, far) for far in blocks]
    return run, [functools.partial(last, b) for b in blocks], [functools.partial(sent, b) for b in blocks]


def line_gather_kernel(value, cid):
    count = lax.axis_size("head")
    seqs, rows, width = value.shape

    def kernel(v_ref, o_ref, us, ur, ds, dr, local):
        z = lax.axis_index("head")
        up, down = {"head": jnp.minimum(z + 1, count - 1)}, {"head": jnp.maximum(z - 1, 0)}

        def place(b):
            return o_ref.at[:, pl.ds(pl.multiple_of(b * rows, rows), rows), :]

        own = pltpu.make_async_copy(v_ref, o_ref.at[:, pl.ds(pl.multiple_of(z * rows, rows), rows), :], local)
        own.start()
        enter([(z < count - 1, up), (z > 0, down)])
        own.wait()
        run, last, sent = line_relay(place, z, count, up, down, (us, ur), (ds, dr))
        for step in (*run, *last, *sent):
            step()

    any_space = pl.BlockSpec(memory_space=pltpu.VMEM)
    return pl.pallas_call(
        kernel,
        out_shape=jax.ShapeDtypeStruct((seqs, count * rows, width), value.dtype),
        in_specs=[any_space],
        out_specs=any_space,
        scratch_shapes=[pltpu.SemaphoreType.DMA((count,))] * 4 + [pltpu.SemaphoreType.DMA],
        compiler_params=pltpu.CompilerParams(
            collective_id=cid, has_side_effects=True, vmem_limit_bytes=16 * MB
        ),
        name="line_gather",
        cost_estimate=pl.CostEstimate(flops=0, bytes_accessed=180 * MB, transcendentals=0),
    )(value)


def tail_kernel(parts, grads, others, cid):
    count, rows, width = parts.shape
    high, wide = grads.shape
    half, quarter, eighth = high // 2, high // 4, high // 8

    apart = others.shape[1]

    def kernel(p_ref, g_ref, a_ref, o_ref, q_ref, gain_ref, attn_ref, a_s, at_s, q_s, up_in, up_out, dn_in, dn_out, s1, r1, s2, r2, r3, *sems):
        us, ur, ds, dr, gus, gur, gds, gdr, aus, aur, ads, adr, xs, ys, cs, yg, cg, ya, ca = sems
        z, f, c = lax.axis_index("head"), lax.axis_index("fsdp"), lax.axis_index("ctx")
        core, upper = lax.rem(c, 2), lax.div(c, 2)
        up, down = {"head": jnp.minimum(z + 1, count - 1)}, {"head": jnp.maximum(z - 1, 0)}
        over_x = {"fsdp": 1 - f}
        over_core = {"ctx": upper * 2 + 1 - core}
        over_y = {"ctx": (1 - upper) * 2 + core}
        enter([(z < count - 1, up), (z > 0, down), (None, over_x), (None, over_core), (None, over_y)])

        def rise(d):
            return send(up_out.at[d], up_in.at[d], (us.at[d], ur.at[d]), up)

        def fall(d):
            return send(dn_out.at[d], dn_in.at[d], (ds.at[d], dr.at[d]), down)

        def rising(d):
            @pl.when(z < d)
            def _():
                @pl.when(z == 0)
                def _():
                    up_out[d] = p_ref[d]

                @pl.when(z > 0)
                def _():
                    rise(d).wait_recv()
                    up_out[d] = (p_ref[d].astype(F32) + up_in[d].astype(F32)).astype(BF)

                rise(d).start()

        def falling(d):
            @pl.when(z > d)
            def _():
                @pl.when(z == count - 1)
                def _():
                    dn_out[d] = p_ref[d]

                @pl.when(z < count - 1)
                def _():
                    fall(d).wait_recv()
                    dn_out[d] = (p_ref[d].astype(F32) + dn_in[d].astype(F32)).astype(BF)

                fall(d).start()

        by_x = send(g_ref.at[pl.ds(pl.multiple_of((1 - f) * half, half), half), :], r1, (xs.at[0], xs.at[1]), over_x)
        by_core = send(
            s1.at[pl.ds(pl.multiple_of((1 - core) * quarter, quarter), quarter), :], r2, (cs.at[0], cs.at[1]), over_core
        )
        by_y = send(
            s2.at[pl.ds(pl.multiple_of((1 - upper) * eighth, eighth), eighth), :], r3, (ys.at[0], ys.at[1]), over_y
        )
        a_s[z] = a_ref[...]
        by_x.start()
        at_low, at_high = z == 0, z == count - 1
        pl.when(at_low)(lambda: rising(count - 1))
        pl.when(at_high)(lambda: falling(0))
        by_x.wait_recv()
        s1[...] = (g_ref[pl.ds(pl.multiple_of(f * half, half), half), :].astype(F32) + r1[...].astype(F32)).astype(BF)
        by_core.start()
        by_core.wait_recv()
        mine = s1[pl.ds(pl.multiple_of(core * quarter, quarter), quarter), :]
        s2[...] = (mine.astype(F32) + r2[...].astype(F32)).astype(BF)
        by_y.start()
        by_y.wait_recv()
        mine = s2[pl.ds(pl.multiple_of(upper * eighth, eighth), eighth), :]
        q_s[core, upper, z] = (mine.astype(F32) + r3[...].astype(F32)).astype(BF)
        run_q, last, sent = line_relay(
            lambda b: q_s.at[core, upper, b], z, count, up, down, (gus, gur), (gds, gdr)
        )
        also, also_last, also_sent = line_relay(
            lambda b: a_s.at[b], z, count, up, down, (aus, aur), (ads, adr)
        )
        run = [(lambda n=n: (run_q[n](), also[n]())) for n in range(count)]
        last, sent = [*last, *also_last], [*sent, *also_sent]
        run[0]()
        for d in range(1, count - 1):
            pl.when(at_low)(lambda d=d: rising(count - 1 - d))
            pl.when(at_high)(lambda d=d: falling(d))
        pl.when(jnp.logical_not(at_low))(lambda: rising(count - 1))
        run[1]()
        pl.when(jnp.logical_not(at_high))(lambda: falling(0))
        run[2]()
        for d in range(1, count - 1):
            pl.when(jnp.logical_not(at_low))(lambda d=d: rising(count - 1 - d))
            pl.when(jnp.logical_not(at_high))(lambda d=d: falling(d))
        for step in (*run[3:], *last):
            step()
        to_y = send(q_s.at[core, upper], q_s.at[core, upper], (yg.at[0], yg.at[1]), over_y)
        to_y.start()
        summed = a_s[0].astype(F32)
        for n in range(1, count):
            summed += a_s[n].astype(F32)
        at_s[core, upper] = summed.astype(BF)
        a_to_y = send(at_s.at[core, upper], at_s.at[core, upper], (ya.at[0], ya.at[1]), over_y)
        a_to_y.start()

        total = p_ref[z].astype(F32)
        o_ref[...] = total

        @pl.when(z > 0)
        def _():
            rise(z).wait_recv()
            o_ref[...] += up_in[z].astype(F32)

        @pl.when(z < count - 1)
        def _():
            fall(z).wait_recv()
            o_ref[...] += dn_in[z].astype(F32)

        to_y.wait_recv()
        to_core = send(q_s.at[core], q_s.at[core], (cg.at[0], cg.at[1]), over_core)
        to_core.start()
        a_to_y.wait_recv()
        a_to_core = send(at_s.at[core], at_s.at[core], (ca.at[0], ca.at[1]), over_core)
        a_to_core.start()
        to_core.wait_recv()
        a_to_core.wait_recv()
        part = width // count
        for a in range(2):
            for b in range(2):
                at = slice((a * 2 + b) * eighth, (a * 2 + b + 1) * eighth)
                gain = jnp.zeros((eighth, 128), F32)
                for n in range(count):
                    block = q_s[a, b, n].astype(F32)
                    for t in range(3):
                        col = t * width + n * part
                        q_ref[at, col : col + part] = block[:, t * part : (t + 1) * part]
                    gain += block[:, wide - 128 :]
                gain_ref[at, :] = gain
                attn_ref[at, :] = at_s[a, b].astype(F32)
        for d in range(count):

            @pl.when(z < d)
            def _(d=d):
                rise(d).wait_send()

            @pl.when(z > d)
            def _(d=d):
                fall(d).wait_send()

        for step in sent:
            step()
        for copy in (by_x, by_core, by_y, to_y, to_core, a_to_y, a_to_core):
            copy.wait_send()

    vmem = pl.BlockSpec(memory_space=pltpu.VMEM)
    block = lambda *shape: pltpu.VMEM(shape, BF)
    return pl.pallas_call(
        kernel,
        out_shape=(
            jax.ShapeDtypeStruct((rows, width), F32),
            jax.ShapeDtypeStruct((half, 3 * width), F32),
            jax.ShapeDtypeStruct((half, 128), F32),
            jax.ShapeDtypeStruct((half, apart), F32),
        ),
        in_specs=[vmem] * 3,
        out_specs=[vmem] * 4,
        scratch_shapes=[block(count, eighth, apart), block(2, 2, eighth, apart), block(2, 2, count, eighth, wide)]
        + [block(count, rows, width)] * 4
        + [block(half, wide), block(half, wide), block(quarter, wide), block(quarter, wide), block(eighth, wide)]
        + [pltpu.SemaphoreType.DMA((count,))] * 12
        + [pltpu.SemaphoreType.DMA((2,))] * 7,
        compiler_params=pltpu.CompilerParams(
            collective_id=cid, has_side_effects=True, vmem_limit_bytes=40 * MB
        ),
        name="tail",
        cost_estimate=pl.CostEstimate(flops=0, bytes_accessed=220 * MB, transcendentals=0),
    )(parts, grads, others)


def dot_t(a, b):
    return lax.dot_general(a, b, (((1,), (1,)), ((), ())), preferred_element_type=F32)


def dot_l(a, b):
    return lax.dot_general(a, b, (((0,), (0,)), ((), ())), preferred_element_type=F32)


def dot(a, b):
    return jnp.dot(a, b, preferred_element_type=F32)


def attend_forward(words, bounds, queries, keys_values, starts, tq, tk, state):
    seqs, rows, width = queries.shape
    heads = width // HEAD_DIM
    blocks = keys_values.shape[0]
    per = rows // tk

    def kernel(word_ref, bounds_ref, q_ref, kv_ref, seg_ref, *refs):
        if state is None:
            acc_ref, row_ref = refs
        else:
            acc_in, row_in, o_ref, low_ref, lse_ref = refs
        s, i = pl.program_id(0), pl.program_id(1)
        here, first = word_ref[0], word_ref[1]
        seg = seg_ref[0]
        row_pos = here * rows + i * tq + lax.broadcasted_iota(jnp.int32, (tk, tq), 1)
        under = lax.broadcasted_iota(jnp.int32, (tk, tq), 0)

        def step(masked, t, carry):
            at = (lax.div(t, per) ^ here) - first
            off = pl.multiple_of(lax.rem(t, per) * tk, tk)
            new = []
            if masked:
                key_pos = t * tk + under
                seen = (key_pos <= row_pos) & (key_pos >= seg)
            for h in range(heads):
                top, total, acc = carry[3 * h : 3 * h + 3]
                cols = slice(h * HEAD_DIM, (h + 1) * HEAD_DIM)
                vals = slice(width + h * HEAD_DIM, width + (h + 1) * HEAD_DIM)
                scores = dot_t(kv_ref[at, 0, pl.ds(off, tk), cols], q_ref[0, :, cols])
                if masked:
                    scores = jnp.where(seen, scores, NEG)
                new_top = jnp.maximum(top, jnp.max(scores, axis=0, keepdims=True))
                weights = jnp.exp(scores - new_top)
                fade = jnp.exp(top - new_top)
                total = total * fade + jnp.sum(weights, axis=0, keepdims=True)
                acc = acc * fade + dot_l(kv_ref[at, 0, pl.ds(off, tk), vals], weights.astype(BF))
                new += [new_top, total, acc]
            return tuple(new)

        carry = []
        for h in range(heads):
            if state is None:
                carry += [jnp.full((1, tq), NEG, F32), jnp.zeros((1, tq), F32), jnp.zeros((HEAD_DIM, tq), F32)]
            else:
                carry += [
                    row_in[0, h : h + 1, :],
                    row_in[0, heads + h : heads + h + 1, :],
                    acc_in[0, h * HEAD_DIM : (h + 1) * HEAD_DIM, :],
                ]
        carry = tuple(carry)
        b = [bounds_ref[s, i, n] for n in range(4)]
        carry = lax.fori_loop(b[0], b[1], functools.partial(step, True), carry)
        carry = lax.fori_loop(b[1], b[2], functools.partial(step, False), carry)
        carry = lax.fori_loop(b[2], b[3], functools.partial(step, True), carry)
        tops, totals, accs = carry[::3], carry[1::3], carry[2::3]
        filler = jnp.zeros((8 - 2 * heads, tq), F32)
        if state is None:
            acc_ref[0] = jnp.concatenate(accs, axis=0)
            row_ref[0] = jnp.concatenate([*tops, *totals, filler], axis=0)
        else:
            result = jnp.concatenate([acc / total for acc, total in zip(accs, totals)], axis=0).T
            o_ref[0] = result
            low_ref[0] = result.astype(BF)
            logs = [top + jnp.log(total) for top, total in zip(tops, totals)]
            lse_ref[0] = jnp.concatenate([*logs, *totals, filler], axis=0)

    rows_spec = pl.BlockSpec((1, tq, width), lambda s, i, *_: (s, i, 0))
    acc_spec = pl.BlockSpec((1, width, tq), lambda s, i, *_: (s, 0, i))
    stat_spec = pl.BlockSpec((1, 8, tq), lambda s, i, *_: (s, 0, i))
    stat_shape = jax.ShapeDtypeStruct((seqs, 8, rows), F32)
    if state is None:
        out_shape = (jax.ShapeDtypeStruct((seqs, width, rows), F32), stat_shape)
        more, out_specs = [], [acc_spec, stat_spec]
    else:
        shape = (seqs, rows, width)
        out_shape = (jax.ShapeDtypeStruct(shape, F32), jax.ShapeDtypeStruct(shape, BF), stat_shape)
        more, out_specs = [acc_spec, stat_spec], [rows_spec, rows_spec, stat_spec]
    return pl.pallas_call(
        kernel,
        out_shape=out_shape,
        grid_spec=pltpu.PrefetchScalarGridSpec(
            num_scalar_prefetch=2,
            grid=(seqs, rows // tq),
            in_specs=[
                rows_spec,
                pl.BlockSpec((blocks, 1, rows, 2 * width), lambda s, i, *_: (0, s, 0, 0)),
                pl.BlockSpec((1, 1, tq), lambda s, i, *_: (s, 0, i)),
                *more,
            ],
            out_specs=out_specs,
        ),
        compiler_params=pltpu.CompilerParams(vmem_limit_bytes=48 * MB),
        name="attend_forward",
        cost_estimate=pl.CostEstimate(
            flops=int(2 * 2 * seqs * heads * rows * rows * 2 * HEAD_DIM * 4),
            bytes_accessed=64 * MB,
            transcendentals=int(seqs * heads * rows * rows * 2),
        ),
    )(words, bounds, queries, keys_values, starts, *(state or ()))


def attend_backward(words, bounds, edges, queries, keys_values, grads, stats, starts, tq, tk):
    seqs, rows, width = queries.shape
    heads = width // HEAD_DIM
    blocks = keys_values.shape[0]
    per = rows // tk

    def kernel(word_ref, bounds_ref, edges_ref, q_ref, kv_ref, do_ref, stat_ref, seg_ref, dq_ref, dkv_ref, acc):
        s = pl.program_id(0)
        here = word_ref[0]
        t = word_ref[2] * per + pl.program_id(1)

        @pl.when(pl.program_id(1) == 0)
        def _():
            dq_ref[...] = jnp.zeros_like(dq_ref)

        acc[...] = jnp.zeros_like(acc)
        lane = lax.broadcasted_iota(jnp.int32, (tk, tq), 1)
        key_pos = t * tk + lax.broadcasted_iota(jnp.int32, (tk, tq), 0)

        def tile(masked, i):
            off = pl.multiple_of(i * tq, tq)
            if masked:
                row_pos = here * rows + off + lane
                seen = (key_pos <= row_pos) & (key_pos >= seg_ref[0, 0:1, pl.ds(off, tq)])
            for h in range(heads):
                cols = slice(h * HEAD_DIM, (h + 1) * HEAD_DIM)
                vals = slice(width + h * HEAD_DIM, width + (h + 1) * HEAD_DIM)
                q = q_ref[0, pl.ds(off, tq), cols]
                do = do_ref[0, pl.ds(off, tq), cols]
                k = kv_ref[0, 0, :, cols]
                v = kv_ref[0, 0, :, vals]
                scores = dot_t(k, q)
                weights = jnp.exp(scores - stat_ref[0, h : h + 1, pl.ds(off, tq)])
                if masked:
                    weights = jnp.where(seen, weights, 0.0)
                dweights = dot_t(v, do)
                dscores = weights * (dweights - stat_ref[0, heads + h : heads + h + 1, pl.ds(off, tq)])
                dscores = dscores.astype(BF)
                acc[h] += dot(dscores, q)
                acc[heads + h] += dot(weights.astype(BF), do)
                dq_ref[0, pl.ds(off, tq), cols] += dot_l(dscores, k)

        def step(i, carry):
            first = here * rows + i * tq
            clear = (edges_ref[s, i] <= t * tk) & (t * tk + tk - 1 <= first)

            @pl.when(clear)
            def _():
                tile(False, i)

            @pl.when(jnp.logical_not(clear))
            def _():
                tile(True, i)

            return carry

        lax.fori_loop(bounds_ref[s, t, 0], bounds_ref[s, t, 1], step, 0)
        dkv_ref[0, 0] = jnp.concatenate([acc[n] for n in range(2 * heads)], axis=1).astype(BF)

    at = lambda s, t, w, *_: (((w[2] + t // per) ^ w[0]) - w[1], s, t % per, 0)
    return pl.pallas_call(
        kernel,
        out_shape=(
            jax.ShapeDtypeStruct((seqs, rows, width), F32),
            jax.ShapeDtypeStruct((blocks, seqs, rows, 2 * width), BF),
        ),
        grid_spec=pltpu.PrefetchScalarGridSpec(
            num_scalar_prefetch=3,
            grid=(seqs, blocks * per),
            in_specs=[
                pl.BlockSpec((1, rows, width), lambda s, t, *_: (s, 0, 0)),
                pl.BlockSpec((1, 1, tk, 2 * width), at),
                pl.BlockSpec((1, rows, width), lambda s, t, *_: (s, 0, 0)),
                pl.BlockSpec((1, 8, rows), lambda s, t, *_: (s, 0, 0)),
                pl.BlockSpec((1, 1, rows), lambda s, t, *_: (s, 0, 0)),
            ],
            out_specs=[
                pl.BlockSpec((1, rows, width), lambda s, t, *_: (s, 0, 0)),
                pl.BlockSpec((1, 1, tk, 2 * width), at),
            ],
            scratch_shapes=[pltpu.VMEM((2 * heads, tk, HEAD_DIM), F32)],
        ),
        compiler_params=pltpu.CompilerParams(vmem_limit_bytes=48 * MB),
        name="attend_backward",
        cost_estimate=pl.CostEstimate(
            flops=int(5 * 2 * seqs * heads * rows * rows * 2 * HEAD_DIM * 4),
            bytes_accessed=100 * MB,
            transcendentals=int(seqs * heads * rows * rows * 2),
        ),
    )(words, bounds, edges, queries, keys_values, grads, stats, starts)


def gated_mlp(rows_in, grads, gates, words, routed, shared, steps, s_steps, groups):
    block_rows, width = rows_in[0].shape
    n_rows = len(rows_in)
    count = block_rows * n_rows
    tile = 256
    chunk = min(512, count)
    all_steps = steps + s_steps
    pieces = [(piece, held, where) for where, lists in enumerate((routed, shared)) for held in (0, 1) for piece in lists[held]]

    def kernel(word_ref, *refs):
        row_refs, d_refs, c_in = refs[:n_rows], refs[n_rows : 2 * n_rows], refs[2 * n_rows]
        refs = refs[2 * n_rows + 1 :]
        piece_refs, refs = refs[: len(pieces)], refs[len(pieces) :]
        y_out, dx_out, dc_ref, one_ref, two_ref, x_ref, xt_ref, d_ref, dt_ref, c_ref, y_ref, dx_ref, w_s, wt_s, wo_s, wot_s, a_s, g_s = refs
        j = pl.program_id(0)

        @pl.when(j == 0)
        def _():
            dc_ref[...] = jnp.zeros_like(dc_ref)
            c_ref[...] = c_in[...]
            y_ref[...] = jnp.zeros_like(y_ref)
            dx_ref[...] = jnp.zeros_like(dx_ref)
            for sources, plain, across in ((row_refs, x_ref, xt_ref), (d_refs, d_ref, dt_ref)):
                for n, ref in enumerate(sources):
                    at = slice(n * block_rows, (n + 1) * block_rows)
                    plain[at, :] = ref[...]
                    across[:, at] = ref[...].T

        @pl.when(j == steps)
        def _():
            c_ref[...] = jnp.ones_like(c_ref)

        def fill(kind):
            for ref, (piece, held, where) in zip(piece_refs, pieces):
                if where != kind:
                    continue
                tall, wide = ref.shape
                row, times, lane_word, lane_times, lane = piece[3:]
                at = pl.ds(pl.multiple_of(word_ref[row], times), tall)
                if lane_word is None:
                    lanes = slice(lane, lane + wide)
                else:
                    lanes = pl.ds(pl.multiple_of(word_ref[lane_word], lane_times), wide)
                (w_s, wo_s)[held][at, lanes] = ref[...]

        pl.when(j < steps)(lambda: fill(0))
        pl.when(j >= steps)(lambda: fill(1))
        wt_s[...] = w_s[...].T
        wot_s[...] = wo_s[...].T

        routed_here = jnp.where(j < steps, 1.0, 0.0)

        def body(n, carry):
            at = pl.ds(pl.multiple_of(n * chunk, chunk), chunk)
            both = dot(x_ref[at, :], w_s[...])
            gate, up = both[:, :tile], both[:, tile:]
            raw = dot(d_ref[at, :], wot_s[...])
            c = c_ref[at, :]
            sig = 0.5 + 0.5 * jnp.tanh(0.5 * gate)
            silu = gate * sig
            act = silu * up

            dc_ref[at, :] += jnp.sum(act * raw, axis=1, keepdims=True) * routed_here
            back = raw * c
            a_low = (act * c).astype(BF)
            dg = (back * up * (sig + silu * (1.0 - sig))).astype(BF)
            du = (back * silu).astype(BF)
            a_s[at, :] = a_low
            g_s[at, :tile] = dg
            g_s[at, tile:] = du
            y_ref[at, :] += dot(a_low, wo_s[...])
            dx_ref[at, :] += dot(g_s[at, :], wt_s[...])
            return carry

        lax.fori_loop(0, count // chunk, body, 0)

        if groups:
            keep = word_ref[1]
            half = width // 2
            r, q = half // groups, tile // 2 // groups
            for ref, which in ((one_ref, keep), (two_ref, 1 - keep)):
                got = dot(xt_ref[pl.ds(pl.multiple_of(which * half, half), half), :], g_s[...]).astype(BF)
                for z in range(groups):
                    for g in range(2):
                        ref[z, 0, g * r : (g + 1) * r, :] = got[z * r : (z + 1) * r, g * tile : (g + 1) * tile]
            for n in range(width // tile):
                got = dot(dt_ref[n * tile : (n + 1) * tile, :], a_s[...]).T.astype(BF)
                low, high = got[: tile // 2], got[tile // 2 :]
                for ref, which in ((one_ref, keep), (two_ref, 1 - keep)):
                    mine = jnp.where(which == 0, low, high)
                    for z in range(groups):
                        ref[z, 0, 2 * r + n * q : 2 * r + (n + 1) * q, :] = mine[z * q : (z + 1) * q]
        else:
            one_ref[0] = dot(xt_ref[...], g_s[...]).astype(BF)
            for n in range(width // tile):
                at = slice(n * tile, (n + 1) * tile)
                two_ref[0, :, at] = dot(dt_ref[at, :], a_s[...]).T.astype(BF)

        @pl.when(j == all_steps - 1)
        def _():
            y_out[...] = y_ref[...].astype(BF)
            dx_out[...] = dx_ref[...].astype(BF)

    once = pl.Buffered(1)
    whole = lambda *shape: pl.BlockSpec(shape, lambda j, *_: (0,) * len(shape), pipeline_mode=once)

    def piece_spec(piece, where):
        index = piece[2]
        if where == 0:
            return pl.BlockSpec(piece[1], lambda j, w: index(jnp.minimum(j, steps - 1), w))
        return pl.BlockSpec(piece[1], lambda j, w: index(jnp.maximum(j - steps, 0), w))

    in_specs = [whole(block_rows, width)] * (2 * n_rows) + [whole(count, 1)]
    in_specs += [piece_spec(piece, where) for piece, _, where in pieces]
    operands = [*rows_in, *grads, gates, *(piece[0] for piece, _, _ in pieces)]
    if groups:
        rows = width // groups + 3 * tile // 2 // groups
        grad_shape = [(groups, all_steps, rows, tile)] * 2
        grad_spec = [pl.BlockSpec((groups, 1, rows, tile), lambda j, *_: (0, j, 0, 0))] * 2
    else:
        grad_shape = [(all_steps, width, 2 * tile), (all_steps, tile, width)]
        grad_spec = [pl.BlockSpec((1,) + shape[1:], lambda j, *_: (j, 0, 0)) for shape in grad_shape]
    return pl.pallas_call(
        kernel,
        out_shape=(
            jax.ShapeDtypeStruct((count, width), BF),
            jax.ShapeDtypeStruct((count, width), BF),
            jax.ShapeDtypeStruct((count, 1), F32),
            *(jax.ShapeDtypeStruct(shape, BF) for shape in grad_shape),
        ),
        grid_spec=pltpu.PrefetchScalarGridSpec(
            num_scalar_prefetch=1,
            grid=(all_steps,),
            in_specs=in_specs,
            out_specs=[whole(count, width), whole(count, width), whole(count, 1), *grad_spec],
            scratch_shapes=[
                *[pltpu.VMEM((count, width), BF), pltpu.VMEM((width, count), BF)] * 2,
                pltpu.VMEM((count, 1), F32),
                pltpu.VMEM((count, width), F32),
                pltpu.VMEM((count, width), F32),
                pltpu.VMEM((width, 2 * tile), BF),
                pltpu.VMEM((2 * tile, width), BF),
                pltpu.VMEM((tile, width), BF),
                pltpu.VMEM((width, tile), BF),
                pltpu.VMEM((count, tile), BF),
                pltpu.VMEM((count, 2 * tile), BF),
            ],
        ),
        compiler_params=pltpu.CompilerParams(vmem_limit_bytes=60 * MB),
        name="gated_mlp",
        cost_estimate=pl.CostEstimate(
            flops=9 * 2 * count * width * tile * all_steps,
            bytes_accessed=40 * MB,
            transcendentals=count * tile * all_steps,
        ),
    )(words, *operands)


def unpack(parts, shards, steps, s_steps, width):
    ctxs, groups, total, wide = parts.shape
    per = wide // shards
    r = width // shards // groups
    q = per // groups
    cols = width // wide
    tall = 2 * r + cols * q
    ff, piece = steps * wide, s_steps * per
    shapes = (
        (ctxs, groups * r, 2 * ff),
        (ctxs, steps * per, width),
        (groups * r, 2 * shards * ctxs * piece),
        (ctxs * piece, width),
    )
    if per % 128 or q % 16:
        made = parts[:, :, : (steps + s_steps) * tall].reshape(ctxs, groups, -1, tall, wide)
        d_in = made[:, :, :, : 2 * r].reshape(ctxs, groups, -1, 2, r, shards, per)
        d_out = made[:, :, :, 2 * r :].reshape(ctxs, groups, -1, cols, q, wide)
        e_in = d_in[:, :, :steps].transpose(0, 1, 4, 3, 5, 2, 6)
        e_out = d_out[:, :, :steps].transpose(0, 2, 1, 4, 3, 5)
        s_in = d_in[:, :, steps:].transpose(1, 4, 3, 5, 0, 2, 6)
        s_out = d_out[:, :, steps:].transpose(0, 2, 1, 4, 3, 5)
        return [g.astype(F32).reshape(shape) for g, shape in zip((e_in, e_out, s_in, s_out), shapes)]

    def kernel(in_ref, ein_ref, eout_ref, sin_ref, sout_ref):
        c = pl.program_id(0)

        def get(z, row, high):
            return in_ref[0, z, row : row + high, :].astype(F32)

        for z in range(groups):
            at = slice(z * r, (z + 1) * r)
            for j in range(steps):
                for g in range(2):
                    got = get(z, j * tall + g * r, r)
                    for n in range(shards):
                        col = g * ff + n * (ff // shards) + j * per
                        ein_ref[0, at, col : col + per] = got[:, n * per : (n + 1) * per]
                for b in range(cols):
                    row = j * per + z * q
                    got = get(z, j * tall + 2 * r + b * q, q)
                    eout_ref[0, row : row + q, b * wide : (b + 1) * wide] = got
            for j in range(s_steps):
                first = (steps + j) * tall
                for g in range(2):
                    got = get(z, first + g * r, r)
                    for n in range(shards):
                        col = ((g * shards + n) * ctxs + c) * piece + j * per
                        sin_ref[at, pl.ds(pl.multiple_of(col, 128), per)] = got[:, n * per : (n + 1) * per]
                for b in range(cols):
                    row = j * per + z * q
                    got = get(z, first + 2 * r + b * q, q)
                    sout_ref[row : row + q, b * wide : (b + 1) * wide] = got

    outs = pl.pallas_call(
        kernel,
        out_shape=tuple(jax.ShapeDtypeStruct(shape, F32) for shape in shapes),
        grid=(ctxs,),
        in_specs=[pl.BlockSpec((1, groups, total, wide), lambda c: (c, 0, 0, 0))],
        out_specs=(
            pl.BlockSpec((1,) + shapes[0][1:], lambda c: (c, 0, 0)),
            pl.BlockSpec((1,) + shapes[1][1:], lambda c: (c, 0, 0)),
            pl.BlockSpec(shapes[2], lambda c: (0, 0), pipeline_mode=pl.Buffered(1)),
            pl.BlockSpec((piece, width), lambda c: (c, 0)),
        ),
        compiler_params=pltpu.CompilerParams(vmem_limit_bytes=58 * MB),
        name="unpack",
        cost_estimate=pl.CostEstimate(flops=0, bytes_accessed=6 * parts.size, transcendentals=0),
    )(parts)
    return outs


def weight_pieces(
    shared_in, shared_out, expert_in, expert_out, near, member, core, shard, shards, ctxs, steps, s_steps, per, piece
):
    rows, width = shared_in.shape[0], shared_out.shape[1]
    ff, tile = steps * per * shards, per * shards
    s_split = shared_in.reshape(rows, 2, shards, ctxs, piece)
    pick = lambda array, who, axis: lax.dynamic_index_in_dim(array, who, axis, keepdims=False)

    if shards != 2:

        def tiles(e, s):
            gathered = []
            for v, count in ((e, steps), (s, s_steps)):
                v = v.reshape(rows, 2, shards, count, per).transpose(3, 0, 1, 2, 4).reshape(count, rows, 2 * tile)
                gathered.append(lax.all_gather(v, "fsdp", axis=1, tiled=True))
            return gathered

        e_in, s_in = tiles(pick(expert_in, member, 0), pick(s_split, member, 3))
        e_out = pick(expert_out, member, 0).reshape(steps, per, width)
        s_out = lax.dynamic_slice_in_dim(shared_out, member * piece, piece, 0).reshape(s_steps, per, width)
        e_out, s_out = (lax.all_gather(v, "fsdp", axis=1, tiled=True) for v in (e_out, s_out))
        made = [
            (
                [(v, (None, width, 2 * tile), lambda j, w: (j, 0, 0), 0, width, None, 0, 0)],
                [(o, (None, tile, width), lambda j, w: (j, 0, 0), 0, tile, None, 0, 0)],
            )
            for v, o in ((e_in, e_out), (s_in, s_out))
        ]
        return made[0], made[1], jnp.zeros((2,), jnp.int32), ((), (), ())

    who, part = member ^ 1, rows // 2
    half = width // 2
    columns = [
        lax.dynamic_slice(shared_in, (core * part, ((g * shards + n) * ctxs + who) * piece), (part, piece))
        for g in range(2)
        for n in range(shards)
    ]
    sent = [
        jnp.concatenate(
            [lax.dynamic_slice(expert_in, (who, core * part, 0), (1, part, 2 * ff))[0], *columns], axis=1
        ),
        jnp.concatenate(
            [
                lax.dynamic_slice(expert_out, (who, 0, core * half), (1, expert_out.shape[1], half))[0],
                lax.dynamic_slice(shared_out, (who * piece, core * half), (piece, half)),
            ],
            axis=0,
        ),
    ]
    got = [swap_with(v, "fsdp", 1) for v in sent]
    sib = [swap_with(once_there(v, near), "ctx", 1) for v in got]
    far_row, far_out = (1 - shard) * rows, (1 - shard) * per
    words = [
        member, core, shard * rows, far_row + core * part, far_row + (1 - core) * part,
        shard * per, far_out, core * half, (1 - core) * half,
    ]
    words = jnp.stack(words).astype(jnp.int32)
    blocks, s_blocks = ff // shards // per, piece // per
    e_ins, s_ins = [], []
    for g in range(2):
        for n in range(shards):
            lane = g * tile + n * per
            e_col = lambda j, g=g, n=n: (g * shards + n) * blocks + j
            s_own = lambda j, w, g=g, n=n: ((g * shards + n) * ctxs + w[0]) * s_blocks + j
            s_far = lambda j, g=g, n=n: 2 * shards * blocks + (g * shards + n) * s_blocks + j
            e_own = lambda j, w, col=e_col: (w[0], 0, col(j))
            e_ins.append((expert_in, (None, rows, per), e_own, 2, 16, None, 0, lane))
            s_ins.append((shared_in, (rows, per), lambda j, w, col=s_own: (0, col(j, w)), 2, 16, None, 0, lane))
            for word, source in ((3, got), (4, sib)):
                e_ins.append((source[0], (part, per), lambda j, w, col=e_col: (0, col(j)), word, 16, None, 0, lane))
                s_ins.append((source[0], (part, per), lambda j, w, col=s_far: (0, col(j)), word, 16, None, 0, lane))
    e_outs = [(expert_out, (None, per, width), lambda j, w: (w[0], j, 0), 5, per, None, 0, 0)]
    s_outs = [(shared_out, (per, width), lambda j, w: (w[0] * s_blocks + j, 0), 5, per, None, 0, 0)]
    for word, source in ((7, got), (8, sib)):
        e_outs.append((source[1], (per, half), lambda j, w: (j, 0), 6, per, word, 128, 0))
        s_outs.append((source[1], (per, half), lambda j, w: (steps + j, 0), 6, per, word, 128, 0))
    return (e_ins, e_outs), (s_ins, s_outs), words, (sent, got, sib)


def inverse_rms(values):
    return lax.rsqrt(jnp.mean(values * values, axis=-1, keepdims=True) + EPS)


def norm_back(values, inverse, gain, grad):
    scaled = grad * gain
    dotted = jnp.mean(scaled * values, axis=-1, keepdims=True)
    return inverse * scaled - values * (inverse * inverse * inverse) * dotted


def half_turn(pairs):
    size = pairs * HEAD_DIM
    row = lax.broadcasted_iota(jnp.int32, (size, size), 0)
    col = lax.broadcasted_iota(jnp.int32, (size, size), 1)
    return (row == (col ^ (HEAD_DIM // 2))).astype(BF)


def on_device(
    tokens,
    segment_ids,
    routes,
    cotangent,
    norm1_gain,
    qkv_weight,
    out_weight,
    norm2_gain,
    router_weight,
    shared_in,
    shared_out,
    expert_in,
    expert_out,
):
    local_len, seqs, width = tokens.shape
    count = local_len * seqs
    groups = lax.axis_size("head")
    ctxs = lax.axis_size("ctx")
    shards = lax.axis_size("fsdp")
    ctx = lax.axis_index("ctx")
    head = lax.axis_index("head")
    shard = lax.axis_index("fsdp")
    group_width = width // groups
    heads = group_width // HEAD_DIM
    block = local_len * groups
    span = seqs * block
    experts = expert_in.shape[0]
    rows_per = width // shards
    ff = expert_in.shape[2] // 2
    fs = shared_in.shape[1] // 2
    fs_part = fs // ctxs
    ctx_word = ctx.astype(jnp.int32).reshape(1)

    member = group_member()
    piece = fs // shards // ctxs
    tile = 256
    per = tile // shards
    steps, s_steps = ff // tile, fs_part // tile
    x_own = tokens.transpose(1, 0, 2)
    w_group = lax.dynamic_index_in_dim(qkv_weight.reshape(-1, 3, groups, group_width), head, 2, keepdims=False)
    w_group = fsdp_gather_small(w_group.reshape(-1, 3 * group_width), 0)
    small = jnp.concatenate([norm1_gain[None], norm2_gain[None], router_weight.T], axis=0)
    small = fsdp_gather_small(small, 1)
    x_line = line_gather_kernel(x_own, 0)
    gain_one, gain_two = small[0].astype(F32), small[1].astype(F32)
    w_router = small[2:]
    w_q, w_kv = w_group[:, :group_width], w_group[:, group_width:]
    w_q_turned = dot(w_q, half_turn(heads)).astype(BF)
    w_kv_turned = dot(w_kv, half_turn(2 * heads)).astype(BF)

    dz_own = cotangent.transpose(1, 0, 2).reshape(count, width)
    scale = HEAD_DIM**-0.5
    lane = lax.broadcasted_iota(jnp.int32, (1, block, 2 * group_width), 2)
    position = ctx * block + lax.broadcasted_iota(jnp.int32, (1, block, 2 * group_width), 1)
    index = (lane % (HEAD_DIM // 2)).astype(F32)
    angle = position.astype(F32) * jnp.exp(-math.log(ROPE_BASE) * 2.0 * index / HEAD_DIM)
    sign = jnp.where(lane % HEAD_DIM < HEAD_DIM // 2, -1.0, 1.0)
    cos_kv = jnp.where(lane < group_width, jnp.cos(angle), 1.0)
    sin_kv = jnp.where(lane < group_width, jnp.sin(angle) * sign, 0.0)
    cos_q, sin_q = cos_kv[:, :, :group_width] * scale, sin_kv[:, :, :group_width] * scale

    dz_blocks = group_gather(dz_own)
    x_f = once_there(x_line, dz_blocks[1], dz_blocks[2]).astype(F32)
    inverse_one = inverse_rms(x_f)
    normed = (x_f * inverse_one * gain_one).astype(BF)
    normed_rows = normed.reshape(span, width)

    def turned(weight, weight_turned, cos_table, sin_table):
        plain = dot(normed_rows, weight).reshape(seqs, block, -1)
        other = dot(normed_rows, weight_turned).reshape(seqs, block, -1)
        return (plain * cos_table + other * sin_table).astype(BF)

    key_value = turned(w_kv, w_kv_turned, cos_kv, sin_kv)
    kv_blocks = ctx_gather(key_value)
    queries = turned(w_q, w_q_turned, cos_q, sin_q)
    kv_near = jnp.stack(kv_blocks[:2])
    kv_far = jnp.stack(kv_blocks[2:])
    w_attn = fsdp_gather_small(out_weight, 0)

    def forward_bounds(tq, tk):
        nq = block // tq
        first = ctx * block + jnp.arange(nq, dtype=jnp.int32) * tq
        low = segment_ids[:, ::tq] // tk
        last_start = segment_ids[:, tq - 1 :: tq]
        clear_to = jnp.broadcast_to(first // tk, low.shape)
        clear_from = jnp.minimum((last_start + tk - 1) // tk, clear_to)
        clear_from = jnp.maximum(clear_from, low)
        clear_to = jnp.maximum(clear_to, clear_from)
        high = jnp.broadcast_to((first + tq - 1) // tk + 1, low.shape)
        return jnp.stack([low, clear_from, clear_to, high], axis=2).astype(jnp.int32)

    fwd_q, fwd_k = min(1024, block), min(512, block)
    bounds = forward_bounds(fwd_q, fwd_k)
    near_base = (ctx // 2) * 2
    far_base = near_base ^ 2
    near_words = jnp.stack([ctx, 0 * ctx, near_base]).astype(jnp.int32)
    far_words = jnp.stack([ctx, 0 * ctx + 2, far_base]).astype(jnp.int32)
    edge = near_base * (block // fwd_k)
    starts = segment_ids[:, None, :]
    state = attend_forward(near_words, jnp.maximum(bounds, edge), queries, kv_near, starts, fwd_q, fwd_k, None)
    e_pieces, s_pieces, words, sent = weight_pieces(
        shared_in, shared_out, expert_in, expert_out, state[0], member, ctx % 2, shard,
        shards, ctxs, steps, s_steps, per, piece,
    )
    attended, attended_low, lse = attend_forward(
        far_words, jnp.minimum(bounds, edge), queries, kv_far, starts, fwd_q, fwd_k, state
    )
    attended_low = after(attended_low, *sent[2], w_attn)
    sent = attended_low.reshape(seqs, groups, local_len, group_width)
    back = lax.all_to_all(sent, "head", split_axis=1, concat_axis=3, tiled=True)
    attn_rows = back.reshape(count, width)

    x_rows = x_own.reshape(count, width).astype(F32)
    hidden = x_rows + dot(attn_rows, w_attn)
    inverse_two = inverse_rms(hidden)
    normed_two = (hidden * inverse_two * gain_two).astype(BF)
    route_rows = routes.reshape(local_len, seqs, 2).transpose(1, 0, 2).reshape(count, 2)
    logits = dot_t(normed_two, w_router)
    ids = jnp.arange(experts, dtype=jnp.int32)
    picks = (route_rows[:, :, None] == ids).astype(F32)
    chosen = jnp.sum(logits[:, None, :] * picks, axis=2)
    gate_first = 1.0 / (1.0 + jnp.exp(chosen[:, 1:] - chosen[:, :1]))
    gates = jnp.concatenate([gate_first, 1.0 - gate_first], axis=1)
    combine = jnp.sum(gates[:, :, None] * picks, axis=1)

    xn_blocks = group_gather(normed_two)
    combine_t = combine.T
    c_one, c_two = group_swap(combine_t, 1), group_swap(combine_t, 2)
    combine_all = jnp.concatenate([combine_t, c_one, c_two, group_swap(c_one, 2)], axis=1)
    c_own = lax.dynamic_index_in_dim(combine_all, member, 0, keepdims=False)[:, None]
    y_part, dx_part, dc, g_one, g_two = gated_mlp(
        xn_blocks, dz_blocks, c_own, words, e_pieces, s_pieces, steps, s_steps, groups if paired() else 0
    )
    dc_blocks = dc.reshape(ctxs, count)
    dc_got = [
        dc_blocks[0],
        group_swap(dc_blocks[1], 1),
        group_swap(dc_blocks[2], 2),
        group_swap(group_swap(dc_blocks[3], 1), 2),
    ]
    dcombine = sum(
        dc_got[k][:, None] * ((member ^ k) == ids).astype(F32)[None, :] for k in range(ctxs)
    )
    dx_blocks = dx_part.reshape(ctxs, count, width)
    dx_near = group_scatter_near([dx_blocks[k] for k in range(ctxs)])
    g_part = sum_parts(g_one, g_two)
    dxn2 = dx_near[0].astype(F32) + group_swap(dx_near[1], 1).astype(F32) + group_swap(dx_near[2], 2).astype(F32)

    dchosen = jnp.sum(dcombine[:, None, :] * picks, axis=2)
    dfirst = gates[:, :1] * gates[:, 1:] * (dchosen[:, :1] - dchosen[:, 1:])
    dlogits = (dfirst * (picks[:, 0] - picks[:, 1])).astype(BF)
    router_part = dot_l(normed_two, dlogits)
    dxn2 = dxn2 + dot(dlogits, w_router)
    dz_rows = dz_own.astype(F32)
    dh = dz_rows + norm_back(hidden, inverse_two, gain_two, dxn2)
    gain_two_part = jnp.sum(dxn2 * hidden * inverse_two, axis=0)
    dh_low = dh.astype(BF)
    g_attn = dot_l(attn_rows, dh_low)
    g_attn = jnp.concatenate(
        [g_attn, gain_two_part[:, None], router_part, jnp.zeros((width, 127 - experts), F32)], axis=1
    ).astype(BF)
    dattn = dot_t(dh_low, w_attn).astype(BF).reshape(seqs, local_len, width)
    grad_out = lax.all_to_all(
        dattn.reshape(seqs, local_len, groups, group_width), "head", split_axis=2, concat_axis=1, tiled=True
    ).reshape(seqs, block, group_width)

    y_blocks = after(y_part, dh_low).reshape(ctxs, count, width)
    y_near = group_scatter_near([y_blocks[k] for k in range(ctxs)])
    y_near = [y_near[0], group_swap(y_near[1], 1), group_swap(y_near[2], 2)]
    grad_out = once_there(grad_out, y_near[1], y_near[2])
    y_own = sum(v.astype(F32) for v in y_near)
    output = (hidden + y_own).astype(BF).reshape(seqs, local_len, width).transpose(1, 0, 2)

    delta = jnp.sum((grad_out.astype(F32) * attended).reshape(seqs, block, heads, HEAD_DIM), axis=3)
    stats = jnp.concatenate(
        [lse[:, :heads], delta.transpose(0, 2, 1), jnp.zeros((seqs, 8 - 2 * heads, block), F32)],
        axis=1,
    )
    tq = tk = min(512, block)
    tile_last = ctx * block + (jnp.arange(block // tq, dtype=jnp.int32) + 1) * tq - 1
    tile_key = jnp.arange(ctxs * block // tk, dtype=jnp.int32)
    q_low = jnp.sum((tile_last[None, :] < (tile_key * tk)[:, None]).astype(jnp.int32), axis=1)
    q_high = jnp.sum(((segment_ids[:, ::tq] // tk)[:, None, :] <= tile_key[None, :, None]).astype(jnp.int32), axis=2)
    q_low = jnp.broadcast_to(q_low, q_high.shape)
    back_bounds = jnp.stack([q_low, q_high], axis=2).astype(jnp.int32)
    edges = segment_ids[:, tq - 1 :: tq]
    dq_far, far_parts = attend_backward(
        far_words, back_bounds, edges, queries, kv_far, grad_out, stats, starts, tq, tk
    )
    far_sum = (far_parts[0].astype(F32) + swap_with(far_parts[1], "ctx", 1).astype(F32)).astype(BF)
    far_got = swap_with(far_sum, "ctx", 2)
    whole_parts = exchange_parts(once_there(g_part, dq_far))
    gathered = share_parts(whole_parts)
    dq_near, near_parts = attend_backward(
        near_words, back_bounds, edges, queries, kv_near, once_there(grad_out, whole_parts, far_sum), stats, starts, tq, tk
    )
    if paired():
        g_attn = half_sum(g_attn, 0, "fsdp", shard, 1, dq_near).astype(BF)
        g_attn = half_sum(g_attn, 0, "ctx", ctx % 2, 1).astype(BF)
        g_attn = half_sum(g_attn, 0, "ctx", ctx // 2, 2).astype(BF)
    dkv = near_parts[0].astype(F32) + swap_with(near_parts[1], "ctx", 1).astype(F32) + far_got.astype(F32)
    dq = ((dq_far + dq_near) * scale).astype(BF).astype(F32)
    dkv = dkv.astype(BF).astype(F32)

    def turned_back(grad, cos_table, sin_table, pairs):
        other = (grad * sin_table).astype(BF).reshape(span, -1)
        back = dot(other, half_turn(pairs)).reshape(seqs, block, -1)
        return (grad * cos_table + back).astype(BF).reshape(span, -1)

    d_q = turned_back(dq, cos_q * HEAD_DIM**0.5, sin_q * HEAD_DIM**0.5, heads)
    d_kv = turned_back(dkv, cos_kv, sin_kv, 2 * heads)
    dxn1_part = (dot_t(d_q, w_q) + dot_t(d_kv, w_kv)).reshape(seqs, block, width)
    g_q, g_kv = dot_l(normed_rows, d_q), dot_l(normed_rows, d_kv)
    gain_one_part = jnp.sum(dxn1_part * x_f * inverse_one, axis=(0, 1))
    filler = jnp.zeros((width, 128 - 3 * group_width % 128 - 1), F32)
    g_qkv = jnp.concatenate([g_q, g_kv, gain_one_part[:, None], filler], axis=1).astype(BF)
    if paired():
        blocks = dxn1_part.astype(BF).reshape(seqs, groups, local_len, width).transpose(1, 0, 2, 3)
        dxn1, qkv_grad, gain_one_grad, g_attn = tail_kernel(blocks.reshape(groups, count, width), g_qkv, g_attn, 1)
        gain_one_grad = gain_one_grad[:, 3 * group_width % 128]
    else:
        dxn1 = line_scatter(dxn1_part.astype(BF), 1).reshape(count, width)
        g_qkv = lax.psum(lax.psum_scatter(g_qkv, "fsdp", scatter_dimension=0, tiled=True), "ctx")
        g_qkv = line_gather(g_qkv[:, None], 1).astype(F32)
        qkv_grad = g_qkv[..., : 3 * group_width].reshape(rows_per, groups, 3, group_width)
        qkv_grad = qkv_grad.transpose(0, 2, 1, 3).reshape(rows_per, 3 * width)
        gain_one_grad = jnp.sum(g_qkv[..., 3 * group_width], axis=1)
        g_attn = lax.psum(lax.psum_scatter(g_attn, "fsdp", scatter_dimension=0, tiled=True), ("ctx", "head"))
        g_attn = g_attn.astype(F32)
    dx_norm = norm_back(x_rows, inverse_rms(x_rows), gain_one, dxn1)
    tokens_grad = (dh + dx_norm).reshape(seqs, local_len, width).transpose(1, 0, 2)

    expert_in_grad, expert_out_grad, shared_in_grad, shared_out_grad = unpack(
        gathered, shards, steps, s_steps, width
    )
    out_grad, side = g_attn[:, :width], g_attn[:, width:]
    return (
        output,
        tokens_grad,
        gain_one_grad,
        qkv_grad,
        out_grad,
        side[:, 0],
        side[:, 1 : 1 + experts],
        shared_in_grad,
        shared_out_grad,
        expert_in_grad,
        expert_out_grad,
    )


def solution(mesh):
    rows = P(("ctx", "head"), "fsdp", None)
    vector = P("fsdp")
    matrix = P("fsdp", None)
    stack = P(None, "fsdp", None)
    return jax.shard_map(
        on_device,
        mesh=mesh,
        in_specs=(
            rows,
            P("fsdp", "ctx"),
            P(("ctx", "head"), "fsdp", None, None),
            rows,
            vector,
            matrix,
            matrix,
            vector,
            matrix,
            matrix,
            matrix,
            stack,
            stack,
        ),
        out_specs=(rows, rows, vector, matrix, matrix, vector, matrix, matrix, matrix, stack, stack),
        check_vma=False,
    )
```

```python
import functools
import math

import jax
import jax.numpy as jnp
from jax import lax
from jax.experimental import pallas as pl
from jax.experimental.pallas import tpu as pltpu
from jax.sharding import PartitionSpec as P

HEAD_DIM = 64
EPS = 1e-06
NEG = -1e30
ROPE_BASE = 10000.0
BF = jnp.bfloat16
F32 = jnp.float32
MB = 1 << 20


def swap_with(value, axis_name, bit):
    size = lax.axis_size(axis_name)
    return lax.ppermute(value, axis_name, [(i, i ^ bit) for i in range(size)])


def fsdp_gather(value, axis):
    return lax.all_gather(value, "fsdp", axis=axis, tiled=True)


def fsdp_gather_small(value, axis):
    if lax.axis_size("fsdp") != 2:
        return fsdp_gather(value, axis)
    other = swap_with(value, "fsdp", 1)
    first = lax.axis_index("fsdp") == 0
    return jnp.where(
        first, jnp.concatenate([value, other], axis=axis), jnp.concatenate([other, value], axis=axis)
    )


def line_gather(value, axis):
    count = lax.axis_size("head")
    mine = lax.axis_index("head")
    part = value.shape[axis]
    up = [(i, i + 1) for i in range(count - 1)]
    down = [(i + 1, i) for i in range(count - 1)]
    below, above = [], []
    rising, falling = value, value
    for _ in range(count - 1):
        rising = lax.ppermute(rising, "head", up)
        falling = lax.ppermute(falling, "head", down)
        below.insert(0, rising)
        above.append(falling)
    line = jnp.concatenate(below + [value] + above, axis=axis)
    return lax.dynamic_slice_in_dim(line, (count - 1 - mine) * part, count * part, axis)


def line_scatter(value, axis):
    count = lax.axis_size("head")
    mine = lax.axis_index("head")
    part = value.shape[axis] // count
    up = [(i, i + 1) for i in range(count - 1)]
    down = [(i + 1, i) for i in range(count - 1)]

    def block(index):
        index = jnp.clip(index, 0, count - 1)
        return lax.dynamic_slice_in_dim(value, index * part, part, axis).astype(F32)

    rising, falling = None, None
    for step in range(count - 1):
        upward = block(count - 1 - step + mine)
        downward = block(step - (count - 1) + mine)
        if step:
            upward = upward + rising.astype(F32)
            downward = downward + falling.astype(F32)
        rising = lax.ppermute(upward.astype(BF), "head", up)
        falling = lax.ppermute(downward.astype(BF), "head", down)
    return block(mine) + rising.astype(F32) + falling.astype(F32)


def after(value, *others):
    return lax.optimization_barrier((value, *others))[0] if others else value


def once_there(value, *others):
    zero = jnp.float32(0)
    for other in others:
        first = lax.slice(other, (0,) * other.ndim, (1,) * other.ndim)
        zero += first.reshape(()).astype(F32) * 0.0
    return value + zero.astype(value.dtype)


def paired():
    return lax.axis_size("fsdp") == 2


def group_member():
    ctx = lax.axis_index("ctx")
    return (ctx // 2) * 2 + lax.axis_index("fsdp") if paired() else ctx


def group_swap(value, bit):
    if paired() and bit == 1:
        return swap_with(value, "fsdp", 1)
    return swap_with(value, "ctx", bit)


def group_gather(value):
    half = value.shape[0] // 2
    one, two = group_swap(value, 1), group_swap(value, 2)
    far = jnp.concatenate([group_swap(one[:half], 2), group_swap(two[half:], 1)], axis=0)
    return [value, one, two, far]


def group_scatter_near(blocks):
    own, one, two, far = blocks
    half = far.shape[0] // 2
    by_one, by_two = group_swap(far[:half], 1), group_swap(far[half:], 2)
    two = jnp.concatenate([(two[:half].astype(F32) + by_one.astype(F32)).astype(BF), two[half:]], axis=0)
    one = jnp.concatenate([one[:half], (one[half:].astype(F32) + by_two.astype(F32)).astype(BF)], axis=0)
    return own, one, two


def half_sum(value, axis, axis_name, bit_value, bit, *others):
    part = value.shape[axis] // 2
    sent = lax.dynamic_slice_in_dim(value, (1 - bit_value) * part, part, axis)
    kept = lax.dynamic_slice_in_dim(value, bit_value * part, part, axis)
    got = once_there(swap_with(sent, axis_name, bit), *others)
    return kept.astype(F32) + got.astype(F32)


def pack(d_in, d_out, parts, wide):
    packed = []
    for d in (d_in, d_out):
        j, r, w = d.shape
        d = d.reshape(j, parts, r // parts, w // wide, wide).transpose(1, 0, 3, 2, 4)
        packed.append(d.reshape(parts, j, -1, wide))
    return jnp.concatenate(packed, axis=2)


def sum_parts(one, two, more=None):
    wide = 256
    groups, shards = lax.axis_size("head"), lax.axis_size("fsdp")
    if paired():
        parts, over = groups, "head"
        packed = one.astype(F32) + swap_with(two, "ctx", 1).astype(F32)
        packed = packed.astype(BF).reshape(parts, -1, wide)
        if more is not None:
            more = half_sum(more, 1, "ctx", lax.axis_index("ctx") % 2, 1).astype(BF)
    else:
        parts, over = groups * shards, ("fsdp", "head")
        packed = pack(one, two, parts, wide).reshape(parts, -1, wide)
    if more is not None:
        j, r, w = more.shape
        more = more.reshape(j, parts, r // parts, w // wide, wide).transpose(1, 0, 3, 2, 4)
        packed = jnp.concatenate([packed, more.reshape(parts, -1, wide)], axis=1)
    packed = packed.reshape(-1, wide)
    return lax.psum_scatter(packed, over, scatter_dimension=0, tiled=True)


def exchange_parts(part, *others):
    if not paired():
        return part
    core, shard = lax.axis_index("ctx") % 2, lax.axis_index("fsdp")
    ctxs = lax.axis_size("ctx")
    moves = [(f * ctxs + c, (1 - f) * ctxs + (c ^ 1)) for f in range(2) for c in range(ctxs) if c % 2 != f]
    got = once_there(lax.ppermute(part, ("fsdp", "ctx"), moves), *others)
    return jnp.where(core == shard, part, got)


def share_parts(part):
    whole = lax.all_gather(part, ("ctx", "head"), axis=0, tiled=False)
    return whole.reshape((lax.axis_size("ctx"), lax.axis_size("head")) + part.shape)


def ctx_gather(value):
    blocks = [value]
    bit = lax.axis_size("ctx") // 2
    found = {0: value}
    while bit:
        for k in list(found):
            found[k ^ bit] = swap_with(found[k], "ctx", bit)
        bit //= 2
    blocks = [found[k] for k in range(len(found))]
    return blocks


def ctx_scatter(blocks):
    held = {k: blocks[k] for k in range(len(blocks))}
    bit = 1
    while len(held) > 1:
        kept = {}
        for k in list(held):
            if not k & bit:
                got = swap_with(held[k | bit], "ctx", bit)
                kept[k] = held[k].astype(F32) + got.astype(F32)
        held = {k: (v if len(kept) == 1 else v.astype(BF)) for k, v in kept.items()}
        bit *= 2
    return held[0]


MESH_ID = pl.DeviceIdType.MESH


def enter(partners):
    barrier = pltpu.get_barrier_semaphore()
    for there, device in partners:
        if there is None:
            pl.semaphore_signal(barrier, inc=1, device_id=device, device_id_type=MESH_ID)
        else:

            @pl.when(there)
            def _(device=device):
                pl.semaphore_signal(barrier, inc=1, device_id=device, device_id_type=MESH_ID)

    here = sum(1 if there is None else there.astype(jnp.int32) for there, _ in partners)
    pl.semaphore_wait(barrier, here)


def send(src, dst, sems, device):
    return pltpu.make_async_remote_copy(
        src_ref=src, dst_ref=dst, send_sem=sems[0], recv_sem=sems[1], device_id=device, device_id_type=MESH_ID
    )


def line_relay(place, z, count, up, down, up_sems, down_sems):
    def copy(b, device, sems):
        return send(place(b), place(b), (sems[0].at[b], sems[1].at[b]), device)

    def pass_on(far):
        low, high = z - far, z + far

        @pl.when((low >= 0) & (z < count - 1))
        def _():
            if far:
                copy(low, up, up_sems).wait_recv()
            copy(low, up, up_sems).start()

        @pl.when((high < count) & (z > 0))
        def _():
            if far:
                copy(high, down, down_sems).wait_recv()
            copy(high, down, down_sems).start()

    def last(b):
        @pl.when((b < z) & (z == count - 1))
        def _():
            copy(b, up, up_sems).wait_recv()

        @pl.when((b > z) & (z == 0))
        def _():
            copy(b, down, down_sems).wait_recv()

    def sent(b):
        @pl.when((b <= z) & (z < count - 1))
        def _():
            copy(b, up, up_sems).wait_send()

        @pl.when((b >= z) & (z > 0))
        def _():
            copy(b, down, down_sems).wait_send()

    blocks = range(count)
    run = [functools.partial(pass_on, far) for far in blocks]
    return run, [functools.partial(last, b) for b in blocks], [functools.partial(sent, b) for b in blocks]


def line_gather_kernel(value, cid):
    count = lax.axis_size("head")
    seqs, rows, width = value.shape

    def kernel(v_ref, o_ref, us, ur, ds, dr, local):
        z = lax.axis_index("head")
        up, down = {"head": jnp.minimum(z + 1, count - 1)}, {"head": jnp.maximum(z - 1, 0)}

        def place(b):
            return o_ref.at[:, pl.ds(pl.multiple_of(b * rows, rows), rows), :]

        own = pltpu.make_async_copy(v_ref, o_ref.at[:, pl.ds(pl.multiple_of(z * rows, rows), rows), :], local)
        own.start()
        enter([(z < count - 1, up), (z > 0, down)])
        own.wait()
        run, last, sent = line_relay(place, z, count, up, down, (us, ur), (ds, dr))
        for step in (*run, *last, *sent):
            step()

    any_space = pl.BlockSpec(memory_space=pltpu.VMEM)
    return pl.pallas_call(
        kernel,
        out_shape=jax.ShapeDtypeStruct((seqs, count * rows, width), value.dtype),
        in_specs=[any_space],
        out_specs=any_space,
        scratch_shapes=[pltpu.SemaphoreType.DMA((count,))] * 4 + [pltpu.SemaphoreType.DMA],
        compiler_params=pltpu.CompilerParams(
            collective_id=cid, has_side_effects=True, vmem_limit_bytes=16 * MB
        ),
        name="line_gather",
        cost_estimate=pl.CostEstimate(flops=0, bytes_accessed=180 * MB, transcendentals=0),
    )(value)


def tail_kernel(parts, grads, others, cid):
    count, rows, width = parts.shape
    high, wide = grads.shape
    half, quarter, eighth = high // 2, high // 4, high // 8

    apart = others.shape[1]

    def kernel(p_ref, g_ref, a_ref, o_ref, q_ref, gain_ref, attn_ref, a_s, at_s, q_s, up_in, up_out, dn_in, dn_out, s1, r1, s2, r2, r3, *sems):
        us, ur, ds, dr, gus, gur, gds, gdr, aus, aur, ads, adr, xs, ys, cs, yg, cg, ya, ca = sems
        z, f, c = lax.axis_index("head"), lax.axis_index("fsdp"), lax.axis_index("ctx")
        core, upper = lax.rem(c, 2), lax.div(c, 2)
        up, down = {"head": jnp.minimum(z + 1, count - 1)}, {"head": jnp.maximum(z - 1, 0)}
        over_x = {"fsdp": 1 - f}
        over_core = {"ctx": upper * 2 + 1 - core}
        over_y = {"ctx": (1 - upper) * 2 + core}
        enter([(z < count - 1, up), (z > 0, down), (None, over_x), (None, over_core), (None, over_y)])

        def rise(d):
            return send(up_out.at[d], up_in.at[d], (us.at[d], ur.at[d]), up)

        def fall(d):
            return send(dn_out.at[d], dn_in.at[d], (ds.at[d], dr.at[d]), down)

        def rising(d):
            @pl.when(z < d)
            def _():
                @pl.when(z == 0)
                def _():
                    up_out[d] = p_ref[d]

                @pl.when(z > 0)
                def _():
                    rise(d).wait_recv()
                    up_out[d] = (p_ref[d].astype(F32) + up_in[d].astype(F32)).astype(BF)

                rise(d).start()

        def falling(d):
            @pl.when(z > d)
            def _():
                @pl.when(z == count - 1)
                def _():
                    dn_out[d] = p_ref[d]

                @pl.when(z < count - 1)
                def _():
                    fall(d).wait_recv()
                    dn_out[d] = (p_ref[d].astype(F32) + dn_in[d].astype(F32)).astype(BF)

                fall(d).start()

        by_x = send(g_ref.at[pl.ds(pl.multiple_of((1 - f) * half, half), half), :], r1, (xs.at[0], xs.at[1]), over_x)
        by_core = send(
            s1.at[pl.ds(pl.multiple_of((1 - core) * quarter, quarter), quarter), :], r2, (cs.at[0], cs.at[1]), over_core
        )
        by_y = send(
            s2.at[pl.ds(pl.multiple_of((1 - upper) * eighth, eighth), eighth), :], r3, (ys.at[0], ys.at[1]), over_y
        )
        a_s[z] = a_ref[...]
        by_x.start()
        at_low, at_high = z == 0, z == count - 1
        pl.when(at_low)(lambda: rising(count - 1))
        pl.when(at_high)(lambda: falling(0))
        by_x.wait_recv()
        s1[...] = (g_ref[pl.ds(pl.multiple_of(f * half, half), half), :].astype(F32) + r1[...].astype(F32)).astype(BF)
        by_core.start()
        by_core.wait_recv()
        mine = s1[pl.ds(pl.multiple_of(core * quarter, quarter), quarter), :]
        s2[...] = (mine.astype(F32) + r2[...].astype(F32)).astype(BF)
        by_y.start()
        by_y.wait_recv()
        mine = s2[pl.ds(pl.multiple_of(upper * eighth, eighth), eighth), :]
        q_s[core, upper, z] = (mine.astype(F32) + r3[...].astype(F32)).astype(BF)
        run_q, last, sent = line_relay(
            lambda b: q_s.at[core, upper, b], z, count, up, down, (gus, gur), (gds, gdr)
        )
        also, also_last, also_sent = line_relay(
            lambda b: a_s.at[b], z, count, up, down, (aus, aur), (ads, adr)
        )
        run = [(lambda n=n: (run_q[n](), also[n]())) for n in range(count)]
        last, sent = [*last, *also_last], [*sent, *also_sent]
        run[0]()
        for d in range(1, count - 1):
            pl.when(at_low)(lambda d=d: rising(count - 1 - d))
            pl.when(at_high)(lambda d=d: falling(d))
        pl.when(jnp.logical_not(at_low))(lambda: rising(count - 1))
        run[1]()
        pl.when(jnp.logical_not(at_high))(lambda: falling(0))
        run[2]()
        for d in range(1, count - 1):
            pl.when(jnp.logical_not(at_low))(lambda d=d: rising(count - 1 - d))
            pl.when(jnp.logical_not(at_high))(lambda d=d: falling(d))
        for step in (*run[3:], *last):
            step()
        to_y = send(q_s.at[core, upper], q_s.at[core, upper], (yg.at[0], yg.at[1]), over_y)
        to_y.start()
        summed = a_s[0].astype(F32)
        for n in range(1, count):
            summed += a_s[n].astype(F32)
        at_s[core, upper] = summed.astype(BF)
        a_to_y = send(at_s.at[core, upper], at_s.at[core, upper], (ya.at[0], ya.at[1]), over_y)
        a_to_y.start()

        total = p_ref[z].astype(F32)
        o_ref[...] = total

        @pl.when(z > 0)
        def _():
            rise(z).wait_recv()
            o_ref[...] += up_in[z].astype(F32)

        @pl.when(z < count - 1)
        def _():
            fall(z).wait_recv()
            o_ref[...] += dn_in[z].astype(F32)

        to_y.wait_recv()
        to_core = send(q_s.at[core], q_s.at[core], (cg.at[0], cg.at[1]), over_core)
        to_core.start()
        a_to_y.wait_recv()
        a_to_core = send(at_s.at[core], at_s.at[core], (ca.at[0], ca.at[1]), over_core)
        a_to_core.start()
        to_core.wait_recv()
        a_to_core.wait_recv()
        part = width // count
        for a in range(2):
            for b in range(2):
                at = slice((a * 2 + b) * eighth, (a * 2 + b + 1) * eighth)
                gain = jnp.zeros((eighth, 128), F32)
                for n in range(count):
                    block = q_s[a, b, n].astype(F32)
                    for t in range(3):
                        col = t * width + n * part
                        q_ref[at, col : col + part] = block[:, t * part : (t + 1) * part]
                    gain += block[:, wide - 128 :]
                gain_ref[at, :] = gain
                attn_ref[at, :] = at_s[a, b].astype(F32)
        for d in range(count):

            @pl.when(z < d)
            def _(d=d):
                rise(d).wait_send()

            @pl.when(z > d)
            def _(d=d):
                fall(d).wait_send()

        for step in sent:
            step()
        for copy in (by_x, by_core, by_y, to_y, to_core, a_to_y, a_to_core):
            copy.wait_send()

    vmem = pl.BlockSpec(memory_space=pltpu.VMEM)
    block = lambda *shape: pltpu.VMEM(shape, BF)
    return pl.pallas_call(
        kernel,
        out_shape=(
            jax.ShapeDtypeStruct((rows, width), F32),
            jax.ShapeDtypeStruct((half, 3 * width), F32),
            jax.ShapeDtypeStruct((half, 128), F32),
            jax.ShapeDtypeStruct((half, apart), F32),
        ),
        in_specs=[vmem] * 3,
        out_specs=[vmem] * 4,
        scratch_shapes=[block(count, eighth, apart), block(2, 2, eighth, apart), block(2, 2, count, eighth, wide)]
        + [block(count, rows, width)] * 4
        + [block(half, wide), block(half, wide), block(quarter, wide), block(quarter, wide), block(eighth, wide)]
        + [pltpu.SemaphoreType.DMA((count,))] * 12
        + [pltpu.SemaphoreType.DMA((2,))] * 7,
        compiler_params=pltpu.CompilerParams(
            collective_id=cid, has_side_effects=True, vmem_limit_bytes=40 * MB
        ),
        name="tail",
        cost_estimate=pl.CostEstimate(flops=0, bytes_accessed=220 * MB, transcendentals=0),
    )(parts, grads, others)


def dot_t(a, b):
    return lax.dot_general(a, b, (((1,), (1,)), ((), ())), preferred_element_type=F32)


def dot_l(a, b):
    return lax.dot_general(a, b, (((0,), (0,)), ((), ())), preferred_element_type=F32)


def dot(a, b):
    return jnp.dot(a, b, preferred_element_type=F32)


def attend_forward(words, bounds, queries, keys_values, starts, tq, tk, state):
    seqs, rows, width = queries.shape
    heads = width // HEAD_DIM
    blocks = keys_values.shape[0]
    per = rows // tk

    def kernel(word_ref, bounds_ref, q_ref, kv_ref, seg_ref, *refs):
        if state is None:
            acc_ref, row_ref = refs
        else:
            acc_in, row_in, o_ref, low_ref, lse_ref = refs
        s, i = pl.program_id(0), pl.program_id(1)
        here, first = word_ref[0], word_ref[1]
        seg = seg_ref[0]
        row_pos = here * rows + i * tq + lax.broadcasted_iota(jnp.int32, (tk, tq), 1)
        under = lax.broadcasted_iota(jnp.int32, (tk, tq), 0)

        def step(masked, t, carry):
            at = (lax.div(t, per) ^ here) - first
            off = pl.multiple_of(lax.rem(t, per) * tk, tk)
            new = []
            if masked:
                key_pos = t * tk + under
                seen = (key_pos <= row_pos) & (key_pos >= seg)
            for h in range(heads):
                top, total, acc = carry[3 * h : 3 * h + 3]
                cols = slice(h * HEAD_DIM, (h + 1) * HEAD_DIM)
                vals = slice(width + h * HEAD_DIM, width + (h + 1) * HEAD_DIM)
                scores = dot_t(kv_ref[at, 0, pl.ds(off, tk), cols], q_ref[0, :, cols])
                if masked:
                    scores = jnp.where(seen, scores, NEG)
                new_top = jnp.maximum(top, jnp.max(scores, axis=0, keepdims=True))
                weights = jnp.exp(scores - new_top)
                fade = jnp.exp(top - new_top)
                total = total * fade + jnp.sum(weights, axis=0, keepdims=True)
                acc = acc * fade + dot_l(kv_ref[at, 0, pl.ds(off, tk), vals], weights.astype(BF))
                new += [new_top, total, acc]
            return tuple(new)

        carry = []
        for h in range(heads):
            if state is None:
                carry += [jnp.full((1, tq), NEG, F32), jnp.zeros((1, tq), F32), jnp.zeros((HEAD_DIM, tq), F32)]
            else:
                carry += [
                    row_in[0, h : h + 1, :],
                    row_in[0, heads + h : heads + h + 1, :],
                    acc_in[0, h * HEAD_DIM : (h + 1) * HEAD_DIM, :],
                ]
        carry = tuple(carry)
        b = [bounds_ref[s, i, n] for n in range(4)]
        carry = lax.fori_loop(b[0], b[1], functools.partial(step, True), carry)
        carry = lax.fori_loop(b[1], b[2], functools.partial(step, False), carry)
        carry = lax.fori_loop(b[2], b[3], functools.partial(step, True), carry)
        tops, totals, accs = carry[::3], carry[1::3], carry[2::3]
        filler = jnp.zeros((8 - 2 * heads, tq), F32)
        if state is None:
            acc_ref[0] = jnp.concatenate(accs, axis=0)
            row_ref[0] = jnp.concatenate([*tops, *totals, filler], axis=0)
        else:
            result = jnp.concatenate([acc / total for acc, total in zip(accs, totals)], axis=0).T
            o_ref[0] = result
            low_ref[0] = result.astype(BF)
            logs = [top + jnp.log(total) for top, total in zip(tops, totals)]
            lse_ref[0] = jnp.concatenate([*logs, *totals, filler], axis=0)

    rows_spec = pl.BlockSpec((1, tq, width), lambda s, i, *_: (s, i, 0))
    acc_spec = pl.BlockSpec((1, width, tq), lambda s, i, *_: (s, 0, i))
    stat_spec = pl.BlockSpec((1, 8, tq), lambda s, i, *_: (s, 0, i))
    stat_shape = jax.ShapeDtypeStruct((seqs, 8, rows), F32)
    if state is None:
        out_shape = (jax.ShapeDtypeStruct((seqs, width, rows), F32), stat_shape)
        more, out_specs = [], [acc_spec, stat_spec]
    else:
        shape = (seqs, rows, width)
        out_shape = (jax.ShapeDtypeStruct(shape, F32), jax.ShapeDtypeStruct(shape, BF), stat_shape)
        more, out_specs = [acc_spec, stat_spec], [rows_spec, rows_spec, stat_spec]
    return pl.pallas_call(
        kernel,
        out_shape=out_shape,
        grid_spec=pltpu.PrefetchScalarGridSpec(
            num_scalar_prefetch=2,
            grid=(seqs, rows // tq),
            in_specs=[
                rows_spec,
                pl.BlockSpec((blocks, 1, rows, 2 * width), lambda s, i, *_: (0, s, 0, 0)),
                pl.BlockSpec((1, 1, tq), lambda s, i, *_: (s, 0, i)),
                *more,
            ],
            out_specs=out_specs,
        ),
        compiler_params=pltpu.CompilerParams(vmem_limit_bytes=48 * MB),
        name="attend_forward",
        cost_estimate=pl.CostEstimate(
            flops=int(2 * 2 * seqs * heads * rows * rows * 2 * HEAD_DIM * 4),
            bytes_accessed=64 * MB,
            transcendentals=int(seqs * heads * rows * rows * 2),
        ),
    )(words, bounds, queries, keys_values, starts, *(state or ()))


def attend_backward(words, bounds, edges, queries, keys_values, grads, stats, starts, tq, tk):
    seqs, rows, width = queries.shape
    heads = width // HEAD_DIM
    blocks = keys_values.shape[0]
    per = rows // tk

    def kernel(word_ref, bounds_ref, edges_ref, q_ref, kv_ref, do_ref, stat_ref, seg_ref, dq_ref, dkv_ref, acc):
        s = pl.program_id(0)
        here = word_ref[0]
        t = word_ref[2] * per + pl.program_id(1)

        @pl.when(pl.program_id(1) == 0)
        def _():
            dq_ref[...] = jnp.zeros_like(dq_ref)

        acc[...] = jnp.zeros_like(acc)
        lane = lax.broadcasted_iota(jnp.int32, (tk, tq), 1)
        key_pos = t * tk + lax.broadcasted_iota(jnp.int32, (tk, tq), 0)

        def tile(masked, i):
            off = pl.multiple_of(i * tq, tq)
            if masked:
                row_pos = here * rows + off + lane
                seen = (key_pos <= row_pos) & (key_pos >= seg_ref[0, 0:1, pl.ds(off, tq)])
            for h in range(heads):
                cols = slice(h * HEAD_DIM, (h + 1) * HEAD_DIM)
                vals = slice(width + h * HEAD_DIM, width + (h + 1) * HEAD_DIM)
                q = q_ref[0, pl.ds(off, tq), cols]
                do = do_ref[0, pl.ds(off, tq), cols]
                k = kv_ref[0, 0, :, cols]
                v = kv_ref[0, 0, :, vals]
                scores = dot_t(k, q)
                weights = jnp.exp(scores - stat_ref[0, h : h + 1, pl.ds(off, tq)])
                if masked:
                    weights = jnp.where(seen, weights, 0.0)
                dweights = dot_t(v, do)
                dscores = weights * (dweights - stat_ref[0, heads + h : heads + h + 1, pl.ds(off, tq)])
                dscores = dscores.astype(BF)
                acc[h] += dot(dscores, q)
                acc[heads + h] += dot(weights.astype(BF), do)
                dq_ref[0, pl.ds(off, tq), cols] += dot_l(dscores, k)

        def step(i, carry):
            first = here * rows + i * tq
            clear = (edges_ref[s, i] <= t * tk) & (t * tk + tk - 1 <= first)

            @pl.when(clear)
            def _():
                tile(False, i)

            @pl.when(jnp.logical_not(clear))
            def _():
                tile(True, i)

            return carry

        lax.fori_loop(bounds_ref[s, t, 0], bounds_ref[s, t, 1], step, 0)
        dkv_ref[0, 0] = jnp.concatenate([acc[n] for n in range(2 * heads)], axis=1).astype(BF)

    at = lambda s, t, w, *_: (((w[2] + t // per) ^ w[0]) - w[1], s, t % per, 0)
    return pl.pallas_call(
        kernel,
        out_shape=(
            jax.ShapeDtypeStruct((seqs, rows, width), F32),
            jax.ShapeDtypeStruct((blocks, seqs, rows, 2 * width), BF),
        ),
        grid_spec=pltpu.PrefetchScalarGridSpec(
            num_scalar_prefetch=3,
            grid=(seqs, blocks * per),
            in_specs=[
                pl.BlockSpec((1, rows, width), lambda s, t, *_: (s, 0, 0)),
                pl.BlockSpec((1, 1, tk, 2 * width), at),
                pl.BlockSpec((1, rows, width), lambda s, t, *_: (s, 0, 0)),
                pl.BlockSpec((1, 8, rows), lambda s, t, *_: (s, 0, 0)),
                pl.BlockSpec((1, 1, rows), lambda s, t, *_: (s, 0, 0)),
            ],
            out_specs=[
                pl.BlockSpec((1, rows, width), lambda s, t, *_: (s, 0, 0)),
                pl.BlockSpec((1, 1, tk, 2 * width), at),
            ],
            scratch_shapes=[pltpu.VMEM((2 * heads, tk, HEAD_DIM), F32)],
        ),
        compiler_params=pltpu.CompilerParams(vmem_limit_bytes=48 * MB),
        name="attend_backward",
        cost_estimate=pl.CostEstimate(
            flops=int(5 * 2 * seqs * heads * rows * rows * 2 * HEAD_DIM * 4),
            bytes_accessed=100 * MB,
            transcendentals=int(seqs * heads * rows * rows * 2),
        ),
    )(words, bounds, edges, queries, keys_values, grads, stats, starts)


def gated_mlp(rows_in, grads, gates, words, routed, shared, steps, s_steps, groups):
    block_rows, width = rows_in[0].shape
    n_rows = len(rows_in)
    count = block_rows * n_rows
    tile = 256
    chunk = min(512, count)
    all_steps = steps + s_steps
    pieces = [(piece, held, where) for where, lists in enumerate((routed, shared)) for held in (0, 1) for piece in lists[held]]

    def kernel(word_ref, *refs):
        row_refs, d_refs, c_in = refs[:n_rows], refs[n_rows : 2 * n_rows], refs[2 * n_rows]
        refs = refs[2 * n_rows + 1 :]
        piece_refs, refs = refs[: len(pieces)], refs[len(pieces) :]
        y_out, dx_out, dc_ref, one_ref, two_ref, x_ref, xt_ref, d_ref, dt_ref, c_ref, y_ref, dx_ref, w_s, wt_s, wo_s, wot_s, a_s, g_s = refs
        j = pl.program_id(0)

        @pl.when(j == 0)
        def _():
            dc_ref[...] = jnp.zeros_like(dc_ref)
            c_ref[...] = c_in[...]
            y_ref[...] = jnp.zeros_like(y_ref)
            dx_ref[...] = jnp.zeros_like(dx_ref)
            for sources, plain, across in ((row_refs, x_ref, xt_ref), (d_refs, d_ref, dt_ref)):
                for n, ref in enumerate(sources):
                    at = slice(n * block_rows, (n + 1) * block_rows)
                    plain[at, :] = ref[...]
                    across[:, at] = ref[...].T

        @pl.when(j == steps)
        def _():
            c_ref[...] = jnp.ones_like(c_ref)

        def fill(kind):
            for ref, (piece, held, where) in zip(piece_refs, pieces):
                if where != kind:
                    continue
                tall, wide = ref.shape
                row, times, lane_word, lane_times, lane = piece[3:]
                at = pl.ds(pl.multiple_of(word_ref[row], times), tall)
                if lane_word is None:
                    lanes = slice(lane, lane + wide)
                else:
                    lanes = pl.ds(pl.multiple_of(word_ref[lane_word], lane_times), wide)
                (w_s, wo_s)[held][at, lanes] = ref[...]

        pl.when(j < steps)(lambda: fill(0))
        pl.when(j >= steps)(lambda: fill(1))
        wt_s[...] = w_s[...].T
        wot_s[...] = wo_s[...].T

        routed_here = jnp.where(j < steps, 1.0, 0.0)

        def body(n, carry):
            at = pl.ds(pl.multiple_of(n * chunk, chunk), chunk)
            both = dot(x_ref[at, :], w_s[...])
            gate, up = both[:, :tile], both[:, tile:]
            raw = dot(d_ref[at, :], wot_s[...])
            c = c_ref[at, :]
            sig = 0.5 + 0.5 * jnp.tanh(0.5 * gate)
            silu = gate * sig
            act = silu * up

            dc_ref[at, :] += jnp.sum(act * raw, axis=1, keepdims=True) * routed_here
            back = raw * c
            a_low = (act * c).astype(BF)
            dg = (back * up * (sig + silu * (1.0 - sig))).astype(BF)
            du = (back * silu).astype(BF)
            a_s[at, :] = a_low
            g_s[at, :tile] = dg
            g_s[at, tile:] = du
            y_ref[at, :] += dot(a_low, wo_s[...])
            dx_ref[at, :] += dot(g_s[at, :], wt_s[...])
            return carry

        lax.fori_loop(0, count // chunk, body, 0)

        if groups:
            keep = word_ref[1]
            half = width // 2
            r, q = half // groups, tile // 2 // groups
            for ref, which in ((one_ref, keep), (two_ref, 1 - keep)):
                got = dot(xt_ref[pl.ds(pl.multiple_of(which * half, half), half), :], g_s[...]).astype(BF)
                for z in range(groups):
                    for g in range(2):
                        ref[z, 0, g * r : (g + 1) * r, :] = got[z * r : (z + 1) * r, g * tile : (g + 1) * tile]
            for n in range(width // tile):
                got = dot(dt_ref[n * tile : (n + 1) * tile, :], a_s[...]).T.astype(BF)
                low, high = got[: tile // 2], got[tile // 2 :]
                for ref, which in ((one_ref, keep), (two_ref, 1 - keep)):
                    mine = jnp.where(which == 0, low, high)
                    for z in range(groups):
                        ref[z, 0, 2 * r + n * q : 2 * r + (n + 1) * q, :] = mine[z * q : (z + 1) * q]
        else:
            one_ref[0] = dot(xt_ref[...], g_s[...]).astype(BF)
            for n in range(width // tile):
                at = slice(n * tile, (n + 1) * tile)
                two_ref[0, :, at] = dot(dt_ref[at, :], a_s[...]).T.astype(BF)

        @pl.when(j == all_steps - 1)
        def _():
            y_out[...] = y_ref[...].astype(BF)
            dx_out[...] = dx_ref[...].astype(BF)

    once = pl.Buffered(1)
    whole = lambda *shape: pl.BlockSpec(shape, lambda j, *_: (0,) * len(shape), pipeline_mode=once)

    def piece_spec(piece, where):
        index = piece[2]
        if where == 0:
            return pl.BlockSpec(piece[1], lambda j, w: index(jnp.minimum(j, steps - 1), w))
        return pl.BlockSpec(piece[1], lambda j, w: index(jnp.maximum(j - steps, 0), w))

    in_specs = [whole(block_rows, width)] * (2 * n_rows) + [whole(count, 1)]
    in_specs += [piece_spec(piece, where) for piece, _, where in pieces]
    operands = [*rows_in, *grads, gates, *(piece[0] for piece, _, _ in pieces)]
    if groups:
        rows = width // groups + 3 * tile // 2 // groups
        grad_shape = [(groups, all_steps, rows, tile)] * 2
        grad_spec = [pl.BlockSpec((groups, 1, rows, tile), lambda j, *_: (0, j, 0, 0))] * 2
    else:
        grad_shape = [(all_steps, width, 2 * tile), (all_steps, tile, width)]
        grad_spec = [pl.BlockSpec((1,) + shape[1:], lambda j, *_: (j, 0, 0)) for shape in grad_shape]
    return pl.pallas_call(
        kernel,
        out_shape=(
            jax.ShapeDtypeStruct((count, width), BF),
            jax.ShapeDtypeStruct((count, width), BF),
            jax.ShapeDtypeStruct((count, 1), F32),
            *(jax.ShapeDtypeStruct(shape, BF) for shape in grad_shape),
        ),
        grid_spec=pltpu.PrefetchScalarGridSpec(
            num_scalar_prefetch=1,
            grid=(all_steps,),
            in_specs=in_specs,
            out_specs=[whole(count, width), whole(count, width), whole(count, 1), *grad_spec],
            scratch_shapes=[
                *[pltpu.VMEM((count, width), BF), pltpu.VMEM((width, count), BF)] * 2,
                pltpu.VMEM((count, 1), F32),
                pltpu.VMEM((count, width), F32),
                pltpu.VMEM((count, width), F32),
                pltpu.VMEM((width, 2 * tile), BF),
                pltpu.VMEM((2 * tile, width), BF),
                pltpu.VMEM((tile, width), BF),
                pltpu.VMEM((width, tile), BF),
                pltpu.VMEM((count, tile), BF),
                pltpu.VMEM((count, 2 * tile), BF),
            ],
        ),
        compiler_params=pltpu.CompilerParams(vmem_limit_bytes=60 * MB),
        name="gated_mlp",
        cost_estimate=pl.CostEstimate(
            flops=9 * 2 * count * width * tile * all_steps,
            bytes_accessed=40 * MB,
            transcendentals=count * tile * all_steps,
        ),
    )(words, *operands)


def unpack(parts, shards, steps, s_steps, width):
    ctxs, groups, total, wide = parts.shape
    per = wide // shards
    r = width // shards // groups
    q = per // groups
    cols = width // wide
    tall = 2 * r + cols * q
    ff, piece = steps * wide, s_steps * per
    shapes = (
        (ctxs, groups * r, 2 * ff),
        (ctxs, steps * per, width),
        (groups * r, 2 * shards * ctxs * piece),
        (ctxs * piece, width),
    )
    if per % 128 or q % 16:
        made = parts[:, :, : (steps + s_steps) * tall].reshape(ctxs, groups, -1, tall, wide)
        d_in = made[:, :, :, : 2 * r].reshape(ctxs, groups, -1, 2, r, shards, per)
        d_out = made[:, :, :, 2 * r :].reshape(ctxs, groups, -1, cols, q, wide)
        e_in = d_in[:, :, :steps].transpose(0, 1, 4, 3, 5, 2, 6)
        e_out = d_out[:, :, :steps].transpose(0, 2, 1, 4, 3, 5)
        s_in = d_in[:, :, steps:].transpose(1, 4, 3, 5, 0, 2, 6)
        s_out = d_out[:, :, steps:].transpose(0, 2, 1, 4, 3, 5)
        return [g.astype(F32).reshape(shape) for g, shape in zip((e_in, e_out, s_in, s_out), shapes)]

    def kernel(in_ref, ein_ref, eout_ref, sin_ref, sout_ref):
        c = pl.program_id(0)

        def get(z, row, high):
            return in_ref[0, z, row : row + high, :].astype(F32)

        for z in range(groups):
            at = slice(z * r, (z + 1) * r)
            for j in range(steps):
                for g in range(2):
                    got = get(z, j * tall + g * r, r)
                    for n in range(shards):
                        col = g * ff + n * (ff // shards) + j * per
                        ein_ref[0, at, col : col + per] = got[:, n * per : (n + 1) * per]
                for b in range(cols):
                    row = j * per + z * q
                    got = get(z, j * tall + 2 * r + b * q, q)
                    eout_ref[0, row : row + q, b * wide : (b + 1) * wide] = got
            for j in range(s_steps):
                first = (steps + j) * tall
                for g in range(2):
                    got = get(z, first + g * r, r)
                    for n in range(shards):
                        col = ((g * shards + n) * ctxs + c) * piece + j * per
                        sin_ref[at, pl.ds(pl.multiple_of(col, 128), per)] = got[:, n * per : (n + 1) * per]
                for b in range(cols):
                    row = j * per + z * q
                    got = get(z, first + 2 * r + b * q, q)
                    sout_ref[row : row + q, b * wide : (b + 1) * wide] = got

    outs = pl.pallas_call(
        kernel,
        out_shape=tuple(jax.ShapeDtypeStruct(shape, F32) for shape in shapes),
        grid=(ctxs,),
        in_specs=[pl.BlockSpec((1, groups, total, wide), lambda c: (c, 0, 0, 0))],
        out_specs=(
            pl.BlockSpec((1,) + shapes[0][1:], lambda c: (c, 0, 0)),
            pl.BlockSpec((1,) + shapes[1][1:], lambda c: (c, 0, 0)),
            pl.BlockSpec(shapes[2], lambda c: (0, 0), pipeline_mode=pl.Buffered(1)),
            pl.BlockSpec((piece, width), lambda c: (c, 0)),
        ),
        compiler_params=pltpu.CompilerParams(vmem_limit_bytes=58 * MB),
        name="unpack",
        cost_estimate=pl.CostEstimate(flops=0, bytes_accessed=6 * parts.size, transcendentals=0),
    )(parts)
    return outs


def weight_pieces(
    shared_in, shared_out, expert_in, expert_out, near, member, core, shard, shards, ctxs, steps, s_steps, per, piece
):
    rows, width = shared_in.shape[0], shared_out.shape[1]
    ff, tile = steps * per * shards, per * shards
    s_split = shared_in.reshape(rows, 2, shards, ctxs, piece)
    pick = lambda array, who, axis: lax.dynamic_index_in_dim(array, who, axis, keepdims=False)

    if shards != 2:

        def tiles(e, s):
            gathered = []
            for v, count in ((e, steps), (s, s_steps)):
                v = v.reshape(rows, 2, shards, count, per).transpose(3, 0, 1, 2, 4).reshape(count, rows, 2 * tile)
                gathered.append(lax.all_gather(v, "fsdp", axis=1, tiled=True))
            return gathered

        e_in, s_in = tiles(pick(expert_in, member, 0), pick(s_split, member, 3))
        e_out = pick(expert_out, member, 0).reshape(steps, per, width)
        s_out = lax.dynamic_slice_in_dim(shared_out, member * piece, piece, 0).reshape(s_steps, per, width)
        e_out, s_out = (lax.all_gather(v, "fsdp", axis=1, tiled=True) for v in (e_out, s_out))
        made = [
            (
                [(v, (None, width, 2 * tile), lambda j, w: (j, 0, 0), 0, width, None, 0, 0)],
                [(o, (None, tile, width), lambda j, w: (j, 0, 0), 0, tile, None, 0, 0)],
            )
            for v, o in ((e_in, e_out), (s_in, s_out))
        ]
        return made[0], made[1], jnp.zeros((2,), jnp.int32), ((), (), ())

    who, part = member ^ 1, rows // 2
    half = width // 2
    columns = [
        lax.dynamic_slice(shared_in, (core * part, ((g * shards + n) * ctxs + who) * piece), (part, piece))
        for g in range(2)
        for n in range(shards)
    ]
    sent = [
        jnp.concatenate(
            [lax.dynamic_slice(expert_in, (who, core * part, 0), (1, part, 2 * ff))[0], *columns], axis=1
        ),
        jnp.concatenate(
            [
                lax.dynamic_slice(expert_out, (who, 0, core * half), (1, expert_out.shape[1], half))[0],
                lax.dynamic_slice(shared_out, (who * piece, core * half), (piece, half)),
            ],
            axis=0,
        ),
    ]
    got = [swap_with(v, "fsdp", 1) for v in sent]
    sib = [swap_with(once_there(v, near), "ctx", 1) for v in got]
    far_row, far_out = (1 - shard) * rows, (1 - shard) * per
    words = [
        member, core, shard * rows, far_row + core * part, far_row + (1 - core) * part,
        shard * per, far_out, core * half, (1 - core) * half,
    ]
    words = jnp.stack(words).astype(jnp.int32)
    blocks, s_blocks = ff // shards // per, piece // per
    e_ins, s_ins = [], []
    for g in range(2):
        for n in range(shards):
            lane = g * tile + n * per
            e_col = lambda j, g=g, n=n: (g * shards + n) * blocks + j
            s_own = lambda j, w, g=g, n=n: ((g * shards + n) * ctxs + w[0]) * s_blocks + j
            s_far = lambda j, g=g, n=n: 2 * shards * blocks + (g * shards + n) * s_blocks + j
            e_own = lambda j, w, col=e_col: (w[0], 0, col(j))
            e_ins.append((expert_in, (None, rows, per), e_own, 2, 16, None, 0, lane))
            s_ins.append((shared_in, (rows, per), lambda j, w, col=s_own: (0, col(j, w)), 2, 16, None, 0, lane))
            for word, source in ((3, got), (4, sib)):
                e_ins.append((source[0], (part, per), lambda j, w, col=e_col: (0, col(j)), word, 16, None, 0, lane))
                s_ins.append((source[0], (part, per), lambda j, w, col=s_far: (0, col(j)), word, 16, None, 0, lane))
    e_outs = [(expert_out, (None, per, width), lambda j, w: (w[0], j, 0), 5, per, None, 0, 0)]
    s_outs = [(shared_out, (per, width), lambda j, w: (w[0] * s_blocks + j, 0), 5, per, None, 0, 0)]
    for word, source in ((7, got), (8, sib)):
        e_outs.append((source[1], (per, half), lambda j, w: (j, 0), 6, per, word, 128, 0))
        s_outs.append((source[1], (per, half), lambda j, w: (steps + j, 0), 6, per, word, 128, 0))
    return (e_ins, e_outs), (s_ins, s_outs), words, (sent, got, sib)


def inverse_rms(values):
    return lax.rsqrt(jnp.mean(values * values, axis=-1, keepdims=True) + EPS)


def norm_back(values, inverse, gain, grad):
    scaled = grad * gain
    dotted = jnp.mean(scaled * values, axis=-1, keepdims=True)
    return inverse * scaled - values * (inverse * inverse * inverse) * dotted


def half_turn(pairs):
    size = pairs * HEAD_DIM
    row = lax.broadcasted_iota(jnp.int32, (size, size), 0)
    col = lax.broadcasted_iota(jnp.int32, (size, size), 1)
    return (row == (col ^ (HEAD_DIM // 2))).astype(BF)


def on_device(
    tokens,
    segment_ids,
    routes,
    cotangent,
    norm1_gain,
    qkv_weight,
    out_weight,
    norm2_gain,
    router_weight,
    shared_in,
    shared_out,
    expert_in,
    expert_out,
):
    local_len, seqs, width = tokens.shape
    count = local_len * seqs
    groups = lax.axis_size("head")
    ctxs = lax.axis_size("ctx")
    shards = lax.axis_size("fsdp")
    ctx = lax.axis_index("ctx")
    head = lax.axis_index("head")
    shard = lax.axis_index("fsdp")
    group_width = width // groups
    heads = group_width // HEAD_DIM
    block = local_len * groups
    span = seqs * block
    experts = expert_in.shape[0]
    rows_per = width // shards
    ff = expert_in.shape[2] // 2
    fs = shared_in.shape[1] // 2
    fs_part = fs // ctxs
    ctx_word = ctx.astype(jnp.int32).reshape(1)

    member = group_member()
    piece = fs // shards // ctxs
    tile = 256
    per = tile // shards
    steps, s_steps = ff // tile, fs_part // tile
    x_own = tokens.transpose(1, 0, 2)
    w_group = lax.dynamic_index_in_dim(qkv_weight.reshape(-1, 3, groups, group_width), head, 2, keepdims=False)
    w_group = fsdp_gather_small(w_group.reshape(-1, 3 * group_width), 0)
    small = jnp.concatenate([norm1_gain[None], norm2_gain[None], router_weight.T], axis=0)
    small = fsdp_gather_small(small, 1)
    x_line = line_gather_kernel(x_own, 0)
    gain_one, gain_two = small[0].astype(F32), small[1].astype(F32)
    w_router = small[2:]
    w_q, w_kv = w_group[:, :group_width], w_group[:, group_width:]
    w_q_turned = dot(w_q, half_turn(heads)).astype(BF)
    w_kv_turned = dot(w_kv, half_turn(2 * heads)).astype(BF)

    dz_own = cotangent.transpose(1, 0, 2).reshape(count, width)
    scale = HEAD_DIM**-0.5
    lane = lax.broadcasted_iota(jnp.int32, (1, block, 2 * group_width), 2)
    position = ctx * block + lax.broadcasted_iota(jnp.int32, (1, block, 2 * group_width), 1)
    index = (lane % (HEAD_DIM // 2)).astype(F32)
    angle = position.astype(F32) * jnp.exp(-math.log(ROPE_BASE) * 2.0 * index / HEAD_DIM)
    sign = jnp.where(lane % HEAD_DIM < HEAD_DIM // 2, -1.0, 1.0)
    cos_kv = jnp.where(lane < group_width, jnp.cos(angle), 1.0)
    sin_kv = jnp.where(lane < group_width, jnp.sin(angle) * sign, 0.0)
    cos_q, sin_q = cos_kv[:, :, :group_width] * scale, sin_kv[:, :, :group_width] * scale

    dz_blocks = group_gather(dz_own)
    x_f = once_there(x_line, dz_blocks[1], dz_blocks[2]).astype(F32)
    inverse_one = inverse_rms(x_f)
    normed = (x_f * inverse_one * gain_one).astype(BF)
    normed_rows = normed.reshape(span, width)

    def turned(weight, weight_turned, cos_table, sin_table):
        plain = dot(normed_rows, weight).reshape(seqs, block, -1)
        other = dot(normed_rows, weight_turned).reshape(seqs, block, -1)
        return (plain * cos_table + other * sin_table).astype(BF)

    key_value = turned(w_kv, w_kv_turned, cos_kv, sin_kv)
    kv_blocks = ctx_gather(key_value)
    queries = turned(w_q, w_q_turned, cos_q, sin_q)
    kv_near = jnp.stack(kv_blocks[:2])
    kv_far = jnp.stack(kv_blocks[2:])
    w_attn = fsdp_gather_small(out_weight, 0)

    def forward_bounds(tq, tk):
        nq = block // tq
        first = ctx * block + jnp.arange(nq, dtype=jnp.int32) * tq
        low = segment_ids[:, ::tq] // tk
        last_start = segment_ids[:, tq - 1 :: tq]
        clear_to = jnp.broadcast_to(first // tk, low.shape)
        clear_from = jnp.minimum((last_start + tk - 1) // tk, clear_to)
        clear_from = jnp.maximum(clear_from, low)
        clear_to = jnp.maximum(clear_to, clear_from)
        high = jnp.broadcast_to((first + tq - 1) // tk + 1, low.shape)
        return jnp.stack([low, clear_from, clear_to, high], axis=2).astype(jnp.int32)

    fwd_q, fwd_k = min(1024, block), min(512, block)
    bounds = forward_bounds(fwd_q, fwd_k)
    near_base = (ctx // 2) * 2
    far_base = near_base ^ 2
    near_words = jnp.stack([ctx, 0 * ctx, near_base]).astype(jnp.int32)
    far_words = jnp.stack([ctx, 0 * ctx + 2, far_base]).astype(jnp.int32)
    edge = near_base * (block // fwd_k)
    starts = segment_ids[:, None, :]
    state = attend_forward(near_words, jnp.maximum(bounds, edge), queries, kv_near, starts, fwd_q, fwd_k, None)
    e_pieces, s_pieces, words, sent = weight_pieces(
        shared_in, shared_out, expert_in, expert_out, state[0], member, ctx % 2, shard,
        shards, ctxs, steps, s_steps, per, piece,
    )
    attended, attended_low, lse = attend_forward(
        far_words, jnp.minimum(bounds, edge), queries, kv_far, starts, fwd_q, fwd_k, state
    )
    attended_low = after(attended_low, *sent[2], w_attn)
    sent = attended_low.reshape(seqs, groups, local_len, group_width)
    back = lax.all_to_all(sent, "head", split_axis=1, concat_axis=3, tiled=True)
    attn_rows = back.reshape(count, width)

    x_rows = x_own.reshape(count, width).astype(F32)
    hidden = x_rows + dot(attn_rows, w_attn)
    inverse_two = inverse_rms(hidden)
    normed_two = (hidden * inverse_two * gain_two).astype(BF)
    route_rows = routes.reshape(local_len, seqs, 2).transpose(1, 0, 2).reshape(count, 2)
    logits = dot_t(normed_two, w_router)
    ids = jnp.arange(experts, dtype=jnp.int32)
    picks = (route_rows[:, :, None] == ids).astype(F32)
    chosen = jnp.sum(logits[:, None, :] * picks, axis=2)
    gate_first = 1.0 / (1.0 + jnp.exp(chosen[:, 1:] - chosen[:, :1]))
    gates = jnp.concatenate([gate_first, 1.0 - gate_first], axis=1)
    combine = jnp.sum(gates[:, :, None] * picks, axis=1)

    xn_blocks = group_gather(normed_two)
    combine_t = combine.T
    c_one, c_two = group_swap(combine_t, 1), group_swap(combine_t, 2)
    combine_all = jnp.concatenate([combine_t, c_one, c_two, group_swap(c_one, 2)], axis=1)
    c_own = lax.dynamic_index_in_dim(combine_all, member, 0, keepdims=False)[:, None]
    y_part, dx_part, dc, g_one, g_two = gated_mlp(
        xn_blocks, dz_blocks, c_own, words, e_pieces, s_pieces, steps, s_steps, groups if paired() else 0
    )
    dc_blocks = dc.reshape(ctxs, count)
    dc_got = [
        dc_blocks[0],
        group_swap(dc_blocks[1], 1),
        group_swap(dc_blocks[2], 2),
        group_swap(group_swap(dc_blocks[3], 1), 2),
    ]
    dcombine = sum(
        dc_got[k][:, None] * ((member ^ k) == ids).astype(F32)[None, :] for k in range(ctxs)
    )
    dx_blocks = dx_part.reshape(ctxs, count, width)
    dx_near = group_scatter_near([dx_blocks[k] for k in range(ctxs)])
    g_part = sum_parts(g_one, g_two)
    dxn2 = dx_near[0].astype(F32) + group_swap(dx_near[1], 1).astype(F32) + group_swap(dx_near[2], 2).astype(F32)

    dchosen = jnp.sum(dcombine[:, None, :] * picks, axis=2)
    dfirst = gates[:, :1] * gates[:, 1:] * (dchosen[:, :1] - dchosen[:, 1:])
    dlogits = (dfirst * (picks[:, 0] - picks[:, 1])).astype(BF)
    router_part = dot_l(normed_two, dlogits)
    dxn2 = dxn2 + dot(dlogits, w_router)
    dz_rows = dz_own.astype(F32)
    dh = dz_rows + norm_back(hidden, inverse_two, gain_two, dxn2)
    gain_two_part = jnp.sum(dxn2 * hidden * inverse_two, axis=0)
    dh_low = dh.astype(BF)
    g_attn = dot_l(attn_rows, dh_low)
    g_attn = jnp.concatenate(
        [g_attn, gain_two_part[:, None], router_part, jnp.zeros((width, 127 - experts), F32)], axis=1
    ).astype(BF)
    dattn = dot_t(dh_low, w_attn).astype(BF).reshape(seqs, local_len, width)
    grad_out = lax.all_to_all(
        dattn.reshape(seqs, local_len, groups, group_width), "head", split_axis=2, concat_axis=1, tiled=True
    ).reshape(seqs, block, group_width)

    y_blocks = after(y_part, dh_low).reshape(ctxs, count, width)
    y_near = group_scatter_near([y_blocks[k] for k in range(ctxs)])
    y_near = [y_near[0], group_swap(y_near[1], 1), group_swap(y_near[2], 2)]
    grad_out = once_there(grad_out, y_near[1], y_near[2])
    y_own = sum(v.astype(F32) for v in y_near)

    delta = jnp.sum((grad_out.astype(F32) * attended).reshape(seqs, block, heads, HEAD_DIM), axis=3)
    stats = jnp.concatenate(
        [lse[:, :heads], delta.transpose(0, 2, 1), jnp.zeros((seqs, 8 - 2 * heads, block), F32)],
        axis=1,
    )
    tq = tk = min(512, block)
    tile_last = ctx * block + (jnp.arange(block // tq, dtype=jnp.int32) + 1) * tq - 1
    tile_key = jnp.arange(ctxs * block // tk, dtype=jnp.int32)
    q_low = jnp.sum((tile_last[None, :] < (tile_key * tk)[:, None]).astype(jnp.int32), axis=1)
    q_high = jnp.sum(((segment_ids[:, ::tq] // tk)[:, None, :] <= tile_key[None, :, None]).astype(jnp.int32), axis=2)
    q_low = jnp.broadcast_to(q_low, q_high.shape)
    back_bounds = jnp.stack([q_low, q_high], axis=2).astype(jnp.int32)
    edges = segment_ids[:, tq - 1 :: tq]
    dq_far, far_parts = attend_backward(
        far_words, back_bounds, edges, queries, kv_far, grad_out, stats, starts, tq, tk
    )
    far_sum = (far_parts[0].astype(F32) + swap_with(far_parts[1], "ctx", 1).astype(F32)).astype(BF)
    far_got = swap_with(far_sum, "ctx", 2)
    whole_parts = exchange_parts(once_there(g_part, dq_far), far_sum)
    gathered = share_parts(whole_parts)
    dq_near, near_parts = attend_backward(
        near_words, back_bounds, edges, queries, kv_near, once_there(grad_out, whole_parts, far_sum), stats, starts, tq, tk
    )
    if paired():
        g_attn = half_sum(g_attn, 0, "fsdp", shard, 1, dq_near).astype(BF)
        g_attn = half_sum(g_attn, 0, "ctx", ctx % 2, 1).astype(BF)
        g_attn = half_sum(g_attn, 0, "ctx", ctx // 2, 2).astype(BF)
    output = once_there(hidden + y_own, dq_near).astype(BF).reshape(seqs, local_len, width).transpose(1, 0, 2)
    dkv = near_parts[0].astype(F32) + swap_with(near_parts[1], "ctx", 1).astype(F32) + far_got.astype(F32)
    dq = ((dq_far + dq_near) * scale).astype(BF).astype(F32)
    dkv = dkv.astype(BF).astype(F32)

    def turned_back(grad, cos_table, sin_table, pairs):
        other = (grad * sin_table).astype(BF).reshape(span, -1)
        back = dot(other, half_turn(pairs)).reshape(seqs, block, -1)
        return (grad * cos_table + back).astype(BF).reshape(span, -1)

    d_q = turned_back(dq, cos_q * HEAD_DIM**0.5, sin_q * HEAD_DIM**0.5, heads)
    d_kv = turned_back(dkv, cos_kv, sin_kv, 2 * heads)
    dxn1_part = (dot_t(d_q, w_q) + dot_t(d_kv, w_kv)).reshape(seqs, block, width)
    g_q, g_kv = dot_l(normed_rows, d_q), dot_l(normed_rows, d_kv)
    gain_one_part = jnp.sum(dxn1_part * x_f * inverse_one, axis=(0, 1))
    filler = jnp.zeros((width, 128 - 3 * group_width % 128 - 1), F32)
    g_qkv = jnp.concatenate([g_q, g_kv, gain_one_part[:, None], filler], axis=1).astype(BF)
    if paired():
        blocks = dxn1_part.astype(BF).reshape(seqs, groups, local_len, width).transpose(1, 0, 2, 3)
        dxn1, qkv_grad, gain_one_grad, g_attn = tail_kernel(blocks.reshape(groups, count, width), g_qkv, g_attn, 1)
        gain_one_grad = gain_one_grad[:, 3 * group_width % 128]
    else:
        dxn1 = line_scatter(dxn1_part.astype(BF), 1).reshape(count, width)
        g_qkv = lax.psum(lax.psum_scatter(g_qkv, "fsdp", scatter_dimension=0, tiled=True), "ctx")
        g_qkv = line_gather(g_qkv[:, None], 1).astype(F32)
        qkv_grad = g_qkv[..., : 3 * group_width].reshape(rows_per, groups, 3, group_width)
        qkv_grad = qkv_grad.transpose(0, 2, 1, 3).reshape(rows_per, 3 * width)
        gain_one_grad = jnp.sum(g_qkv[..., 3 * group_width], axis=1)
        g_attn = lax.psum(lax.psum_scatter(g_attn, "fsdp", scatter_dimension=0, tiled=True), ("ctx", "head"))
        g_attn = g_attn.astype(F32)
    dx_norm = norm_back(x_rows, inverse_rms(x_rows), gain_one, dxn1)
    tokens_grad = (dh + dx_norm).reshape(seqs, local_len, width).transpose(1, 0, 2)

    expert_in_grad, expert_out_grad, shared_in_grad, shared_out_grad = unpack(
        gathered, shards, steps, s_steps, width
    )
    out_grad, side = g_attn[:, :width], g_attn[:, width:]
    return (
        output,
        tokens_grad,
        gain_one_grad,
        qkv_grad,
        out_grad,
        side[:, 0],
        side[:, 1 : 1 + experts],
        shared_in_grad,
        shared_out_grad,
        expert_in_grad,
        expert_out_grad,
    )


def solution(mesh):
    rows = P(("ctx", "head"), "fsdp", None)
    vector = P("fsdp")
    matrix = P("fsdp", None)
    stack = P(None, "fsdp", None)
    return jax.shard_map(
        on_device,
        mesh=mesh,
        in_specs=(
            rows,
            P("fsdp", "ctx"),
            P(("ctx", "head"), "fsdp", None, None),
            rows,
            vector,
            matrix,
            matrix,
            vector,
            matrix,
            matrix,
            matrix,
            stack,
            stack,
        ),
        out_specs=(rows, rows, vector, matrix, matrix, vector, matrix, matrix, matrix, stack, stack),
        check_vma=False,
    )
```
